32 devices in a mesh: group: 8 (over y, x, core), dp: 4 (over z).
Axes of the slice: x: 2, y: 2, z: 4, core: 2. Of those that a mesh axis runs over, the one named last changes fastest.
Arguments:
- latents: bfloat16 [8, 128, 6144], P('group', 'dp'), may hold values from -6 to 6
- steps: int32 [8], P('group'), may hold values from 0 to 15
- segment_ids: int32 [128], replicated, may hold values from 0 to 3, never falling along the last dimension, each value on 1 to 64 neighbouring positions
- mod_table: float32 [16, 2, 6144], replicated, may hold values from -3 to 3
- w_query: bfloat16 [6144, 1024], P(None, 'dp')
- w_key: bfloat16 [6144, 1024], P(None, 'dp')
- w_value: bfloat16 [6144, 1024], P(None, 'dp'), may hold values from -0.3125 to 0.3125
Outputs:
- attended: bfloat16 [8, 128, 1024], P('group', 'dp')
The draws below stay inside these ranges and needn't reach their ends.
Inputs may be any that keep to these rules, and one draw needn't show every extreme that they name: `segment_ids`: rows of one clip are contiguous; every clip index occurs, a clip holds 1 to 64 rows and one holds exactly that many.
All inputs are finite; a program needn't handle non-finite values.
Results may differ from the reference program's by a relative error of at most 0.011.
Values may be sent and summed in bfloat16 or wider, within the bound.
No kernel may reach another device: no remote copies, remote signals or barrier semaphores. Data moves between devices by JAX's collectives and lax.ppermute only.
A program may use at most 128 MiB of HBM per device.

```python
import math
import jax
import jax.numpy as jnp
import numpy as np
from jax import lax

D = 6144
HD = 128
STEPS = 16
ROWS = 32
HEADS = 8
TOKC = 128
GROUPS = 8
N_DP = 4


def shared_keys(key):
    return jax.random.normal(jax.random.fold_in(key, 11), (D, HEADS * HD), jnp.float32) / jnp.sqrt(jnp.float32(D))


def draw_w_key(key, part):
    return shared_keys(key).astype(jnp.bfloat16)


def draw_w_query(key, part):
    fresh = jax.random.normal(jax.random.fold_in(key, 12), (D, HEADS * HD), jnp.float32) * (2.0 / jnp.sqrt(jnp.float32(D)))
    return fresh.astype(jnp.bfloat16)


def set_ends(array, stream_key, low, high):
    spot = [jax.random.randint(jax.random.fold_in(stream_key, axis), (), 0, length) for axis, length in enumerate(array.shape)]
    widest = array.shape.index(max(array.shape))
    beside = spot[:widest] + [(spot[widest] + 1) % array.shape[widest]] + spot[widest + 1:]
    return array.at[tuple(spot)].set(low).at[tuple(beside)].set(high)


def levels(key, extent, pieces, low, high):
    gain = 1.0
    for position, shards_of in pieces:
        draws = jax.random.uniform(jax.random.fold_in(jax.random.fold_in(key, 6), position), (shards_of,), jnp.float32, low / len(pieces), high / len(pieces))
        gain = gain * jnp.repeat(jnp.exp(draws), extent[position] // shards_of).reshape((-1,) + (1,) * (len(extent) - 1 - position))
    return gain


def length_profile(amount, total, most, lean):
    loads = [(1 << 20) // math.isqrt(standing ** lean) + 1 for standing in range(2, amount + 1)]
    surplus, given = total - most - (amount - 1), [1] * (amount - 1)
    while surplus > 0:
        movable = [i for i in range(amount - 1) if given[i] < most]
        whole, left = sum([loads[i] for i in movable]), surplus
        for i in movable:
            extra = min(most - given[i], max(1, left * loads[i] // whole), surplus)
            given[i] = given[i] + extra
            surplus = surplus - extra
    return np.array([most] + given)


def uneven_parts(stream_key, number_of, total, bound, skew):
    if number_of == 2:
        one = jax.random.randint(stream_key, (), max(1, total - bound), min(bound, total - 1) + 1)
        return jnp.stack([one, total - one])
    tallies = jnp.asarray(length_profile(number_of, total, bound, skew), jnp.int32)
    pairs = (number_of - 1) // 2
    giver, taker = tallies[1:1 + 2 * pairs:2], tallies[2:2 + 2 * pairs:2]
    slack = jnp.minimum(giver - 1, bound - taker)
    passed = jax.random.randint(jax.random.fold_in(stream_key, 1), (pairs,), 0, 1 << 20) % (slack + 1)
    tallies = tallies.at[1:1 + 2 * pairs:2].set(giver - passed).at[2:2 + 2 * pairs:2].set(taker + passed)
    return tallies[jax.random.permutation(jax.random.fold_in(stream_key, 2), number_of)]


def noise(stream_key, dims, width, bound, split=(), kind=jnp.bfloat16):
    loudness = levels(stream_key, dims, split, -0.22, 0.18) if split else 1.0
    values = jax.random.normal(stream_key, dims, jnp.float32) * width * loudness
    return jnp.minimum(jnp.maximum(values, -bound), bound).astype(kind)


def setup_inputs(seed: int = 0) -> dict:
    key_list = jax.random.split(jax.random.key(seed), 8)
    latents = noise(key_list[0], (GROUPS, TOKC, D), 1.0, 6.0, ((0, 8), (1, 4)))
    steps = set_ends(jax.random.randint(key_list[1], (GROUPS,), 0, STEPS), jax.random.fold_in(key_list[1], 1), 0, STEPS - 1).astype(jnp.int32)
    segment_ids = jnp.searchsorted(jnp.cumsum(uneven_parts(key_list[2], N_DP, TOKC, 2 * ROWS, 2)), jnp.arange(TOKC), side="right").astype(jnp.int32)
    mod_table = noise(key_list[3], (STEPS, 2, D), 0.5, 3.0, (), jnp.float32)
    w_query = draw_w_query(jax.random.fold_in(key_list[7], 71), 0)
    w_key = draw_w_key(jax.random.fold_in(key_list[7], 71), 0)
    w_value = noise(key_list[6], (D, HEADS * HD), (D // 16) ** -0.5, 0.3125, ((1, 4),))
    return dict(latents=latents, steps=steps, segment_ids=segment_ids, mod_table=mod_table, w_query=w_query, w_key=w_key, w_value=w_value)


def reference(latents, steps, segment_ids, mod_table, w_query, w_key, w_value):
    groups = latents.shape[0]
    tokc = latents.shape[1]
    x = latents.astype(jnp.float32)
    normed = x * lax.rsqrt(lax.optimization_barrier(jnp.mean(x * x, axis=-1, keepdims=True)) + 1e-06)
    picker = (steps[:, None] == jnp.arange(STEPS, dtype=jnp.int32)[None, :]).astype(jnp.float32)
    modulation = jnp.dot(picker, mod_table.reshape(STEPS, 2 * D), precision=lax.Precision.HIGHEST)
    rows = (normed * (1.0 + modulation[:, None, :D]) + modulation[:, None, D:]).astype(jnp.bfloat16)
    rows = rows.reshape(groups * tokc, D)
    query = jnp.dot(rows, w_query, preferred_element_type=jnp.float32).astype(jnp.bfloat16).reshape(groups, tokc, HEADS, HD)
    keys = jnp.dot(rows, w_key, preferred_element_type=jnp.float32).astype(jnp.bfloat16).reshape(groups, tokc, HEADS, HD)
    values = jnp.dot(rows, w_value, preferred_element_type=jnp.float32).astype(jnp.bfloat16).reshape(groups, tokc, HEADS, HD)
    same_clip = segment_ids[:, None] == segment_ids[None, :]
    inverse = 1.0 / math.sqrt(HD)
    outputs = []
    for group in range(groups):
        key_rows = keys[:group + 1].reshape((group + 1) * tokc, HEADS, HD).astype(jnp.float32)
        value_rows = values[:group + 1].reshape((group + 1) * tokc, HEADS, HD).astype(jnp.float32)
        allowed = jnp.tile(same_clip, (1, group + 1))
        scores = jnp.einsum('thd,khd->htk', query[group].astype(jnp.float32), key_rows) * inverse
        scores = jnp.where(allowed[None], scores, -1e+30)
        highest = lax.optimization_barrier(jnp.max(scores, axis=-1, keepdims=True))
        weights = jnp.where(allowed[None], jnp.exp(scores - highest), 0.0)
        total = lax.optimization_barrier(jnp.sum(weights, axis=-1))
        rounded = lax.optimization_barrier(weights.astype(jnp.bfloat16))
        summed = jnp.einsum('htk,khd->thd', rounded.astype(jnp.float32), value_rows)
        result = summed / jnp.transpose(total)[:, :, None]
        outputs.append(result.reshape(tokc, HEADS * HD).astype(jnp.bfloat16))
    return jnp.stack(outputs)
```

```python
import functools
import math

import jax
import jax.numpy as jnp
from jax import lax
from jax.experimental import pallas as pl
from jax.experimental.pallas import tpu as pltpu
from jax.sharding import PartitionSpec as P

HD = 128
CHUNKS = 2
VMEM = pltpu.MemorySpace.VMEM
BIG = 100 * 1024 * 1024 // 2


def params():
    return pltpu.CompilerParams(vmem_limit_bytes=BIG)


def modulate_kernel(steps, x_ref, table_ref, *outs):
    x = x_ref[...].astype(jnp.float32)
    scale = lax.rsqrt(jnp.mean(x * x, axis=-1, keepdims=True) + 1e-06)
    rows = (x * scale * (1.0 + table_ref[0, 0:1]) + table_ref[0, 1:2]).astype(jnp.bfloat16)
    width = outs[0].shape[1]
    for index, out in enumerate(outs):
        out[...] = rows[:, index * width : (index + 1) * width]


def modulate(latents, steps, mod_table):
    rows, depth = latents.shape
    width = depth // CHUNKS
    return pl.pallas_call(
        modulate_kernel,
        grid_spec=pltpu.PrefetchScalarGridSpec(
            num_scalar_prefetch=1,
            grid=(1,),
            in_specs=[
                pl.BlockSpec((rows, depth), lambda i, steps: (0, 0)),
                pl.BlockSpec((1, 2, depth), lambda i, steps: (steps[0], 0, 0)),
            ],
            out_specs=[pl.BlockSpec((rows, width), lambda i, steps: (0, 0))] * CHUNKS,
        ),
        out_shape=[jax.ShapeDtypeStruct((rows, width), jnp.bfloat16)] * CHUNKS,
        compiler_params=params(),
        name="modulate",
    )(steps, latents, mod_table)


def project_kernel(places, first, last, *refs):
    pieces, refs = refs[: len(places)], refs[len(places) :]
    weights, refs = refs[:3], refs[3:]
    if not first:
        start, refs = refs[0], refs[1:]
    width = weights[0].shape[1]
    depth = pieces[0].shape[1]
    for index, weight in enumerate(weights):
        total = None if first else start[:, index * width : (index + 1) * width]
        for place, piece in zip(places, pieces):
            part = jnp.dot(
                piece[...],
                weight[place * depth : (place + 1) * depth, :],
                preferred_element_type=jnp.float32,
            )
            total = part if total is None else total + part
        if not last:
            refs[0][:, index * width : (index + 1) * width] = total
        elif index == 0:
            refs[0][...] = total.astype(jnp.bfloat16)
        else:
            refs[1][:, (index - 1) * width : index * width] = total.astype(jnp.bfloat16)


def project(pieces, places, weights, start, last):
    rows = pieces[0].shape[0]
    width = weights[0].shape[1]
    if last:
        shapes = [
            jax.ShapeDtypeStruct((rows, width), jnp.bfloat16),
            jax.ShapeDtypeStruct((rows, 2 * width), jnp.bfloat16),
        ]
    else:
        shapes = [jax.ShapeDtypeStruct((rows, 3 * width), jnp.float32)]
    extra = [] if start is None else [start]
    whole = pl.BlockSpec(memory_space=VMEM)
    return pl.pallas_call(
        functools.partial(project_kernel, tuple(places), start is None, last),
        in_specs=[whole] * (len(pieces) + 3 + len(extra)),
        out_specs=[whole] * len(shapes),
        out_shape=shapes,
        compiler_params=params(),
        name="project",
    )(*pieces, *weights, *extra)


def attend_kernel(shards, sources, mine, seg_col, seg_row, *refs):
    queries, refs = refs[:shards], refs[shards:]
    early, refs = refs[:sources], refs[sources:]
    late, refs = refs[:sources], refs[sources:]
    outs, (q_all, kv_all) = refs[:shards], refs[shards:]
    rows, width = queries[0].shape
    heads = width // HD
    tokc = rows * shards
    many = early[0].shape[0]
    for s in range(shards):
        q_all[s * rows : (s + 1) * rows, :] = queries[s][...]
    for m in range(sources):
        kv_all[m * tokc : m * tokc + many, :] = early[m][...]
        kv_all[m * tokc + many : (m + 1) * tokc, :] = late[m][...]
    here = mine[0]
    column = lax.broadcasted_iota(jnp.int32, (1, tokc), 1)
    clip = []
    for m in range(sources):
        usable = jnp.where((here ^ m) <= here, 0, 1000)
        clip.append(seg_row[...] + usable + column * 0)
    clip = jnp.concatenate(clip, axis=1)
    inverse = 1.0 / math.sqrt(HD)
    block = min(tokc, 128)
    for b in range(tokc // block):
        span = slice(b * block, (b + 1) * block)
        allowed = seg_col[span, :] == clip
        for h in range(heads):
            cols = slice(h * HD, (h + 1) * HD)
            vcols = slice(width + h * HD, width + (h + 1) * HD)
            scores = lax.dot_general(
                q_all[span, cols],
                kv_all[:, cols],
                (((1,), (1,)), ((), ())),
                preferred_element_type=jnp.float32,
            )
            scores = jnp.where(allowed, scores * inverse, -1e30)
            best = jnp.max(scores, axis=-1, keepdims=True)
            weights = jnp.where(allowed, jnp.exp(scores - best), 0.0)
            total = jnp.sum(weights, axis=-1, keepdims=True)
            summed = jnp.dot(
                weights.astype(jnp.bfloat16), kv_all[:, vcols], preferred_element_type=jnp.float32
            )
            result = (summed / total).astype(jnp.bfloat16)
            for s in range(block // rows):
                outs[b * (block // rows) + s][:, cols] = result[s * rows : (s + 1) * rows]


def attend(mine, segments, queries, early, late):
    shards, sources = len(queries), len(early)
    rows, width = queries[0].shape
    tokc = rows * shards
    whole = pl.BlockSpec(memory_space=VMEM)
    return pl.pallas_call(
        functools.partial(attend_kernel, shards, sources),
        in_specs=[pl.BlockSpec(memory_space=pltpu.MemorySpace.SMEM)]
        + [whole] * (2 + shards + 2 * sources),
        out_specs=[whole] * shards,
        out_shape=[jax.ShapeDtypeStruct((rows, width), jnp.bfloat16)] * shards,
        scratch_shapes=[
            pltpu.VMEM((tokc, width), jnp.bfloat16),
            pltpu.VMEM((sources * tokc, 2 * width), jnp.bfloat16),
        ],
        compiler_params=params(),
        name="attend",
    )(mine, segments[:, None], segments[None, :], *queries, *early, *late)


def place_kernel(place, *refs):
    pieces, out = refs[:-1], refs[-1]
    width = pieces[0].shape[1]
    count = len(pieces)
    for s, piece in enumerate(pieces):
        column = lax.rem(place[0] + s, count) * width
        out[0, :, pl.ds(pl.multiple_of(column, width), width)] = piece[...]


def place_columns(place, pieces):
    rows, width = pieces[0].shape
    whole = pl.BlockSpec(memory_space=VMEM)
    return pl.pallas_call(
        place_kernel,
        in_specs=[pl.BlockSpec(memory_space=pltpu.MemorySpace.SMEM)] + [whole] * len(pieces),
        out_specs=whole,
        out_shape=jax.ShapeDtypeStruct((1, rows, width * len(pieces)), jnp.bfloat16),
        compiler_params=params(),
        name="place",
    )(place, *pieces)


def share(block, groups):
    held = {0: block}
    for m in range(2, groups, 2):
        held[m] = lax.ppermute(block, "group", [(i, i ^ m) for i in range(groups)])
    for m in range(0, groups, 2):
        held[m + 1] = lax.ppermute(held[m], "group", [(i, i ^ 1) for i in range(groups)])
    return [held[m] for m in range(groups)]


def per_device(latents, steps, segment_ids, mod_table, w_query, w_key, w_value):
    shards = lax.axis_size("dp")
    groups = lax.axis_size("group")
    rows = latents.shape[1]
    place = lax.axis_index("dp").astype(jnp.int32)
    mine = lax.axis_index("group").astype(jnp.int32)
    ring = [(i, (i + 1) % shards) for i in range(shards)]

    weights = [pltpu.with_memory_space_constraint(w, VMEM) for w in (w_query, w_key, w_value)]
    pieces = modulate(latents[0], steps, mod_table)
    arrived = [list(pieces)]
    for s in range(1, shards):
        arrived.append([lax.ppermute(piece, "dp", ring) for piece in arrived[-1]])

    order = [lax.rem(place - s + shards, shards) for s in range(shards)]
    segments = jnp.concatenate(
        [lax.dynamic_slice_in_dim(segment_ids, o * rows, rows) for o in order]
    )

    queries, shared = [], []
    for s in range(shards):
        if s < shards - 1:
            query, keyval = project(arrived[s], range(CHUNKS), weights, None, True)
        else:
            start = project(arrived[s][:-1], range(CHUNKS - 1), weights, None, False)[0]
            query, keyval = project(arrived[s][-1:], [CHUNKS - 1], weights, start, True)
        queries.append(query)
        shared.append(keyval)
    early = share(jnp.concatenate(shared[:-1], axis=0), groups)
    late = share(shared[-1], groups)
    results = attend(mine[None], segments, queries, early, late)
    landed = [results[0]]
    for s in range(1, shards):
        landed.append(
            lax.ppermute(results[s], "dp", [(i, (i - s) % shards) for i in range(shards)])
        )
    return place_columns(place[None], landed)


def solution(mesh):
    placed = (
        P("group", "dp", None),
        P("group"),
        P(),
        P(),
        P(None, "dp"),
        P(None, "dp"),
        P(None, "dp"),
    )
    return jax.shard_map(
        per_device, mesh=mesh, in_specs=placed, out_specs=P("group", "dp", None), check_vma=False
    )
```

```python
import functools
import math

import jax
import jax.numpy as jnp
from jax import lax
from jax.experimental import pallas as pl
from jax.experimental.pallas import tpu as pltpu
from jax.sharding import PartitionSpec as P

HD = 128
CHUNKS = 3
VMEM = pltpu.MemorySpace.VMEM
HBM = pltpu.MemorySpace.HBM
SMEM = pltpu.MemorySpace.SMEM
IN_VMEM = pl.BlockSpec(memory_space=VMEM)
IN_HBM = pl.BlockSpec(memory_space=HBM)
IN_SMEM = pl.BlockSpec(memory_space=SMEM)


def params(mebibytes):
    return pltpu.CompilerParams(vmem_limit_bytes=mebibytes * 1024 * 1024)


def near(*arrays):
    return [pltpu.with_memory_space_constraint(a, VMEM) for a in arrays]


def far(*arrays):
    return [pltpu.with_memory_space_constraint(a, HBM) for a in arrays]


def modulate_kernel(chunks, steps_ref, x_hbm, table_hbm, *refs):
    outs, (x_ref, table, steps, sems) = refs[:chunks], refs[chunks:]
    copies = [
        pltpu.make_async_copy(x_hbm.at[0], x_ref, sems.at[0]),
        pltpu.make_async_copy(table_hbm, table, sems.at[1]),
        pltpu.make_async_copy(steps_ref, steps, sems.at[2]),
    ]
    for copy in copies:
        copy.start()
    for copy in copies:
        copy.wait()
    x = x_ref[...].astype(jnp.float32)
    scale = lax.rsqrt(jnp.mean(x * x, axis=-1, keepdims=True) + 1e-06)
    mod = table[steps[0, 0]]
    rows = (x * scale * (1.0 + mod[0:1]) + mod[1:2]).astype(jnp.bfloat16)
    width = outs[0].shape[1]
    for index, out in enumerate(outs):
        out[...] = rows[:, index * width : (index + 1) * width]


def modulate(latents, steps, mod_table):
    _, rows, depth = latents.shape
    width = depth // CHUNKS
    return pl.pallas_call(
        functools.partial(modulate_kernel, CHUNKS),
        in_specs=[pl.BlockSpec((1, 1)), IN_HBM, IN_HBM],
        out_specs=[IN_VMEM] * CHUNKS,
        out_shape=[VMEM((rows, width), jnp.bfloat16)] * CHUNKS,
        scratch_shapes=[
            pltpu.VMEM((rows, depth), jnp.bfloat16),
            pltpu.VMEM(mod_table.shape, jnp.float32),
            pltpu.SMEM((1, 1), jnp.int32),
            pltpu.SemaphoreType.DMA((3,)),
        ],
        compiler_params=params(4),
        name="modulate",
    )(steps[None], *far(latents, mod_table))


def load_kernel(shards, place, segments, *refs):
    sources, outs, (seg_col, seg_row, sems) = refs[:3], refs[3:6], refs[6:]
    copies = [pltpu.make_async_copy(sources[i], outs[i], sems.at[i]) for i in range(3)]
    for copy in copies:
        copy.start()
    tokc = segments.shape[1]
    rows = tokc // shards

    def owner(position):
        shard = place[0] - position // rows
        return jnp.where(shard < 0, shard + shards, shard) * rows + position % rows

    down = lax.broadcasted_iota(jnp.int32, (tokc, tokc), 0)
    across = lax.broadcasted_iota(jnp.int32, (tokc, tokc), 1)
    natural = segments[...]
    column = jnp.sum(jnp.where(down == across, natural, 0), axis=1, keepdims=True)
    seg_col[...] = jnp.sum(jnp.where(owner(down) == across, natural, 0), axis=1, keepdims=True)
    seg_row[...] = jnp.sum(jnp.where(owner(across) == down, column, 0), axis=0, keepdims=True)
    for copy in copies:
        copy.wait()


def load(weights, segments, place, shards):
    tokc = segments.shape[0]
    return pl.pallas_call(
        functools.partial(load_kernel, shards),
        in_specs=[IN_SMEM, pl.BlockSpec((1, tokc))] + [IN_HBM] * 3,
        out_specs=[IN_VMEM] * 5,
        out_shape=[VMEM(w.shape, w.dtype) for w in weights]
        + [VMEM((tokc, 1), jnp.int32), VMEM((1, tokc), jnp.int32)],
        scratch_shapes=[pltpu.SemaphoreType.DMA((3,))],
        compiler_params=params(2 + tokc * tokc * 32 // 2**20),
        name="load",
    )(place, segments[None], *far(*weights))


def project_kernel(places, first, last, before, *refs):
    pieces, refs = refs[: len(places)], refs[len(places) :]
    weights, refs = refs[:3], refs[3:]
    if not first:
        start, refs = refs[0], refs[1:]
    older, refs = refs[:before], refs[before:]
    width = weights[0].shape[1]
    rows, depth = pieces[0].shape
    for s in range(before):
        refs[1][s * rows : (s + 1) * rows, :] = older[s][...]
    for index, weight in enumerate(weights):
        total = None if first else start[:, index * width : (index + 1) * width]
        for place, piece in zip(places, pieces):
            part = jnp.dot(
                piece[...],
                weight[place * depth : (place + 1) * depth, :],
                preferred_element_type=jnp.float32,
            )
            total = part if total is None else total + part
        if not last:
            refs[0][:, index * width : (index + 1) * width] = total
        elif index == 0:
            refs[0][...] = total.astype(jnp.bfloat16)
        else:
            refs[1][before * rows :, (index - 1) * width : index * width] = total.astype(
                jnp.bfloat16
            )


def project(pieces, places, weights, start, last, older=()):
    rows = pieces[0].shape[0]
    width = weights[0].shape[1]
    if last:
        shapes = [
            VMEM((rows, width), jnp.bfloat16),
            VMEM((rows * (len(older) + 1), 2 * width), jnp.bfloat16),
        ]
    else:
        shapes = [VMEM((rows, 3 * width), jnp.float32)]
    extra = ([] if start is None else [start]) + list(older)
    return pl.pallas_call(
        functools.partial(project_kernel, tuple(places), start is None, last, len(older)),
        in_specs=[IN_VMEM] * (len(pieces) + 3 + len(extra)),
        out_specs=[IN_VMEM] * len(shapes),
        out_shape=shapes,
        compiler_params=params(2),
        name="project",
    )(*near(*pieces, *weights, *extra))


def attend_kernel(shards, sources, mine, seg_col, seg_row, *refs):
    queries, refs = refs[:shards], refs[shards:]
    early, refs = refs[:sources], refs[sources:]
    late, refs = refs[:sources], refs[sources:]
    outs, (q_all, kv_all) = refs[:shards], refs[shards:]
    rows, width = queries[0].shape
    heads = width // HD
    tokc = rows * shards
    many = early[0].shape[0]
    for s in range(shards):
        q_all[s * rows : (s + 1) * rows, :] = queries[s][...]
    for m in range(sources):
        kv_all[m * tokc : m * tokc + many, :] = early[m][...]
        kv_all[m * tokc + many : (m + 1) * tokc, :] = late[m][...]
    here = mine[0]
    clip = []
    for m in range(sources):
        usable = jnp.where((here ^ m) <= here, 0, 1000)
        clip.append(seg_row[...] + usable)
    clip = jnp.concatenate(clip, axis=1)
    inverse = 1.0 / math.sqrt(HD)
    block = min(tokc, 128)
    for b in range(tokc // block):
        span = slice(b * block, (b + 1) * block)
        allowed = seg_col[span, :] == clip
        for h in range(heads):
            cols = slice(h * HD, (h + 1) * HD)
            vcols = slice(width + h * HD, width + (h + 1) * HD)
            scores = lax.dot_general(
                q_all[span, cols],
                kv_all[:, cols],
                (((1,), (1,)), ((), ())),
                preferred_element_type=jnp.float32,
            )
            scores = jnp.where(allowed, scores * inverse, -1e30)
            best = jnp.max(scores, axis=-1, keepdims=True)
            weights = jnp.where(allowed, jnp.exp(scores - best), 0.0)
            total = jnp.sum(weights, axis=-1, keepdims=True)
            summed = jnp.dot(
                weights.astype(jnp.bfloat16), kv_all[:, vcols], preferred_element_type=jnp.float32
            )
            result = (summed / total).astype(jnp.bfloat16)
            for s in range(block // rows):
                outs[b * (block // rows) + s][:, cols] = result[s * rows : (s + 1) * rows]


def attend(mine, seg_col, seg_row, queries, early, late):
    shards, sources = len(queries), len(early)
    rows, width = queries[0].shape
    tokc = rows * shards
    return pl.pallas_call(
        functools.partial(attend_kernel, shards, sources),
        in_specs=[IN_SMEM] + [IN_VMEM] * (2 + shards + 2 * sources),
        out_specs=[IN_VMEM] * shards,
        out_shape=[VMEM((rows, width), jnp.bfloat16)] * shards,
        scratch_shapes=[
            pltpu.VMEM((tokc, width), jnp.bfloat16),
            pltpu.VMEM((sources * tokc, 2 * width), jnp.bfloat16),
        ],
        compiler_params=params(3 + sources * tokc * 8 // 2048),
        name="attend",
    )(mine, *near(seg_col, seg_row, *queries, *early, *late))


def place_kernel(place, *refs):
    pieces, out = refs[:-1], refs[-1]
    width = pieces[0].shape[1]
    count = len(pieces)
    for s, piece in enumerate(pieces):
        column = lax.rem(place[0] + s, count) * width
        out[0, :, pl.ds(pl.multiple_of(column, width), width)] = piece[...]


def place_columns(place, pieces):
    rows, width = pieces[0].shape
    return pl.pallas_call(
        place_kernel,
        in_specs=[IN_SMEM] + [IN_VMEM] * len(pieces),
        out_specs=IN_VMEM,
        out_shape=jax.ShapeDtypeStruct((1, rows, width * len(pieces)), jnp.bfloat16),
        compiler_params=params(2),
        name="place",
    )(place, *near(*pieces))


def share(block, groups):
    held = {0: block}
    for m in range(2, groups, 2):
        held[m] = lax.ppermute(block, "group", [(i, i ^ m) for i in range(groups)])
    for m in range(0, groups, 2):
        held[m + 1] = lax.ppermute(held[m], "group", [(i, i ^ 1) for i in range(groups)])
    return [held[m] for m in range(groups)]


def per_device(latents, steps, segment_ids, mod_table, w_query, w_key, w_value):
    shards = lax.axis_size("dp")
    groups = lax.axis_size("group")
    rows = latents.shape[1]
    place = lax.axis_index("dp").astype(jnp.int32)
    mine = lax.axis_index("group").astype(jnp.int32)
    ring = [(i, (i + 1) % shards) for i in range(shards)]

    pieces = list(modulate(latents, steps, mod_table))
    *weights, seg_col, seg_row = load(
        (w_query, w_key, w_value), segment_ids, place[None], shards
    )
    moved = [lax.ppermute(piece, "dp", ring) for piece in pieces]
    queries, shared, early = [], [], None
    for s in range(shards - 1):
        if s == shards - 2:
            early = share(shared[-1], groups)
            moved[0], pieces, early = lax.optimization_barrier((moved[0], pieces, early))
            shared = []
        older = shared if s == shards - 3 else ()
        query, keyval = project(pieces, range(CHUNKS), weights, None, True, older)
        queries.append(query)
        shared.append(keyval)
        pieces = moved
        if s < shards - 2:
            first, keyval = lax.optimization_barrier((moved[0], keyval))
            shared[-1] = keyval
            moved = [lax.ppermute(piece, "dp", ring) for piece in [first] + moved[1:]]
    start = project(pieces[:-1], range(CHUNKS - 1), weights, None, False)[0]
    query, keyval = project(pieces[-1:], [CHUNKS - 1], weights, start, True, shared)
    queries.append(query)
    late = share(keyval, groups)
    results = attend(mine[None], seg_col, seg_row, queries, early, late)
    landed = [results[0]]
    for s in range(1, shards):
        landed.append(
            lax.ppermute(results[s], "dp", [(i, (i - s) % shards) for i in range(shards)])
        )
    return place_columns(place[None], landed)


def solution(mesh):
    placed = (
        P("group", "dp", None),
        P("group"),
        P(),
        P(),
        P(None, "dp"),
        P(None, "dp"),
        P(None, "dp"),
    )
    return jax.shard_map(
        per_device, mesh=mesh, in_specs=placed, out_specs=P("group", "dp", None), check_vma=False
    )
```

```python
import functools
import math

import jax
import jax.numpy as jnp
from jax import lax
from jax.experimental import pallas as pl
from jax.experimental.pallas import tpu as pltpu
from jax.sharding import PartitionSpec as P

HD = 128
CHUNKS = 2
VMEM = pltpu.MemorySpace.VMEM
HBM = pltpu.MemorySpace.HBM
SMEM = pltpu.MemorySpace.SMEM
IN_VMEM = pl.BlockSpec(memory_space=VMEM)
IN_HBM = pl.BlockSpec(memory_space=HBM)
IN_SMEM = pl.BlockSpec(memory_space=SMEM)


def params(mebibytes):
    return pltpu.CompilerParams(vmem_limit_bytes=mebibytes * 1024 * 1024)


def near(*arrays):
    return [pltpu.with_memory_space_constraint(a, VMEM) for a in arrays]


def far(*arrays):
    return [pltpu.with_memory_space_constraint(a, HBM) for a in arrays]


def modulate_kernel(chunks, steps_ref, x_hbm, table_hbm, *refs):
    outs, (x_ref, table, steps, sems) = refs[:chunks], refs[chunks:]
    copies = [
        pltpu.make_async_copy(x_hbm.at[0], x_ref, sems.at[0]),
        pltpu.make_async_copy(table_hbm, table, sems.at[1]),
        pltpu.make_async_copy(steps_ref, steps, sems.at[2]),
    ]
    for copy in copies:
        copy.start()
    for copy in copies:
        copy.wait()
    x = x_ref[...].astype(jnp.float32)
    scale = lax.rsqrt(jnp.mean(x * x, axis=-1, keepdims=True) + 1e-06)
    mod = table[steps[0]]
    rows = (x * scale * (1.0 + mod[0:1]) + mod[1:2]).astype(jnp.bfloat16)
    width = outs[0].shape[1]
    for index, out in enumerate(outs):
        out[...] = rows[:, index * width : (index + 1) * width]


def modulate(latents, steps, mod_table):
    _, rows, depth = latents.shape
    width = depth // CHUNKS
    return pl.pallas_call(
        functools.partial(modulate_kernel, CHUNKS),
        in_specs=[IN_HBM, IN_HBM, IN_HBM],
        out_specs=[IN_VMEM] * CHUNKS,
        out_shape=[VMEM((rows, width), jnp.bfloat16)] * CHUNKS,
        scratch_shapes=[
            pltpu.VMEM((rows, depth), jnp.bfloat16),
            pltpu.VMEM(mod_table.shape, jnp.float32),
            pltpu.SMEM((1,), jnp.int32),
            pltpu.SemaphoreType.DMA((3,)),
        ],
        compiler_params=params(4),
        name="modulate",
    )(steps, *far(latents, mod_table))


def begin_kernel(shards, place, segments, *refs):
    sources, refs = refs[:3], refs[3:]
    pieces, refs = refs[:CHUNKS], refs[CHUNKS:]
    query, keyval = refs[:2]
    outs, (seg_col, seg_row, sems) = refs[2:5], refs[5:]
    depth = pieces[0].shape[1]
    width = query.shape[1]
    spans = [slice(k * depth, (k + 1) * depth) for k in range(CHUNKS)]
    copies = [
        [
            pltpu.make_async_copy(sources[i].at[span], outs[i].at[span], sems.at[i, k])
            for k, span in enumerate(spans)
        ]
        for i in range(3)
    ]
    for column in copies:
        for copy in column:
            copy.start()
    tokc = segments.shape[1]
    rows = tokc // shards

    def owner(position):
        shard = place[0] - position // rows
        return jnp.where(shard < 0, shard + shards, shard) * rows + position % rows

    down = lax.broadcasted_iota(jnp.int32, (tokc, tokc), 0)
    across = lax.broadcasted_iota(jnp.int32, (tokc, tokc), 1)
    natural = segments[...]
    column = jnp.sum(jnp.where(down == across, natural, 0), axis=1, keepdims=True)
    seg_col[...] = jnp.sum(jnp.where(owner(down) == across, natural, 0), axis=1, keepdims=True)
    seg_row[...] = jnp.sum(jnp.where(owner(across) == down, column, 0), axis=0, keepdims=True)
    for i in range(3):
        total = None
        for k, span in enumerate(spans):
            copies[i][k].wait()
            part = jnp.dot(pieces[k][...], outs[i][span], preferred_element_type=jnp.float32)
            total = part if total is None else total + part
        if i == 0:
            query[...] = total.astype(jnp.bfloat16)
        else:
            keyval[:, (i - 1) * width : i * width] = total.astype(jnp.bfloat16)


def begin(weights, segments, pieces, place, shards):
    tokc = segments.shape[0]
    rows = pieces[0].shape[0]
    width = weights[0].shape[1]
    return pl.pallas_call(
        functools.partial(begin_kernel, shards),
        in_specs=[IN_SMEM, pl.BlockSpec((1, tokc))] + [IN_HBM] * 3 + [IN_VMEM] * CHUNKS,
        out_specs=[IN_VMEM] * 7,
        out_shape=[VMEM((rows, width), jnp.bfloat16), VMEM((rows, 2 * width), jnp.bfloat16)]
        + [VMEM(w.shape, w.dtype) for w in weights]
        + [VMEM((tokc, 1), jnp.int32), VMEM((1, tokc), jnp.int32)],
        scratch_shapes=[pltpu.SemaphoreType.DMA((3, CHUNKS))],
        compiler_params=params(2 + tokc * tokc * 32 // 2**20),
        name="begin",
    )(place, segments[None], *far(*weights), *near(*pieces))


def project_kernel(count, places, first, last, older, *refs):
    pieces, refs = refs[: count * len(places)], refs[count * len(places) :]
    weights, refs = refs[:3], refs[3:]
    if not first:
        start, refs = refs[0], refs[1:]
    if older:
        before, refs = refs[0], refs[1:]
        refs[1][:older, :] = before[...]
    width = weights[0].shape[1]
    depth = pieces[0].shape[1]
    stacked = [
        jnp.concatenate([pieces[s * len(places) + k][...] for s in range(count)], axis=0)
        for k in range(len(places))
    ]
    for index, weight in enumerate(weights):
        total = None if first else start[:, index * width : (index + 1) * width]
        for k, place in enumerate(places):
            part = jnp.dot(
                stacked[k],
                weight[place * depth : (place + 1) * depth, :],
                preferred_element_type=jnp.float32,
            )
            total = part if total is None else total + part
        if not last:
            refs[0][:, index * width : (index + 1) * width] = total
        elif index == 0:
            refs[0][...] = total.astype(jnp.bfloat16)
        else:
            refs[1][older:, (index - 1) * width : index * width] = total.astype(jnp.bfloat16)


def project(shard_pieces, places, weights, start, last, before=None):
    count = len(shard_pieces)
    rows = shard_pieces[0][0].shape[0] * count
    older = 0 if before is None else before.shape[0]
    width = weights[0].shape[1]
    if last:
        shapes = [
            VMEM((rows, width), jnp.bfloat16),
            VMEM((older + rows, 2 * width), jnp.bfloat16),
        ]
    else:
        shapes = [VMEM((rows, 3 * width), jnp.float32)]
    pieces = [piece for shard in shard_pieces for piece in shard]
    extra = [array for array in (start, before) if array is not None]
    return pl.pallas_call(
        functools.partial(project_kernel, count, tuple(places), start is None, last, older),
        in_specs=[IN_VMEM] * (len(pieces) + 3 + len(extra)),
        out_specs=[IN_VMEM] * len(shapes),
        out_shape=shapes,
        compiler_params=params(3 + count),
        name="project",
    )(*near(*pieces, *weights, *extra))


def attend_kernel(shards, parts, sources, mine, seg_col, seg_row, *refs):
    queries, refs = refs[:parts], refs[parts:]
    early, refs = refs[:sources], refs[sources:]
    late, refs = refs[:sources], refs[sources:]
    outs, (q_all, kv_all) = refs[:shards], refs[shards:]
    tokc, width = q_all.shape
    rows = tokc // shards
    heads = width // HD
    many = early[0].shape[0]
    filled = 0
    for query in queries:
        q_all[filled : filled + query.shape[0], :] = query[...]
        filled += query.shape[0]
    for m in range(sources):
        kv_all[m * tokc : m * tokc + many, :] = early[m][...]
        kv_all[m * tokc + many : (m + 1) * tokc, :] = late[m][...]
    here = mine[0]
    clip = []
    for m in range(sources):
        usable = jnp.where((here ^ m) <= here, 0, 1000)
        clip.append(seg_row[...] + usable)
    clip = jnp.concatenate(clip, axis=1)
    inverse = 1.0 / math.sqrt(HD)
    block = min(tokc, 128)
    for b in range(tokc // block):
        span = slice(b * block, (b + 1) * block)
        allowed = seg_col[span, :] == clip
        for h in range(heads):
            cols = slice(h * HD, (h + 1) * HD)
            vcols = slice(width + h * HD, width + (h + 1) * HD)
            scores = lax.dot_general(
                q_all[span, cols],
                kv_all[:, cols],
                (((1,), (1,)), ((), ())),
                preferred_element_type=jnp.float32,
            )
            scores = jnp.where(allowed, scores * inverse, -1e30)
            best = jnp.max(scores, axis=-1, keepdims=True)
            weights = jnp.where(allowed, jnp.exp(scores - best), 0.0)
            total = jnp.sum(weights, axis=-1, keepdims=True)
            summed = jnp.dot(
                weights.astype(jnp.bfloat16), kv_all[:, vcols], preferred_element_type=jnp.float32
            )
            result = (summed / total).astype(jnp.bfloat16)
            for s in range(block // rows):
                outs[b * (block // rows) + s][:, cols] = result[s * rows : (s + 1) * rows]


def attend(shards, mine, seg_col, seg_row, queries, early, late):
    sources = len(early)
    width = queries[0].shape[1]
    tokc = seg_col.shape[0]
    rows = tokc // shards
    return pl.pallas_call(
        functools.partial(attend_kernel, shards, len(queries), sources),
        in_specs=[IN_SMEM] + [IN_VMEM] * (2 + len(queries) + 2 * sources),
        out_specs=[IN_VMEM] * shards,
        out_shape=[VMEM((rows, width), jnp.bfloat16)] * shards,
        scratch_shapes=[
            pltpu.VMEM((tokc, width), jnp.bfloat16),
            pltpu.VMEM((sources * tokc, 2 * width), jnp.bfloat16),
        ],
        compiler_params=params(3 + sources * tokc * 8 // 2048),
        name="attend",
    )(mine, *near(seg_col, seg_row, *queries, *early, *late))


def place_kernel(place, *refs):
    pieces, out = refs[:-1], refs[-1]
    width = pieces[0].shape[1]
    count = len(pieces)
    for s, piece in enumerate(pieces):
        column = lax.rem(place[0] + s, count) * width
        out[0, :, pl.ds(pl.multiple_of(column, width), width)] = piece[...]


def place_columns(place, pieces):
    rows, width = pieces[0].shape
    return pl.pallas_call(
        place_kernel,
        in_specs=[IN_SMEM] + [IN_VMEM] * len(pieces),
        out_specs=IN_VMEM,
        out_shape=jax.ShapeDtypeStruct((1, rows, width * len(pieces)), jnp.bfloat16),
        compiler_params=params(2),
        name="place",
    )(place, *near(*pieces))


def across_chips(block, groups):
    return [block] + [
        lax.ppermute(block, "group", [(i, i ^ m) for i in range(groups)])
        for m in range(2, groups, 2)
    ]


def across_cores(held, groups):
    swap = [(i, i ^ 1) for i in range(groups)]
    return [each for block in held for each in (block, lax.ppermute(block, "group", swap))]


def per_device(latents, steps, segment_ids, mod_table, w_query, w_key, w_value):
    shards = lax.axis_size("dp")
    groups = lax.axis_size("group")
    rows = latents.shape[1]
    place = lax.axis_index("dp").astype(jnp.int32)
    mine = lax.axis_index("group").astype(jnp.int32)
    ring = [(i, (i + 1) % shards) for i in range(shards)]

    pieces = list(modulate(latents, steps, mod_table))
    query, keyval, *rest = begin(
        (w_query, w_key, w_value), segment_ids, pieces, place[None], shards
    )
    weights, (seg_col, seg_row) = rest[:3], rest[3:]
    queries = [query]
    pieces = [lax.ppermute(piece, "dp", ring) for piece in pieces]
    pieces[0], keyval = lax.optimization_barrier((pieces[0], keyval))
    arrived = []
    for s in range(1, shards - 2):
        arrived.append(pieces)
        pieces = [lax.ppermute(piece, "dp", ring) for piece in pieces]
    query, keyval = project(arrived, range(CHUNKS), weights, None, True, keyval)
    queries.append(query)
    early = across_chips(keyval, groups)
    pieces[-1], early = lax.optimization_barrier((pieces[-1], early))
    early = across_cores(early, groups)
    moved = [lax.ppermute(piece, "dp", ring) for piece in pieces]
    moved[0], early = lax.optimization_barrier((moved[0], early))
    query, keyval = project([pieces], range(CHUNKS), weights, None, True)
    queries.append(query)
    start = project([moved[:-1]], range(CHUNKS - 1), weights, None, False)[0]
    query, keyval = project([moved[-1:]], [CHUNKS - 1], weights, start, True, keyval)
    queries.append(query)
    late = across_cores(across_chips(keyval, groups), groups)
    results = attend(shards, mine[None], seg_col, seg_row, queries, early, late)
    landed = [results[0]]
    for s in range(1, shards):
        landed.append(
            lax.ppermute(results[s], "dp", [(i, (i - s) % shards) for i in range(shards)])
        )
    return place_columns(place[None], landed)


def solution(mesh):
    placed = (
        P("group", "dp", None),
        P("group"),
        P(),
        P(),
        P(None, "dp"),
        P(None, "dp"),
        P(None, "dp"),
    )
    return jax.shard_map(
        per_device, mesh=mesh, in_specs=placed, out_specs=P("group", "dp", None), check_vma=False
    )
```

```python
import functools
import math

import jax
import jax.numpy as jnp
from jax import lax
from jax.experimental import pallas as pl
from jax.experimental.pallas import tpu as pltpu
from jax.sharding import PartitionSpec as P

HD = 128
LANES = 128
CHUNKS = 2
PARTS = 2
AHEAD = 6
VMEM = pltpu.MemorySpace.VMEM
HBM = pltpu.MemorySpace.HBM
SMEM = pltpu.MemorySpace.SMEM
IN_VMEM = pl.BlockSpec(memory_space=VMEM)
IN_HBM = pl.BlockSpec(memory_space=HBM)
IN_SMEM = pl.BlockSpec(memory_space=SMEM)


def params(mebibytes):
    return pltpu.CompilerParams(vmem_limit_bytes=mebibytes * 1024 * 1024)


def near(*arrays):
    return [pltpu.with_memory_space_constraint(a, VMEM) for a in arrays]


def far(*arrays):
    return [pltpu.with_memory_space_constraint(a, HBM) for a in arrays]


def split_kernel(x_hbm, *refs):
    outs, (x_ref, sem) = refs[:CHUNKS], refs[CHUNKS:]
    copy = pltpu.make_async_copy(x_hbm.at[0], x_ref, sem)
    copy.start()
    copy.wait()
    width = outs[-1].shape[1]
    for index, out in enumerate(outs):
        out[:, :width] = x_ref[:, index * width : (index + 1) * width]
    x = x_ref[...].astype(jnp.float32)
    scale = lax.rsqrt(jnp.mean(x * x, axis=-1, keepdims=True) + 1e-06)
    high = scale.astype(jnp.bfloat16).astype(jnp.float32)
    middle = (scale - high).astype(jnp.bfloat16).astype(jnp.float32)
    lane = lax.broadcasted_iota(jnp.int32, (x.shape[0], LANES), 1)
    parts = jnp.where(lane == 0, high, jnp.where(lane == 1, middle, scale - high - middle))
    outs[0][:, width:] = parts.astype(jnp.bfloat16)


def split(latents):
    _, rows, depth = latents.shape
    width = depth // CHUNKS
    return pl.pallas_call(
        split_kernel,
        in_specs=[IN_HBM],
        out_specs=[IN_VMEM] * CHUNKS,
        out_shape=[VMEM((rows, width + (0 if k else LANES)), jnp.bfloat16) for k in range(CHUNKS)],
        scratch_shapes=[pltpu.VMEM((rows, depth), jnp.bfloat16), pltpu.SemaphoreType.DMA],
        compiler_params=params(4),
        name="split",
    )(*far(latents))


def scale_of(piece):
    parts = piece[:, piece.shape[1] - LANES :].astype(jnp.float32)
    return parts[:, 0:1] + (parts[:, 1:2] + parts[:, 2:3])


def modulated(piece, scale, gain, k, width):
    span = slice(k * width, (k + 1) * width)
    x = piece[:, :width].astype(jnp.float32)
    return (x * scale * gain[0:1, span] + gain[1:2, span]).astype(jnp.bfloat16)


def begin_kernel(shards, place, steps, seg_hbm, table, *refs):
    sources, refs = refs[:3], refs[3:]
    pieces, refs = refs[:CHUNKS], refs[CHUNKS:]
    query, keyval = refs[:2]
    outs, (gain, seg_col, seg_row, segments, sems, small) = refs[2:5], refs[5:]
    depth = pieces[-1].shape[1]
    width = query.shape[1]
    reads = [
        pltpu.make_async_copy(table.at[steps[0]], gain, small.at[0]),
        pltpu.make_async_copy(seg_hbm, segments, small.at[1]),
    ]
    for copy in reads:
        copy.start()
    short = depth // PARTS
    spans = [slice(k * short, (k + 1) * short) for k in range(CHUNKS * PARTS)]
    copies = [
        pltpu.make_async_copy(sources[i].at[span], outs[i].at[span], sems.at[i, k])
        for i in range(3)
        for k, span in enumerate(spans)
    ]
    for copy in copies[:AHEAD]:
        copy.start()
    for copy in reads:
        copy.wait()
    gain[0:1, :] = 1.0 + gain[0:1, :]
    scale = scale_of(pieces[0])
    own = [modulated(piece, scale, gain, k, depth) for k, piece in enumerate(pieces)]
    tokc = segments.shape[1]
    rows = tokc // shards

    def owner(position):
        shard = place[0] - position // rows
        return jnp.where(shard < 0, shard + shards, shard) * rows + position % rows

    down = lax.broadcasted_iota(jnp.int32, (tokc, tokc), 0)
    across = lax.broadcasted_iota(jnp.int32, (tokc, tokc), 1)
    natural = segments[...]
    column = jnp.sum(jnp.where(down == across, natural, 0), axis=1, keepdims=True)
    seg_col[...] = jnp.sum(jnp.where(owner(down) == across, natural, 0), axis=1, keepdims=True)
    seg_row[...] = jnp.sum(jnp.where(owner(across) == down, column, 0), axis=0, keepdims=True)
    for i in range(3):
        total = None
        for k, span in enumerate(spans):
            index = i * len(spans) + k
            copies[index].wait()
            if index + AHEAD < len(copies):
                copies[index + AHEAD].start()
            part = k % PARTS
            part = jnp.dot(
                own[k // PARTS][:, part * short : (part + 1) * short],
                outs[i][span],
                preferred_element_type=jnp.float32,
            )
            total = part if total is None else total + part
        if i == 0:
            query[...] = total.astype(jnp.bfloat16)
        else:
            keyval[:, (i - 1) * width : i * width] = total.astype(jnp.bfloat16)


def begin(weights, segments, steps, mod_table, pieces, place, shards):
    tokc = segments.shape[0]
    rows = pieces[0].shape[0]
    width = weights[0].shape[1]
    return pl.pallas_call(
        functools.partial(begin_kernel, shards),
        in_specs=[IN_SMEM] * 2 + [IN_HBM] * 5 + [IN_VMEM] * CHUNKS,
        out_specs=[IN_VMEM] * 8,
        out_shape=[VMEM((rows, width), jnp.bfloat16), VMEM((rows, 2 * width), jnp.bfloat16)]
        + [VMEM(w.shape, w.dtype) for w in weights]
        + [VMEM(mod_table.shape[1:], jnp.float32)]
        + [VMEM((tokc, 1), jnp.int32), VMEM((1, tokc), jnp.int32)],
        scratch_shapes=[
            pltpu.VMEM((1, tokc), jnp.int32),
            pltpu.SemaphoreType.DMA((3, CHUNKS * PARTS)),
            pltpu.SemaphoreType.DMA((2,)),
        ],
        compiler_params=params(4 + tokc * tokc * 32 // 2**20),
        name="begin",
    )(place, steps, *far(segments[None], mod_table, *weights), *near(*pieces))


def project_kernel(count, places, first, last, older, *refs):
    known = len({0, *places})
    pieces, refs = refs[: count * known], refs[count * known :]
    gain, weights, refs = refs[0], refs[1:4], refs[4:]
    if not first:
        start, refs = refs[0], refs[1:]
    if older:
        before, refs = refs[0], refs[1:]
        refs[1][:older, :] = before[...]
    width = weights[0].shape[1]
    depth = weights[0].shape[0] // CHUNKS
    scales = [scale_of(pieces[s * known]) for s in range(count)]
    stacked = [
        jnp.concatenate(
            [
                modulated(pieces[s * known + known - len(places) + i], scales[s], gain, k, depth)
                for s in range(count)
            ],
            axis=0,
        )
        for i, k in enumerate(places)
    ]
    for index, weight in enumerate(weights):
        total = None if first else start[:, index * width : (index + 1) * width]
        for k, place in enumerate(places):
            part = jnp.dot(
                stacked[k],
                weight[place * depth : (place + 1) * depth, :],
                preferred_element_type=jnp.float32,
            )
            total = part if total is None else total + part
        if not last:
            refs[0][:, index * width : (index + 1) * width] = total
        elif index == 0:
            refs[0][...] = total.astype(jnp.bfloat16)
        else:
            refs[1][older:, (index - 1) * width : index * width] = total.astype(jnp.bfloat16)


def project(shard_pieces, places, gain, weights, start, last, before=None):
    count = len(shard_pieces)
    rows = shard_pieces[0][0].shape[0] * count
    older = 0 if before is None else before.shape[0]
    width = weights[0].shape[1]
    if last:
        shapes = [
            VMEM((rows, width), jnp.bfloat16),
            VMEM((older + rows, 2 * width), jnp.bfloat16),
        ]
    else:
        shapes = [VMEM((rows, 3 * width), jnp.float32)]
    pieces = [shard[k] for shard in shard_pieces for k in sorted({0, *places})]
    extra = [array for array in (start, before) if array is not None]
    return pl.pallas_call(
        functools.partial(project_kernel, count, tuple(places), start is None, last, older),
        in_specs=[IN_VMEM] * (len(pieces) + 4 + len(extra)),
        out_specs=[IN_VMEM] * len(shapes),
        out_shape=shapes,
        compiler_params=params(4 + count * 2),
        name="project",
    )(*near(*pieces, gain, *weights, *extra))


def attend_kernel(shards, parts, sources, mine, seg_col, seg_row, *refs):
    queries, refs = refs[:parts], refs[parts:]
    early, refs = refs[:sources], refs[sources:]
    late, refs = refs[:sources], refs[sources:]
    outs, (q_all, kv_all) = refs[:shards], refs[shards:]
    tokc, width = q_all.shape
    rows = tokc // shards
    heads = width // HD
    many = early[0].shape[0]
    filled = 0
    for query in queries:
        q_all[filled : filled + query.shape[0], :] = query[...]
        filled += query.shape[0]
    for m in range(sources):
        kv_all[m * tokc : m * tokc + many, :] = early[m][...]
        kv_all[m * tokc + many : (m + 1) * tokc, :] = late[m][...]
    here = mine[0]
    clip = []
    for m in range(sources):
        usable = jnp.where((here ^ m) <= here, 0, 1000)
        clip.append(seg_row[...] + usable)
    clip = jnp.concatenate(clip, axis=1)
    inverse = 1.0 / math.sqrt(HD)
    block = min(tokc, 128)
    for b in range(tokc // block):
        span = slice(b * block, (b + 1) * block)
        allowed = seg_col[span, :] == clip
        for h in range(heads):
            cols = slice(h * HD, (h + 1) * HD)
            vcols = slice(width + h * HD, width + (h + 1) * HD)
            scores = lax.dot_general(
                q_all[span, cols],
                kv_all[:, cols],
                (((1,), (1,)), ((), ())),
                preferred_element_type=jnp.float32,
            )
            scores = jnp.where(allowed, scores * inverse, -1e30)
            best = jnp.max(scores, axis=-1, keepdims=True)
            weights = jnp.where(allowed, jnp.exp(scores - best), 0.0)
            total = jnp.sum(weights, axis=-1, keepdims=True)
            summed = jnp.dot(
                weights.astype(jnp.bfloat16), kv_all[:, vcols], preferred_element_type=jnp.float32
            )
            result = (summed / total).astype(jnp.bfloat16)
            for s in range(block // rows):
                outs[b * (block // rows) + s][:, cols] = result[s * rows : (s + 1) * rows]


def attend(shards, mine, seg_col, seg_row, queries, early, late):
    sources = len(early)
    width = queries[0].shape[1]
    tokc = seg_col.shape[0]
    rows = tokc // shards
    return pl.pallas_call(
        functools.partial(attend_kernel, shards, len(queries), sources),
        in_specs=[IN_SMEM] + [IN_VMEM] * (2 + len(queries) + 2 * sources),
        out_specs=[IN_VMEM] * shards,
        out_shape=[VMEM((rows, width), jnp.bfloat16)] * shards,
        scratch_shapes=[
            pltpu.VMEM((tokc, width), jnp.bfloat16),
            pltpu.VMEM((sources * tokc, 2 * width), jnp.bfloat16),
        ],
        compiler_params=params(3 + sources * tokc * 8 // 2048),
        name="attend",
    )(mine, *near(seg_col, seg_row, *queries, *early, *late))


def place_kernel(order, place, *refs):
    pieces, out = refs[:-1], refs[-1]
    width = pieces[0].shape[1]
    count = len(pieces)
    for s, piece in zip(order, pieces):
        column = lax.rem(place[0] + s, count) * width
        out[0, :, pl.ds(pl.multiple_of(column, width), width)] = piece[...]


def place_columns(place, pieces):
    rows, width = pieces[0].shape
    order = [0, *range(2, len(pieces)), 1]
    return pl.pallas_call(
        functools.partial(place_kernel, order),
        in_specs=[IN_SMEM] + [IN_VMEM] * len(pieces),
        out_specs=IN_VMEM,
        out_shape=jax.ShapeDtypeStruct((1, rows, width * len(pieces)), jnp.bfloat16),
        compiler_params=params(2),
        name="place",
    )(place, *near(*[pieces[s] for s in order]))


def across_chips(block, groups):
    return [block] + [
        lax.ppermute(block, "group", [(i, i ^ m) for i in range(groups)])
        for m in range(2, groups, 2)
    ]


def across_cores(held, groups):
    swap = [(i, i ^ 1) for i in range(groups)]
    return [each for block in held for each in (block, lax.ppermute(block, "group", swap))]


def per_device(latents, steps, segment_ids, mod_table, w_query, w_key, w_value):
    shards = lax.axis_size("dp")
    groups = lax.axis_size("group")
    rows = latents.shape[1]
    place = lax.axis_index("dp").astype(jnp.int32)
    mine = lax.axis_index("group").astype(jnp.int32)
    ring = [(i, (i + 1) % shards) for i in range(shards)]

    pieces = list(split(latents))
    query, keyval, *rest = begin(
        (w_query, w_key, w_value), segment_ids, steps, mod_table, pieces, place[None], shards
    )
    weights, (gain, seg_col, seg_row) = rest[:3], rest[3:]
    queries = [query]
    pieces = [lax.ppermute(piece, "dp", ring) for piece in pieces]
    pieces[0], keyval = lax.optimization_barrier((pieces[0], keyval))
    arrived = []
    for s in range(1, shards - 2):
        arrived.append(pieces)
        pieces = [lax.ppermute(piece, "dp", ring) for piece in pieces]
    query, keyval = project(arrived, range(CHUNKS), gain, weights, None, True, keyval)
    queries.append(query)
    pieces[0], keyval = lax.optimization_barrier((pieces[0], keyval))
    early = across_chips(keyval, groups)
    _, early = lax.optimization_barrier((pieces[-1], early))
    early = across_cores(early, groups)
    moved = [lax.ppermute(piece, "dp", ring) for piece in pieces]
    moved[0], early = lax.optimization_barrier((moved[0], early))
    both = [pieces, moved]
    start = project(both, range(CHUNKS - 1), gain, weights, None, False)[0]
    query, keyval = project(both, [CHUNKS - 1], gain, weights, start, True)
    queries.append(query)
    late = across_cores(across_chips(keyval, groups), groups)
    results = attend(shards, mine[None], seg_col, seg_row, queries, early, late)
    landed = [results[0]]
    for s in range(1, shards):
        landed.append(
            lax.ppermute(results[s], "dp", [(i, (i - s) % shards) for i in range(shards)])
        )
    return place_columns(place[None], landed)


def solution(mesh):
    placed = (
        P("group", "dp", None),
        P("group"),
        P(),
        P(),
        P(None, "dp"),
        P(None, "dp"),
        P(None, "dp"),
    )
    return jax.shard_map(
        per_device, mesh=mesh, in_specs=placed, out_specs=P("group", "dp", None), check_vma=False
    )
```

```python
import functools
import math

import jax
import jax.numpy as jnp
from jax import lax
from jax.experimental import pallas as pl
from jax.experimental.pallas import tpu as pltpu
from jax.sharding import PartitionSpec as P

HD = 128
LANES = 128
EDGES = (0, 1, 2)
CHUNKS = len(EDGES) - 1
PARTS = 4
AHEAD = 6
VMEM = pltpu.MemorySpace.VMEM
HBM = pltpu.MemorySpace.HBM
SMEM = pltpu.MemorySpace.SMEM
IN_VMEM = pl.BlockSpec(memory_space=VMEM)
IN_HBM = pl.BlockSpec(memory_space=HBM)
IN_SMEM = pl.BlockSpec(memory_space=SMEM)


def spans_of(depth):
    edges = [depth * edge // EDGES[-1] for edge in EDGES]
    return [slice(low, high) for low, high in zip(edges, edges[1:])]


def params(mebibytes):
    return pltpu.CompilerParams(vmem_limit_bytes=mebibytes * 1024 * 1024)


def near(*arrays):
    return [pltpu.with_memory_space_constraint(a, VMEM) for a in arrays]


def far(*arrays):
    return [pltpu.with_memory_space_constraint(a, HBM) for a in arrays]


def split_kernel(x_hbm, *refs):
    outs, (x_ref, sem) = refs[:CHUNKS], refs[CHUNKS:]
    copy = pltpu.make_async_copy(x_hbm.at[0], x_ref, sem)
    copy.start()
    copy.wait()
    for span, out in zip(spans_of(x_ref.shape[1]), outs):
        out[:, : span.stop - span.start] = x_ref[:, span]
    x = x_ref[...].astype(jnp.float32)
    scale = lax.rsqrt(jnp.mean(x * x, axis=-1, keepdims=True) + 1e-06)
    high = scale.astype(jnp.bfloat16).astype(jnp.float32)
    middle = (scale - high).astype(jnp.bfloat16).astype(jnp.float32)
    lane = lax.broadcasted_iota(jnp.int32, (x.shape[0], LANES), 1)
    parts = jnp.where(lane == 0, high, jnp.where(lane == 1, middle, scale - high - middle))
    outs[0][:, outs[0].shape[1] - LANES :] = parts.astype(jnp.bfloat16)


def split(latents):
    _, rows, depth = latents.shape
    widths = [span.stop - span.start for span in spans_of(depth)]
    widths[0] += LANES
    return pl.pallas_call(
        split_kernel,
        in_specs=[IN_HBM],
        out_specs=[IN_VMEM] * CHUNKS,
        out_shape=[VMEM((rows, width), jnp.bfloat16) for width in widths],
        scratch_shapes=[pltpu.VMEM((rows, depth), jnp.bfloat16), pltpu.SemaphoreType.DMA],
        compiler_params=params(1),
        name="split",
    )(*far(latents))


def scale_of(piece):
    parts = piece[:, piece.shape[1] - LANES :].astype(jnp.float32)
    return parts[:, 0:1] + (parts[:, 1:2] + parts[:, 2:3])


def modulated(piece, scale, gain, span):
    x = piece[:, : span.stop - span.start].astype(jnp.float32)
    return (x * scale * gain[0:1, span] + gain[1:2, span]).astype(jnp.bfloat16)


def begin_kernel(shards, place, steps, seg_hbm, table, *refs):
    sources, refs = refs[:3], refs[3:]
    pieces, refs = refs[:CHUNKS], refs[CHUNKS:]
    query, keyval = refs[:2]
    outs, (gain, seg_col, seg_row, segments, sems, small) = refs[2:5], refs[5:]
    depth = outs[0].shape[0]
    width = query.shape[1]
    chunks = spans_of(depth)
    reads = [
        pltpu.make_async_copy(table.at[steps[0]], gain, small.at[0]),
        pltpu.make_async_copy(seg_hbm, segments, small.at[1]),
    ]
    for copy in reads:
        copy.start()
    short = depth // PARTS
    spans = [slice(k * short, (k + 1) * short) for k in range(PARTS)]
    copies = [
        pltpu.make_async_copy(sources[i].at[span], outs[i].at[span], sems.at[i, k])
        for i in range(3)
        for k, span in enumerate(spans)
    ]
    for copy in copies[:AHEAD]:
        copy.start()
    for copy in reads:
        copy.wait()
    gain[0:1, :] = 1.0 + gain[0:1, :]
    scale = scale_of(pieces[0])
    own = jnp.concatenate(
        [modulated(piece, scale, gain, chunk) for piece, chunk in zip(pieces, chunks)], axis=1
    )
    tokc = segments.shape[1]
    rows = tokc // shards

    def owner(position):
        shard = place[0] - position // rows
        return jnp.where(shard < 0, shard + shards, shard) * rows + position % rows

    down = lax.broadcasted_iota(jnp.int32, (tokc, tokc), 0)
    across = lax.broadcasted_iota(jnp.int32, (tokc, tokc), 1)
    natural = segments[...]
    column = jnp.sum(jnp.where(down == across, natural, 0), axis=1, keepdims=True)
    seg_col[...] = jnp.sum(jnp.where(owner(down) == across, natural, 0), axis=1, keepdims=True)
    seg_row[...] = jnp.sum(jnp.where(owner(across) == down, column, 0), axis=0, keepdims=True)
    for i in range(3):
        total = None
        for k, span in enumerate(spans):
            index = i * len(spans) + k
            copies[index].wait()
            if index + AHEAD < len(copies):
                copies[index + AHEAD].start()
            part = jnp.dot(own[:, span], outs[i][span], preferred_element_type=jnp.float32)
            total = part if total is None else total + part
        if i == 0:
            query[...] = total.astype(jnp.bfloat16)
        else:
            keyval[:, (i - 1) * width : i * width] = total.astype(jnp.bfloat16)


def begin(weights, segments, steps, mod_table, pieces, place, shards):
    tokc = segments.shape[0]
    rows = pieces[0].shape[0]
    width = weights[0].shape[1]
    return pl.pallas_call(
        functools.partial(begin_kernel, shards),
        in_specs=[IN_SMEM] * 2 + [IN_HBM] * 5 + [IN_VMEM] * CHUNKS,
        out_specs=[IN_VMEM] * 8,
        out_shape=[VMEM((rows, width), jnp.bfloat16), VMEM((rows, 2 * width), jnp.bfloat16)]
        + [VMEM(w.shape, w.dtype) for w in weights]
        + [VMEM(mod_table.shape[1:], jnp.float32)]
        + [VMEM((tokc, 1), jnp.int32), VMEM((1, tokc), jnp.int32)],
        scratch_shapes=[
            pltpu.VMEM((1, tokc), jnp.int32),
            pltpu.SemaphoreType.DMA((3, PARTS)),
            pltpu.SemaphoreType.DMA((2,)),
        ],
        compiler_params=params(2 + tokc * tokc * 32 // 2**20),
        name="begin",
    )(place, steps, *far(segments[None], mod_table, *weights), *near(*pieces))


def project_kernel(count, places, kinds, first, last, older, *refs):
    known = len({0, *places})
    pieces, refs = refs[: count * known], refs[count * known :]
    gain, weights, refs = refs[0], refs[1 : 1 + len(kinds)], refs[1 + len(kinds) :]
    if not first:
        start, refs = refs[0], refs[1:]
    if older:
        before, refs = refs[0], refs[1:]
        refs[-1][:older, :] = before[...]
    width = weights[0].shape[1]
    chunks = spans_of(weights[0].shape[0])
    scales = [scale_of(pieces[s * known]) for s in range(count)]
    stacked = [
        jnp.concatenate(
            [
                modulated(pieces[s * known + known - len(places) + i], scales[s], gain, chunks[k])
                for s in range(count)
            ],
            axis=0,
        )
        for i, k in enumerate(places)
    ]
    for index, (kind, weight) in enumerate(zip(kinds, weights)):
        total = None if first else start[:, index * width : (index + 1) * width]
        for k, place in enumerate(places):
            part = jnp.dot(
                stacked[k],
                weight[chunks[place], :],
                preferred_element_type=jnp.float32,
            )
            total = part if total is None else total + part
        if not last:
            refs[0][:, index * width : (index + 1) * width] = total
        elif kind == 0:
            refs[0][...] = total.astype(jnp.bfloat16)
        else:
            refs[-1][older:, (kind - 1) * width : kind * width] = total.astype(jnp.bfloat16)


def project(shard_pieces, places, gain, weights, kinds, start, last, before=None):
    count = len(shard_pieces)
    rows = shard_pieces[0][0].shape[0] * count
    older = 0 if before is None else before.shape[0]
    width = weights[0].shape[1]
    if last:
        shapes = [VMEM((rows, width), jnp.bfloat16)] if 0 in kinds else []
        if 1 in kinds:
            shapes.append(VMEM((older + rows, 2 * width), jnp.bfloat16))
    else:
        shapes = [VMEM((rows, len(kinds) * width), jnp.float32)]
    pieces = [shard[k] for shard in shard_pieces for k in sorted({0, *places})]
    extra = [array for array in (start, before) if array is not None]
    used = [weights[kind] for kind in kinds]
    return pl.pallas_call(
        functools.partial(
            project_kernel, count, tuple(places), tuple(kinds), start is None, last, older
        ),
        in_specs=[IN_VMEM] * (len(pieces) + 1 + len(used) + len(extra)),
        out_specs=[IN_VMEM] * len(shapes),
        out_shape=shapes,
        compiler_params=params(1 + count // 2),
        name="project",
    )(*near(*pieces, gain, *used, *extra))


def bias_of(sources, mine, seg_col, seg_row):
    here = mine[0]
    clip = jnp.concatenate(
        [seg_row + jnp.where((here ^ m) <= here, 0, 1000) for m in range(sources)], axis=1
    )
    return jnp.where(seg_col == clip, 0.0, -1e30)


def stack(blocks, out):
    many = blocks[0].shape[0]
    for m, block in enumerate(blocks):
        out[m * many : (m + 1) * many, :] = block[...]


def blocks_of(tokc):
    block = min(tokc, 128)
    return [slice(start, start + block) for start in range(0, tokc, block)]


def weigh(queries, keys, values, bias, floors):
    scores = [
        lax.dot_general(q, k, (((1,), (1,)), ((), ())), preferred_element_type=jnp.float32)
        for q, k in zip(queries, keys)
    ]
    scores = [s * (1.0 / math.sqrt(HD)) + bias for s in scores]
    bests = [jnp.max(s, axis=-1, keepdims=True) for s in scores]
    if floors is not None:
        bests = [jnp.maximum(best, floor) for best, floor in zip(bests, floors)]
    weights = [jnp.exp(s - best) for s, best in zip(scores, bests)]
    sums = [
        jnp.dot(w.astype(jnp.bfloat16), v, preferred_element_type=jnp.float32)
        for w, v in zip(weights, values)
    ]
    totals = [jnp.sum(w, axis=-1, keepdims=True) for w in weights]
    return bests, totals, sums


def columns(ref, span, count, start=0):
    return [ref[span, start + h * HD : start + (h + 1) * HD] for h in range(count)]


def attend_early_kernel(parts, sources, mine, seg_col, seg_row, *refs):
    queries, refs = refs[:parts], refs[parts:]
    early, refs = refs[:sources], refs[sources:]
    q_all, sums, bests, totals, bias_late, kv_all = refs
    filled = 0
    for query in queries:
        q_all[filled : filled + query.shape[0], :] = query[...]
        filled += query.shape[0]
    stack(early, kv_all)
    many = early[0].shape[0]
    heads = q_all.shape[1] // HD
    every = slice(0, kv_all.shape[0])
    for span in blocks_of(q_all.shape[0]):
        bias = bias_of(sources, mine, seg_col[span, :], seg_row[:, :many])
        state = weigh(
            columns(q_all, span, heads),
            columns(kv_all, every, heads),
            columns(kv_all, every, heads, heads * HD),
            bias,
            None,
        )
        for h, (best, total, summed) in enumerate(zip(*state)):
            bests[span, h * HD : (h + 1) * HD] = jnp.broadcast_to(best, summed.shape)
            totals[span, h * HD : (h + 1) * HD] = jnp.broadcast_to(total, summed.shape)
            sums[span, h * HD : (h + 1) * HD] = summed
        bias_late[span, :] = bias_of(sources, mine, seg_col[span, :], seg_row[:, many:])


def attend_early(mine, seg_col, seg_row, queries, early):
    sources, many = len(early), early[0].shape[0]
    tokc, width = seg_col.shape[0], queries[0].shape[1]
    return pl.pallas_call(
        functools.partial(attend_early_kernel, len(queries), sources),
        in_specs=[IN_SMEM] + [IN_VMEM] * (2 + len(queries) + sources),
        out_specs=[IN_VMEM] * 5,
        out_shape=[VMEM((tokc, width), jnp.bfloat16)]
        + [VMEM((tokc, width), jnp.float32)] * 3
        + [VMEM((tokc, sources * (tokc - many)), jnp.float32)],
        scratch_shapes=[pltpu.VMEM((sources * many, 2 * width), jnp.bfloat16)],
        compiler_params=params(3 * (sources * tokc // 1024)),
        name="attend_early",
    )(mine, *near(seg_col, seg_row, *queries, *early))


def attend_kernel(shards, sources, q_all, sums, bests, totals, bias, *refs):
    late, outs, kv_all = refs[:sources], refs[sources:-1], refs[-1]
    tokc, width = q_all.shape
    rows = tokc // shards
    heads = width // HD
    stack(late, kv_all)
    every = slice(0, kv_all.shape[0])
    for span in blocks_of(tokc):
        floors = [floor[:, 0:1] for floor in columns(bests, span, heads)]
        state = weigh(
            columns(q_all, span, heads),
            columns(kv_all, every, heads),
            columns(kv_all, every, heads, heads * HD),
            bias[span, :],
            floors,
        )
        before = zip(floors, columns(totals, span, heads), columns(sums, span, heads))
        for h, (best, total, summed) in enumerate(zip(*state)):
            floor, old_total, old_sum = next(before)
            fade = jnp.exp(floor - best)
            scale = 1.0 / (total + old_total[:, 0:1] * fade)
            result = ((summed + old_sum * fade) * scale).astype(jnp.bfloat16)
            for s in range(span.start // rows, span.stop // rows):
                outs[s][:, h * HD : (h + 1) * HD] = result[
                    s * rows - span.start : (s + 1) * rows - span.start
                ]


def attend(shards, state, late):
    sources, many = len(late), late[0].shape[0]
    tokc, width = state[0].shape
    rows = tokc // shards
    return pl.pallas_call(
        functools.partial(attend_kernel, shards, sources),
        in_specs=[IN_VMEM] * (len(state) + sources),
        out_specs=[IN_VMEM] * shards,
        out_shape=[VMEM((rows, width), jnp.bfloat16)] * shards,
        scratch_shapes=[pltpu.VMEM((sources * many, 2 * width), jnp.bfloat16)],
        compiler_params=params(3 * (sources * tokc // 1024)),
        name="attend",
    )(*near(*state, *late))


def place_kernel(order, place, *refs):
    pieces, out = refs[:-1], refs[-1]
    width = pieces[0].shape[1]
    count = len(pieces)
    for s, piece in zip(order, pieces):
        column = lax.rem(place[0] + s, count) * width
        out[0, :, pl.ds(pl.multiple_of(column, width), width)] = piece[...]


def place_columns(place, pieces):
    rows, width = pieces[0].shape
    order = [0, *range(2, len(pieces)), 1]
    return pl.pallas_call(
        functools.partial(place_kernel, order),
        in_specs=[IN_SMEM] + [IN_VMEM] * len(pieces),
        out_specs=IN_VMEM,
        out_shape=jax.ShapeDtypeStruct((1, rows, width * len(pieces)), jnp.bfloat16),
        compiler_params=params(1),
        name="place",
    )(place, *near(*[pieces[s] for s in order]))


def across_chips(block, groups):
    return [block] + [
        lax.ppermute(block, "group", [(i, i ^ m) for i in range(groups)])
        for m in range(2, groups, 2)
    ]


def across_cores(held, groups):
    swap = [(i, i ^ 1) for i in range(groups)]
    return [each for block in held for each in (block, lax.ppermute(block, "group", swap))]


def per_device(latents, steps, segment_ids, mod_table, w_query, w_key, w_value):
    shards = lax.axis_size("dp")
    groups = lax.axis_size("group")
    rows = latents.shape[1]
    place = lax.axis_index("dp").astype(jnp.int32)
    mine = lax.axis_index("group").astype(jnp.int32)
    ring = [(i, (i + 1) % shards) for i in range(shards)]

    latents, place, mine = lax.optimization_barrier((latents, place[None], mine[None]))
    pieces = list(split(latents))
    query, keyval, *rest = begin(
        (w_query, w_key, w_value), segment_ids, steps, mod_table, pieces, place, shards
    )
    weights, (gain, seg_col, seg_row) = rest[:3], rest[3:]
    queries = [query]
    pieces = [lax.ppermute(piece, "dp", ring) for piece in pieces]
    pieces[0], keyval = lax.optimization_barrier((pieces[0], keyval))
    arrived = []
    for s in range(1, shards - 2):
        arrived.append(pieces)
        pieces = [lax.ppermute(piece, "dp", ring) for piece in pieces]
    query, keyval = project(arrived, range(CHUNKS), gain, weights, (0, 1, 2), None, True, keyval)
    queries.append(query)
    pieces[0], keyval = lax.optimization_barrier((pieces[0], keyval))
    early = across_chips(keyval, groups)
    _, early = lax.optimization_barrier((pieces[-1], early))
    early = across_cores(early, groups)
    moved = [lax.ppermute(piece, "dp", ring) for piece in pieces]
    moved[0], early = lax.optimization_barrier((moved[0], early))
    both = [pieces, moved]
    start = project(both, range(CHUNKS - 1), gain, weights, (1, 2), None, False)[0]
    keyval = project(both, [CHUNKS - 1], gain, weights, (1, 2), start, True)[0]
    gain, keyval = lax.optimization_barrier((gain, keyval))
    late = across_chips(keyval, groups)
    query = project(both, range(CHUNKS), gain, weights, (0,), None, True)[0]
    queries.append(query)
    state = attend_early(mine, seg_col, seg_row, queries, early)
    late[1:], state = lax.optimization_barrier((late[1:], state))
    late = across_cores(late, groups)
    results = attend(shards, state, late)
    landed = [results[0]]
    for s in range(1, shards):
        landed.append(
            lax.ppermute(results[s], "dp", [(i, (i - s) % shards) for i in range(shards)])
        )
    return place_columns(place, landed)


def solution(mesh):
    placed = (
        P("group", "dp", None),
        P("group"),
        P(),
        P(),
        P(None, "dp"),
        P(None, "dp"),
        P(None, "dp"),
    )
    return jax.shard_map(
        per_device, mesh=mesh, in_specs=placed, out_specs=P("group", "dp", None), check_vma=False
    )
```

```python
import functools
import math

import jax
import jax.numpy as jnp
from jax import lax
from jax.experimental import pallas as pl
from jax.experimental.pallas import tpu as pltpu
from jax.sharding import PartitionSpec as P

HD = 128
LANES = 128
EXTRA = 16
EDGES = (0, 25, 48)
CHUNKS = len(EDGES) - 1
PARTS = 4
AHEAD = 6
VMEM = pltpu.MemorySpace.VMEM
HBM = pltpu.MemorySpace.HBM
SMEM = pltpu.MemorySpace.SMEM
IN_VMEM = pl.BlockSpec(memory_space=VMEM)
IN_HBM = pl.BlockSpec(memory_space=HBM)
IN_SMEM = pl.BlockSpec(memory_space=SMEM)


def spans_of(depth):
    edges = [depth * edge // EDGES[-1] for edge in EDGES]
    return [slice(low, high) for low, high in zip(edges, edges[1:])]


def params(mebibytes):
    return pltpu.CompilerParams(vmem_limit_bytes=mebibytes * 1024 * 1024)


def near(*arrays):
    return [pltpu.with_memory_space_constraint(a, VMEM) for a in arrays]


def far(*arrays):
    return [pltpu.with_memory_space_constraint(a, HBM) for a in arrays]


def split_kernel(x_hbm, *refs):
    outs, sems = refs[:CHUNKS], refs[CHUNKS]
    copies = [
        pltpu.make_async_copy(x_hbm.at[0, :, span], out, sems.at[k])
        for k, (span, out) in enumerate(zip(spans_of(x_hbm.shape[2]), outs))
    ]
    for copy in copies:
        copy.start()
    for copy in copies:
        copy.wait()


def split(latents):
    _, rows, depth = latents.shape
    widths = [span.stop - span.start for span in spans_of(depth)]
    return pl.pallas_call(
        split_kernel,
        in_specs=[IN_HBM],
        out_specs=[IN_VMEM] * CHUNKS,
        out_shape=[VMEM((rows, width), jnp.bfloat16) for width in widths],
        scratch_shapes=[pltpu.SemaphoreType.DMA((CHUNKS,))],
        compiler_params=params(1),
        name="split",
    )(*far(latents))


def squares(piece):
    x = piece[...].astype(jnp.float32)
    return jnp.sum(x * x, axis=-1, keepdims=True)


def scale_from(total, depth):
    return lax.rsqrt(total * (1.0 / depth) + 1e-06)


def scale_of(pieces):
    depth = sum(piece.shape[1] for piece in pieces)
    return scale_from(sum(squares(piece) for piece in pieces), depth)


def modulated(piece, scale, gain, span):
    x = piece[...].astype(jnp.float32)
    return (x * scale * gain[0:1, span] + gain[1:2, span]).astype(jnp.bfloat16)


def begin_kernel(shards, place, steps, seg_hbm, table, *refs):
    sources, refs = refs[:3], refs[3:]
    pieces, refs = refs[:CHUNKS], refs[CHUNKS:]
    query, keyval = refs[:2]
    outs, (gain, seg_col, seg_row, segments, sems, small) = refs[2:5], refs[5:]
    depth = outs[0].shape[0]
    width = query.shape[1]
    chunks = spans_of(depth)
    reads = [
        pltpu.make_async_copy(table.at[steps[0]], gain, small.at[0]),
        pltpu.make_async_copy(seg_hbm, segments, small.at[1]),
    ]
    for copy in reads:
        copy.start()
    short = depth // PARTS
    spans = [slice(k * short, (k + 1) * short) for k in range(PARTS)]
    copies = [
        pltpu.make_async_copy(sources[i].at[span], outs[i].at[span], sems.at[i, k])
        for i in range(3)
        for k, span in enumerate(spans)
    ]
    for copy in copies[:AHEAD]:
        copy.start()
    for copy in reads:
        copy.wait()
    gain[0:1, :] = 1.0 + gain[0:1, :]
    scale = scale_of(pieces)
    own = jnp.concatenate(
        [modulated(piece, scale, gain, chunk) for piece, chunk in zip(pieces, chunks)], axis=1
    )
    tokc = segments.shape[1]
    rows = tokc // shards

    def owner(position):
        shard = place[0] - position // rows
        return jnp.where(shard < 0, shard + shards, shard) * rows + position % rows

    down = lax.broadcasted_iota(jnp.int32, (tokc, tokc), 0)
    across = lax.broadcasted_iota(jnp.int32, (tokc, tokc), 1)
    natural = segments[...]
    column = jnp.sum(jnp.where(down == across, natural, 0), axis=1, keepdims=True)
    seg_col[...] = jnp.sum(jnp.where(owner(down) == across, natural, 0), axis=1, keepdims=True)
    seg_row[...] = jnp.sum(jnp.where(owner(across) == down, column, 0), axis=0, keepdims=True)
    for i in range(3):
        total = None
        for k, span in enumerate(spans):
            index = i * len(spans) + k
            copies[index].wait()
            if index + AHEAD < len(copies):
                copies[index + AHEAD].start()
            part = jnp.dot(own[:, span], outs[i][span], preferred_element_type=jnp.float32)
            total = part if total is None else total + part
        if i == 0:
            query[...] = total.astype(jnp.bfloat16)
        else:
            keyval[:, (i - 1) * width : i * width] = total.astype(jnp.bfloat16)


def begin(weights, segments, steps, mod_table, pieces, place, shards):
    tokc = segments.shape[0]
    rows = pieces[0].shape[0]
    width = weights[0].shape[1]
    return pl.pallas_call(
        functools.partial(begin_kernel, shards),
        in_specs=[IN_SMEM] * 2 + [IN_HBM] * 5 + [IN_VMEM] * CHUNKS,
        out_specs=[IN_VMEM] * 8,
        out_shape=[VMEM((rows, width), jnp.bfloat16), VMEM((rows, 2 * width), jnp.bfloat16)]
        + [VMEM(w.shape, w.dtype) for w in weights]
        + [VMEM(mod_table.shape[1:], jnp.float32)]
        + [VMEM((tokc, 1), jnp.int32), VMEM((1, tokc), jnp.int32)],
        scratch_shapes=[
            pltpu.VMEM((1, tokc), jnp.int32),
            pltpu.SemaphoreType.DMA((3, PARTS)),
            pltpu.SemaphoreType.DMA((2,)),
        ],
        compiler_params=params(2 + tokc * tokc * 32 // 2**20),
        name="begin",
    )(place, steps, *far(segments[None], mod_table, *weights), *near(*pieces))


def project_kernel(count, kinds, older, *refs):
    pieces, refs = refs[: count * CHUNKS], refs[count * CHUNKS :]
    gain, weights, refs = refs[0], refs[1 : 1 + len(kinds)], refs[1 + len(kinds) :]
    if older:
        before, refs = refs[0], refs[1:]
        refs[-1][:older, :] = before[...]
    width = weights[0].shape[1]
    chunks = spans_of(weights[0].shape[0])
    shards = [pieces[s * CHUNKS : (s + 1) * CHUNKS] for s in range(count)]
    scales = [scale_of(shard) for shard in shards]
    stacked = [
        jnp.concatenate(
            [modulated(shard[k], scale, gain, chunk) for shard, scale in zip(shards, scales)],
            axis=0,
        )
        for k, chunk in enumerate(chunks)
    ]
    for kind, weight in zip(kinds, weights):
        total = None
        for rows, chunk in zip(stacked, chunks):
            part = jnp.dot(rows, weight[chunk, :], preferred_element_type=jnp.float32)
            total = part if total is None else total + part
        if kind == 0:
            refs[0][...] = total.astype(jnp.bfloat16)
        else:
            refs[-1][older:, (kind - 1) * width : kind * width] = total.astype(jnp.bfloat16)


def project(shards, gain, weights, kinds, before=None):
    count = len(shards)
    rows = shards[0][0].shape[0] * count
    older = 0 if before is None else before.shape[0]
    width = weights[0].shape[1]
    shapes = [VMEM((rows, width), jnp.bfloat16)] if 0 in kinds else []
    if 1 in kinds:
        shapes.append(VMEM((older + rows, 2 * width), jnp.bfloat16))
    pieces = [piece for shard in shards for piece in shard]
    extra = [] if before is None else [before]
    used = [weights[kind] for kind in kinds]
    return pl.pallas_call(
        functools.partial(project_kernel, count, tuple(kinds), older),
        in_specs=[IN_VMEM] * (len(pieces) + 1 + len(used) + len(extra)),
        out_specs=[IN_VMEM] * len(shapes),
        out_shape=shapes,
        compiler_params=params(max(1, 2 * count - 2)),
        name="project",
    )(*near(*pieces, gain, *used, *extra))


def lead_kernel(*refs):
    whole, refs = refs[:CHUNKS], refs[CHUNKS:]
    parts, refs = refs[: CHUNKS - 1], refs[CHUNKS - 1 :]
    gain, weights, out = refs[0], refs[1:-1], refs[-1]
    width = weights[0].shape[1]
    chunks = spans_of(weights[0].shape[0])
    rows = whole[0].shape[0]
    scale = scale_of(whole)
    row = lax.broadcasted_iota(jnp.int32, (EXTRA, 1), 0)
    stacked = []
    for k, piece in enumerate(parts):
        shift = gain[1:2, chunks[k]]
        high = shift.astype(jnp.bfloat16).astype(jnp.float32)
        added = jnp.where(row == 0, high, jnp.where(row == 1, shift - high, 0.0))
        unscaled = piece[...].astype(jnp.float32) * gain[0:1, chunks[k]]
        stacked.append(
            jnp.concatenate(
                [
                    modulated(whole[k], scale, gain, chunks[k]),
                    unscaled.astype(jnp.bfloat16),
                    added.astype(jnp.bfloat16),
                ],
                axis=0,
            )
        )
    for index, weight in enumerate(weights):
        total = sum(
            jnp.dot(lines, weight[chunk, :], preferred_element_type=jnp.float32)
            for lines, chunk in zip(stacked, chunks)
        )
        out[:, index * width : (index + 1) * width] = total
    seen = sum(squares(piece) for piece in parts)
    last = slice(len(weights) * width, len(weights) * width + LANES)
    out[:rows, last] = jnp.broadcast_to(scale, (rows, LANES))
    out[rows : 2 * rows, last] = jnp.broadcast_to(seen, (rows, LANES))


def lead(whole, parts, gain, weights):
    rows = whole[0].shape[0]
    width = weights[0].shape[1]
    return pl.pallas_call(
        lead_kernel,
        in_specs=[IN_VMEM] * (2 * CHUNKS + len(weights)),
        out_specs=IN_VMEM,
        out_shape=VMEM((2 * rows + EXTRA, len(weights) * width + LANES), jnp.float32),
        compiler_params=params(2),
        name="lead",
    )(*near(*whole, *parts, gain, *weights))


def finish_kernel(whole, piece, gain, *refs):
    weights, (start, out) = refs[:-2], refs[-2:]
    width = weights[0].shape[1]
    depth = weights[0].shape[0]
    chunk = spans_of(depth)[-1]
    rows = whole.shape[0]
    last = len(weights) * width
    scale = scale_from(start[rows : 2 * rows, last : last + 1] + squares(piece), depth)
    lines = jnp.concatenate(
        [
            modulated(whole, start[:rows, last : last + 1], gain, chunk),
            modulated(piece, scale, gain, chunk),
        ],
        axis=0,
    )
    for index, weight in enumerate(weights):
        cols = slice(index * width, (index + 1) * width)
        shift = start[2 * rows : 2 * rows + 1, cols] + start[2 * rows + 1 : 2 * rows + 2, cols]
        total = jnp.dot(lines, weight[chunk, :], preferred_element_type=jnp.float32)
        out[:rows, cols] = (total[:rows] + start[:rows, cols]).astype(jnp.bfloat16)
        known = start[rows : 2 * rows, cols] * scale + shift
        out[rows:, cols] = (total[rows:] + known).astype(jnp.bfloat16)


def finish(whole, piece, gain, weights, start):
    rows = whole.shape[0]
    width = weights[0].shape[1]
    return pl.pallas_call(
        finish_kernel,
        in_specs=[IN_VMEM] * (4 + len(weights)),
        out_specs=IN_VMEM,
        out_shape=VMEM((2 * rows, len(weights) * width), jnp.bfloat16),
        compiler_params=params(2),
        name="finish",
    )(*near(whole, piece, gain, *weights, start))


def bias_of(sources, mine, seg_col, seg_row):
    here = mine[0]
    clip = jnp.concatenate(
        [seg_row + jnp.where((here ^ m) <= here, 0, 1000) for m in range(sources)], axis=1
    )
    return jnp.where(seg_col == clip, 0.0, -1e30)


def stack(blocks, out):
    many = blocks[0].shape[0]
    for m, block in enumerate(blocks):
        out[m * many : (m + 1) * many, :] = block[...]


def blocks_of(tokc):
    block = min(tokc, 128)
    return [slice(start, start + block) for start in range(0, tokc, block)]


def weigh(queries, keys, values, bias, floors):
    scores = [
        lax.dot_general(q, k, (((1,), (1,)), ((), ())), preferred_element_type=jnp.float32)
        for q, k in zip(queries, keys)
    ]
    scores = [s * (1.0 / math.sqrt(HD)) + bias for s in scores]
    bests = [jnp.max(s, axis=-1, keepdims=True) for s in scores]
    if floors is not None:
        bests = [jnp.maximum(best, floor) for best, floor in zip(bests, floors)]
    weights = [jnp.exp(s - best) for s, best in zip(scores, bests)]
    sums = [
        jnp.dot(w.astype(jnp.bfloat16), v, preferred_element_type=jnp.float32)
        for w, v in zip(weights, values)
    ]
    totals = [jnp.sum(w, axis=-1, keepdims=True) for w in weights]
    return bests, totals, sums


def columns(ref, span, count, start=0):
    return [ref[span, start + h * HD : start + (h + 1) * HD] for h in range(count)]


def attend_early_kernel(parts, sources, mine, seg_col, seg_row, *refs):
    queries, refs = refs[:parts], refs[parts:]
    early, refs = refs[:sources], refs[sources:]
    q_all, sums, bests, totals, bias_late, kv_all = refs
    filled = 0
    for query in queries:
        q_all[filled : filled + query.shape[0], :] = query[...]
        filled += query.shape[0]
    stack(early, kv_all)
    many = early[0].shape[0]
    heads = q_all.shape[1] // HD
    every = slice(0, kv_all.shape[0])
    for span in blocks_of(q_all.shape[0]):
        bias = bias_of(sources, mine, seg_col[span, :], seg_row[:, :many])
        state = weigh(
            columns(q_all, span, heads),
            columns(kv_all, every, heads),
            columns(kv_all, every, heads, heads * HD),
            bias,
            None,
        )
        for h, (best, total, summed) in enumerate(zip(*state)):
            bests[span, h * HD : (h + 1) * HD] = jnp.broadcast_to(best, summed.shape)
            totals[span, h * HD : (h + 1) * HD] = jnp.broadcast_to(total, summed.shape)
            sums[span, h * HD : (h + 1) * HD] = summed
        bias_late[span, :] = bias_of(sources, mine, seg_col[span, :], seg_row[:, many:])


def attend_early(mine, seg_col, seg_row, queries, early):
    sources, many = len(early), early[0].shape[0]
    tokc, width = seg_col.shape[0], queries[0].shape[1]
    return pl.pallas_call(
        functools.partial(attend_early_kernel, len(queries), sources),
        in_specs=[IN_SMEM] + [IN_VMEM] * (2 + len(queries) + sources),
        out_specs=[IN_VMEM] * 5,
        out_shape=[VMEM((tokc, width), jnp.bfloat16)]
        + [VMEM((tokc, width), jnp.float32)] * 3
        + [VMEM((tokc, sources * (tokc - many)), jnp.float32)],
        scratch_shapes=[pltpu.VMEM((sources * many, 2 * width), jnp.bfloat16)],
        compiler_params=params(3 * (sources * tokc // 1024)),
        name="attend_early",
    )(mine, *near(seg_col, seg_row, *queries, *early))


def attend_kernel(shards, sources, place, q_all, sums, bests, totals, bias, *refs):
    late, outs, kv_all, held = refs[:sources], refs[sources:-2], refs[-2], refs[-1]
    tokc, width = q_all.shape
    rows = tokc // shards
    heads = width // HD
    stack(late, kv_all)
    every = slice(0, kv_all.shape[0])
    for span in blocks_of(tokc):
        floors = [floor[:, 0:1] for floor in columns(bests, span, heads)]
        state = weigh(
            columns(q_all, span, heads),
            columns(kv_all, every, heads),
            columns(kv_all, every, heads, heads * HD),
            bias[span, :],
            floors,
        )
        before = zip(floors, columns(totals, span, heads), columns(sums, span, heads))
        for h, (best, total, summed) in enumerate(zip(*state)):
            floor, old_total, old_sum = next(before)
            fade = jnp.exp(floor - best)
            scale = 1.0 / (total + old_total[:, 0:1] * fade)
            result = ((summed + old_sum * fade) * scale).astype(jnp.bfloat16)
            held[span, h * HD : (h + 1) * HD] = result
    for m, out in enumerate(outs):
        spot = lax.rem(place[0] - (place[0] ^ m) + shards, shards) * rows
        out[...] = held[pl.ds(pl.multiple_of(spot, rows), rows), :]


def attend(shards, place, state, late):
    sources, many = len(late), late[0].shape[0]
    tokc, width = state[0].shape
    rows = tokc // shards
    return pl.pallas_call(
        functools.partial(attend_kernel, shards, sources),
        in_specs=[IN_SMEM] + [IN_VMEM] * (len(state) + sources),
        out_specs=[IN_VMEM] * shards,
        out_shape=[VMEM((rows, width), jnp.bfloat16)] * shards,
        scratch_shapes=[
            pltpu.VMEM((sources * many, 2 * width), jnp.bfloat16),
            pltpu.VMEM((tokc, width), jnp.bfloat16),
        ],
        compiler_params=params(3 * (sources * tokc // 1024)),
        name="attend",
    )(place, *near(*state, *late))


def place_kernel(order, place, *refs):
    pieces, out = refs[:-1], refs[-1]
    width = pieces[0].shape[1]
    count = len(pieces)
    for s, piece in zip(order, pieces):
        column = (place[0] ^ s) * width
        out[0, :, pl.ds(pl.multiple_of(column, width), width)] = piece[...]


def place_columns(place, pieces):
    rows, width = pieces[0].shape
    order = [0, *range(2, len(pieces)), 1]
    return pl.pallas_call(
        functools.partial(place_kernel, order),
        in_specs=[IN_SMEM] + [IN_VMEM] * len(pieces),
        out_specs=IN_VMEM,
        out_shape=jax.ShapeDtypeStruct((1, rows, width * len(pieces)), jnp.bfloat16),
        compiler_params=params(1),
        name="place",
    )(place, *near(*[pieces[s] for s in order]))


def across_chips(block, groups):
    return [block] + [
        lax.ppermute(block, "group", [(i, i ^ m) for i in range(groups)])
        for m in range(2, groups, 2)
    ]


def across_cores(held, groups):
    swap = [(i, i ^ 1) for i in range(groups)]
    return [each for block in held for each in (block, lax.ppermute(block, "group", swap))]


def per_device(latents, steps, segment_ids, mod_table, w_query, w_key, w_value):
    shards = lax.axis_size("dp")
    groups = lax.axis_size("group")
    rows = latents.shape[1]
    place = lax.axis_index("dp").astype(jnp.int32)
    mine = lax.axis_index("group").astype(jnp.int32)
    ring = [(i, (i + 1) % shards) for i in range(shards)]

    latents, place, mine = lax.optimization_barrier((latents, place[None], mine[None]))
    pieces = list(split(latents))
    query, keyval, *rest = begin(
        (w_query, w_key, w_value), segment_ids, steps, mod_table, pieces, place, shards
    )
    weights, (gain, seg_col, seg_row) = rest[:3], rest[3:]
    queries = [query]
    pieces = [lax.ppermute(piece, "dp", ring) for piece in pieces]
    pieces[0], keyval = lax.optimization_barrier((pieces[0], keyval))
    arrived = []
    for s in range(1, shards - 2):
        arrived.append(pieces)
        pieces = [lax.ppermute(piece, "dp", ring) for piece in pieces]
    query, keyval = project(arrived, gain, weights, (0, 1, 2), keyval)
    queries.append(query)
    pieces[0], keyval = lax.optimization_barrier((pieces[0], keyval))
    early = across_chips(keyval, groups)
    _, early = lax.optimization_barrier((pieces[-1], early))
    early = across_cores(early, groups)
    moved = [lax.ppermute(piece, "dp", ring) for piece in pieces]
    moved[0], early = lax.optimization_barrier((moved[0], early))
    both = [pieces, moved]
    start = lead(pieces, moved[:-1], gain, weights[1:])
    keyval = finish(pieces[-1], moved[-1], gain, weights[1:], start)
    gain, keyval = lax.optimization_barrier((gain, keyval))
    late = across_chips(keyval, groups)
    query = project(both, gain, weights, (0,))[0]
    queries.append(query)
    state = attend_early(mine, seg_col, seg_row, queries, early)
    late[1:], state = lax.optimization_barrier((late[1:], state))
    late = across_cores(late, groups)
    results = attend(shards, place, state, late)
    landed = [results[0]]
    for s in range(1, shards):
        landed.append(
            lax.ppermute(results[s], "dp", [(i, i ^ s) for i in range(shards)])
        )
    return place_columns(place, landed)


def solution(mesh):
    placed = (
        P("group", "dp", None),
        P("group"),
        P(),
        P(),
        P(None, "dp"),
        P(None, "dp"),
        P(None, "dp"),
    )
    return jax.shard_map(
        per_device, mesh=mesh, in_specs=placed, out_specs=P("group", "dp", None), check_vma=False
    )
```

```python
import functools
import math

import jax
import jax.numpy as jnp
from jax import lax
from jax.experimental import pallas as pl
from jax.experimental.pallas import tpu as pltpu
from jax.sharding import PartitionSpec as P

HD = 128
LANES = 128
EXTRA = 16
EDGES = (0, 25, 48)
CHUNKS = len(EDGES) - 1
PARTS = 4
AHEAD = 6
VMEM = pltpu.MemorySpace.VMEM
HBM = pltpu.MemorySpace.HBM
SMEM = pltpu.MemorySpace.SMEM
IN_VMEM = pl.BlockSpec(memory_space=VMEM)
IN_HBM = pl.BlockSpec(memory_space=HBM)
IN_SMEM = pl.BlockSpec(memory_space=SMEM)


def spans_of(depth):
    edges = [depth * edge // EDGES[-1] for edge in EDGES]
    return [slice(low, high) for low, high in zip(edges, edges[1:])]


def params(mebibytes):
    return pltpu.CompilerParams(vmem_limit_bytes=mebibytes * 1024 * 1024)


def near(*arrays):
    return [pltpu.with_memory_space_constraint(a, VMEM) for a in arrays]


def far(*arrays):
    return [pltpu.with_memory_space_constraint(a, HBM) for a in arrays]


def split_kernel(x_hbm, *refs):
    outs, sems = refs[:CHUNKS], refs[CHUNKS]
    copies = [
        pltpu.make_async_copy(x_hbm.at[0, :, span], out, sems.at[k])
        for k, (span, out) in enumerate(zip(spans_of(x_hbm.shape[2]), outs))
    ]
    for copy in copies:
        copy.start()
    for copy in copies:
        copy.wait()


def split(latents):
    _, rows, depth = latents.shape
    widths = [span.stop - span.start for span in spans_of(depth)]
    return pl.pallas_call(
        split_kernel,
        in_specs=[IN_HBM],
        out_specs=[IN_VMEM] * CHUNKS,
        out_shape=[VMEM((rows, width), jnp.bfloat16) for width in widths],
        scratch_shapes=[pltpu.SemaphoreType.DMA((CHUNKS,))],
        compiler_params=params(1),
        name="split",
    )(*far(latents))


def squares(piece):
    x = piece[...].astype(jnp.float32)
    return jnp.sum(x * x, axis=-1, keepdims=True)


def scale_from(total, depth):
    return lax.rsqrt(total * (1.0 / depth) + 1e-06)


def scale_of(pieces):
    depth = sum(piece.shape[1] for piece in pieces)
    return scale_from(sum(squares(piece) for piece in pieces), depth)


def modulated(piece, scale, gain, span):
    x = piece[...].astype(jnp.float32)
    return (x * scale * gain[0:1, span] + gain[1:2, span]).astype(jnp.bfloat16)


def begin_kernel(shards, place, steps, seg_hbm, table, *refs):
    sources, refs = refs[:3], refs[3:]
    pieces, refs = refs[:CHUNKS], refs[CHUNKS:]
    query, keyval = refs[:2]
    outs, (gain, seg_col, seg_row, segments, sems, small) = refs[2:5], refs[5:]
    depth = outs[0].shape[0]
    width = query.shape[1]
    chunks = spans_of(depth)
    reads = [
        pltpu.make_async_copy(table.at[steps[0]], gain, small.at[0]),
        pltpu.make_async_copy(seg_hbm, segments, small.at[1]),
    ]
    for copy in reads:
        copy.start()
    short = depth // PARTS
    spans = [slice(k * short, (k + 1) * short) for k in range(PARTS)]
    copies = [
        pltpu.make_async_copy(sources[i].at[span], outs[i].at[span], sems.at[i, k])
        for i in range(3)
        for k, span in enumerate(spans)
    ]
    for copy in copies[:AHEAD]:
        copy.start()
    for copy in reads:
        copy.wait()
    gain[0:1, :] = 1.0 + gain[0:1, :]
    scale = scale_of(pieces)
    own = jnp.concatenate(
        [modulated(piece, scale, gain, chunk) for piece, chunk in zip(pieces, chunks)], axis=1
    )
    tokc = segments.shape[1]
    rows = tokc // shards

    def owner(position):
        shard = place[0] - position // rows
        return jnp.where(shard < 0, shard + shards, shard) * rows + position % rows

    down = lax.broadcasted_iota(jnp.int32, (tokc, tokc), 0)
    across = lax.broadcasted_iota(jnp.int32, (tokc, tokc), 1)
    natural = segments[...]
    column = jnp.sum(jnp.where(down == across, natural, 0), axis=1, keepdims=True)
    seg_col[...] = jnp.sum(jnp.where(owner(down) == across, natural, 0), axis=1, keepdims=True)
    seg_row[...] = jnp.sum(jnp.where(owner(across) == down, column, 0), axis=0, keepdims=True)
    for i in range(3):
        total = None
        for k, span in enumerate(spans):
            index = i * len(spans) + k
            copies[index].wait()
            if index + AHEAD < len(copies):
                copies[index + AHEAD].start()
            part = jnp.dot(own[:, span], outs[i][span], preferred_element_type=jnp.float32)
            total = part if total is None else total + part
        if i == 0:
            query[...] = total.astype(jnp.bfloat16)
        else:
            keyval[:, (i - 1) * width : i * width] = total.astype(jnp.bfloat16)


def begin(weights, segments, steps, mod_table, pieces, place, shards):
    tokc = segments.shape[0]
    rows = pieces[0].shape[0]
    width = weights[0].shape[1]
    return pl.pallas_call(
        functools.partial(begin_kernel, shards),
        in_specs=[IN_SMEM] * 2 + [IN_HBM] * 5 + [IN_VMEM] * CHUNKS,
        out_specs=[IN_VMEM] * 8,
        out_shape=[VMEM((rows, width), jnp.bfloat16), VMEM((rows, 2 * width), jnp.bfloat16)]
        + [VMEM(w.shape, w.dtype) for w in weights]
        + [VMEM(mod_table.shape[1:], jnp.float32)]
        + [VMEM((tokc, 1), jnp.int32), VMEM((1, tokc), jnp.int32)],
        scratch_shapes=[
            pltpu.VMEM((1, tokc), jnp.int32),
            pltpu.SemaphoreType.DMA((3, PARTS)),
            pltpu.SemaphoreType.DMA((2,)),
        ],
        compiler_params=params(2 + tokc * tokc * 32 // 2**20),
        name="begin",
    )(place, steps, *far(segments[None], mod_table, *weights), *near(*pieces))


def project_kernel(count, kinds, older, *refs):
    pieces, refs = refs[: count * CHUNKS], refs[count * CHUNKS :]
    gain, weights, refs = refs[0], refs[1 : 1 + len(kinds)], refs[1 + len(kinds) :]
    if older:
        before, refs = refs[0], refs[1:]
        refs[-1][:older, :] = before[...]
    width = weights[0].shape[1]
    chunks = spans_of(weights[0].shape[0])
    shards = [pieces[s * CHUNKS : (s + 1) * CHUNKS] for s in range(count)]
    scales = [scale_of(shard) for shard in shards]
    stacked = [
        jnp.concatenate(
            [modulated(shard[k], scale, gain, chunk) for shard, scale in zip(shards, scales)],
            axis=0,
        )
        for k, chunk in enumerate(chunks)
    ]
    for kind, weight in zip(kinds, weights):
        total = None
        for rows, chunk in zip(stacked, chunks):
            part = jnp.dot(rows, weight[chunk, :], preferred_element_type=jnp.float32)
            total = part if total is None else total + part
        if kind == 0:
            refs[0][...] = total.astype(jnp.bfloat16)
        else:
            refs[-1][older:, (kind - 1) * width : kind * width] = total.astype(jnp.bfloat16)


def project(shards, gain, weights, kinds, before=None):
    count = len(shards)
    rows = shards[0][0].shape[0] * count
    older = 0 if before is None else before.shape[0]
    width = weights[0].shape[1]
    shapes = [VMEM((rows, width), jnp.bfloat16)] if 0 in kinds else []
    if 1 in kinds:
        shapes.append(VMEM((older + rows, 2 * width), jnp.bfloat16))
    pieces = [piece for shard in shards for piece in shard]
    extra = [] if before is None else [before]
    used = [weights[kind] for kind in kinds]
    return pl.pallas_call(
        functools.partial(project_kernel, count, tuple(kinds), older),
        in_specs=[IN_VMEM] * (len(pieces) + 1 + len(used) + len(extra)),
        out_specs=[IN_VMEM] * len(shapes),
        out_shape=shapes,
        compiler_params=params(max(1, 2 * count - 2)),
        name="project",
    )(*near(*pieces, gain, *used, *extra))


def lead_kernel(*refs):
    whole, refs = refs[:CHUNKS], refs[CHUNKS:]
    parts, refs = refs[: CHUNKS - 1], refs[CHUNKS - 1 :]
    gain, weights, out = refs[0], refs[1:-1], refs[-1]
    width = weights[0].shape[1]
    chunks = spans_of(weights[0].shape[0])
    rows = whole[0].shape[0]
    scale = scale_of(whole)
    row = lax.broadcasted_iota(jnp.int32, (EXTRA, 1), 0)
    stacked = []
    for k, piece in enumerate(parts):
        shift = gain[1:2, chunks[k]]
        high = shift.astype(jnp.bfloat16).astype(jnp.float32)
        added = jnp.where(row == 0, high, jnp.where(row == 1, shift - high, 0.0))
        unscaled = piece[...].astype(jnp.float32) * gain[0:1, chunks[k]]
        stacked.append(
            jnp.concatenate(
                [
                    modulated(whole[k], scale, gain, chunks[k]),
                    unscaled.astype(jnp.bfloat16),
                    added.astype(jnp.bfloat16),
                ],
                axis=0,
            )
        )
    for index, weight in enumerate(weights):
        total = sum(
            jnp.dot(lines, weight[chunk, :], preferred_element_type=jnp.float32)
            for lines, chunk in zip(stacked, chunks)
        )
        out[:, index * width : (index + 1) * width] = total
    seen = sum(squares(piece) for piece in parts)
    last = slice(len(weights) * width, len(weights) * width + LANES)
    out[:rows, last] = jnp.broadcast_to(scale, (rows, LANES))
    out[rows : 2 * rows, last] = jnp.broadcast_to(seen, (rows, LANES))


def lead(whole, parts, gain, weights):
    rows = whole[0].shape[0]
    width = weights[0].shape[1]
    return pl.pallas_call(
        lead_kernel,
        in_specs=[IN_VMEM] * (2 * CHUNKS + len(weights)),
        out_specs=IN_VMEM,
        out_shape=VMEM((2 * rows + EXTRA, len(weights) * width + LANES), jnp.float32),
        compiler_params=params(2),
        name="lead",
    )(*near(*whole, *parts, gain, *weights))


def finish_kernel(whole, piece, gain, *refs):
    weights, (start, out) = refs[:-2], refs[-2:]
    width = weights[0].shape[1]
    depth = weights[0].shape[0]
    chunk = spans_of(depth)[-1]
    rows = whole.shape[0]
    last = len(weights) * width
    scale = scale_from(start[rows : 2 * rows, last : last + 1] + squares(piece), depth)
    lines = jnp.concatenate(
        [
            modulated(whole, start[:rows, last : last + 1], gain, chunk),
            modulated(piece, scale, gain, chunk),
        ],
        axis=0,
    )
    for index, weight in enumerate(weights):
        cols = slice(index * width, (index + 1) * width)
        shift = start[2 * rows : 2 * rows + 1, cols] + start[2 * rows + 1 : 2 * rows + 2, cols]
        total = jnp.dot(lines, weight[chunk, :], preferred_element_type=jnp.float32)
        out[:rows, cols] = (total[:rows] + start[:rows, cols]).astype(jnp.bfloat16)
        known = start[rows : 2 * rows, cols] * scale + shift
        out[rows:, cols] = (total[rows:] + known).astype(jnp.bfloat16)


def finish(whole, piece, gain, weights, start):
    rows = whole.shape[0]
    width = weights[0].shape[1]
    return pl.pallas_call(
        finish_kernel,
        in_specs=[IN_VMEM] * (4 + len(weights)),
        out_specs=IN_VMEM,
        out_shape=VMEM((2 * rows, len(weights) * width), jnp.bfloat16),
        compiler_params=params(2),
        name="finish",
    )(*near(whole, piece, gain, *weights, start))


def bias_of(sources, mine, seg_col, seg_row):
    here = mine[0]
    clip = jnp.concatenate(
        [seg_row + jnp.where((here ^ m) <= here, 0, 1000) for m in range(sources)], axis=1
    )
    return jnp.where(seg_col == clip, 0.0, -1e30)


def stack(blocks, out):
    many = blocks[0].shape[0]
    for m, block in enumerate(blocks):
        out[m * many : (m + 1) * many, :] = block[...]


def blocks_of(tokc):
    block = min(tokc, 128)
    return [slice(start, start + block) for start in range(0, tokc, block)]


def weigh(queries, keys, values, bias, floors):
    scores = [
        lax.dot_general(q, k, (((1,), (1,)), ((), ())), preferred_element_type=jnp.float32)
        for q, k in zip(queries, keys)
    ]
    scores = [s * (1.0 / math.sqrt(HD)) + bias for s in scores]
    bests = [jnp.max(s, axis=-1, keepdims=True) for s in scores]
    if floors is not None:
        bests = [jnp.maximum(best, floor) for best, floor in zip(bests, floors)]
    weights = [jnp.exp(s - best) for s, best in zip(scores, bests)]
    sums = [
        jnp.dot(w.astype(jnp.bfloat16), v, preferred_element_type=jnp.float32)
        for w, v in zip(weights, values)
    ]
    totals = [jnp.sum(w, axis=-1, keepdims=True) for w in weights]
    return bests, totals, sums


def columns(ref, span, count, start=0):
    return [ref[span, start + h * HD : start + (h + 1) * HD] for h in range(count)]


def attend_early_kernel(parts, sources, mine, seg_col, seg_row, *refs):
    queries, refs = refs[:parts], refs[parts:]
    early, refs = refs[:sources], refs[sources:]
    q_all, sums, bests, totals, bias_late, kv_all = refs
    filled = 0
    for query in queries:
        q_all[filled : filled + query.shape[0], :] = query[...]
        filled += query.shape[0]
    stack(early, kv_all)
    many = early[0].shape[0]
    heads = q_all.shape[1] // HD
    every = slice(0, kv_all.shape[0])
    for span in blocks_of(q_all.shape[0]):
        bias = bias_of(sources, mine, seg_col[span, :], seg_row[:, :many])
        state = weigh(
            columns(q_all, span, heads),
            columns(kv_all, every, heads),
            columns(kv_all, every, heads, heads * HD),
            bias,
            None,
        )
        for h, (best, total, summed) in enumerate(zip(*state)):
            bests[span, h * HD : (h + 1) * HD] = jnp.broadcast_to(best, summed.shape)
            totals[span, h * HD : (h + 1) * HD] = jnp.broadcast_to(total, summed.shape)
            sums[span, h * HD : (h + 1) * HD] = summed
        bias_late[span, :] = bias_of(sources, mine, seg_col[span, :], seg_row[:, many:])


def attend_early(mine, seg_col, seg_row, queries, early):
    sources, many = len(early), early[0].shape[0]
    tokc, width = seg_col.shape[0], queries[0].shape[1]
    return pl.pallas_call(
        functools.partial(attend_early_kernel, len(queries), sources),
        in_specs=[IN_SMEM] + [IN_VMEM] * (2 + len(queries) + sources),
        out_specs=[IN_VMEM] * 5,
        out_shape=[VMEM((tokc, width), jnp.bfloat16)]
        + [VMEM((tokc, width), jnp.float32)] * 3
        + [VMEM((tokc, sources * (tokc - many)), jnp.float32)],
        scratch_shapes=[pltpu.VMEM((sources * many, 2 * width), jnp.bfloat16)],
        compiler_params=params(3 * (sources * tokc // 1024)),
        name="attend_early",
    )(mine, *near(seg_col, seg_row, *queries, *early))


def attend_kernel(shards, sources, place, q_all, sums, bests, totals, bias, *refs):
    late, outs, kv_all, held = refs[:sources], refs[sources:-2], refs[-2], refs[-1]
    tokc, width = q_all.shape
    rows = tokc // shards
    heads = width // HD
    stack(late, kv_all)
    every = slice(0, kv_all.shape[0])
    for span in blocks_of(tokc):
        floors = [floor[:, 0:1] for floor in columns(bests, span, heads)]
        state = weigh(
            columns(q_all, span, heads),
            columns(kv_all, every, heads),
            columns(kv_all, every, heads, heads * HD),
            bias[span, :],
            floors,
        )
        before = zip(floors, columns(totals, span, heads), columns(sums, span, heads))
        for h, (best, total, summed) in enumerate(zip(*state)):
            floor, old_total, old_sum = next(before)
            fade = jnp.exp(floor - best)
            scale = 1.0 / (total + old_total[:, 0:1] * fade)
            result = ((summed + old_sum * fade) * scale).astype(jnp.bfloat16)
            held[span, h * HD : (h + 1) * HD] = result
    for m, out in enumerate(outs):
        spot = lax.rem(place[0] - (place[0] ^ m) + shards, shards) * rows
        out[...] = held[pl.ds(pl.multiple_of(spot, rows), rows), :]


def attend(shards, place, state, late):
    sources, many = len(late), late[0].shape[0]
    tokc, width = state[0].shape
    rows = tokc // shards
    return pl.pallas_call(
        functools.partial(attend_kernel, shards, sources),
        in_specs=[IN_SMEM] + [IN_VMEM] * (len(state) + sources),
        out_specs=[IN_VMEM] * shards,
        out_shape=[VMEM((rows, width), jnp.bfloat16)] * shards,
        scratch_shapes=[
            pltpu.VMEM((sources * many, 2 * width), jnp.bfloat16),
            pltpu.VMEM((tokc, width), jnp.bfloat16),
        ],
        compiler_params=params(3 * (sources * tokc // 1024)),
        name="attend",
    )(place, *near(*state, *late))


def place_kernel(order, place, *refs):
    pieces, out = refs[:-1], refs[-1]
    width = pieces[0].shape[1]
    count = len(pieces)
    for s, piece in zip(order, pieces):
        column = (place[0] ^ s) * width
        out[0, :, pl.ds(pl.multiple_of(column, width), width)] = piece[...]


def place_columns(place, pieces):
    rows, width = pieces[0].shape
    order = [0, *range(2, len(pieces)), 1]
    return pl.pallas_call(
        functools.partial(place_kernel, order),
        in_specs=[IN_SMEM] + [IN_VMEM] * len(pieces),
        out_specs=IN_VMEM,
        out_shape=jax.ShapeDtypeStruct((1, rows, width * len(pieces)), jnp.bfloat16),
        compiler_params=params(1),
        name="place",
    )(place, *near(*[pieces[s] for s in order]))


def across_chips(block, groups):
    return [block] + [
        lax.ppermute(block, "group", [(i, i ^ m) for i in range(groups)])
        for m in range(2, groups, 2)
    ]


def across_cores(held, groups):
    swap = [(i, i ^ 1) for i in range(groups)]
    return [each for block in held for each in (block, lax.ppermute(block, "group", swap))]


def per_device(latents, steps, segment_ids, mod_table, w_query, w_key, w_value):
    shards = lax.axis_size("dp")
    groups = lax.axis_size("group")
    rows = latents.shape[1]
    place = lax.axis_index("dp").astype(jnp.int32)
    mine = lax.axis_index("group").astype(jnp.int32)
    ring = [(i, (i + 1) % shards) for i in range(shards)]

    latents, place, mine = lax.optimization_barrier((latents, place[None], mine[None]))
    pieces = list(split(latents))
    query, keyval, *rest = begin(
        (w_query, w_key, w_value), segment_ids, steps, mod_table, pieces, place, shards
    )
    weights, (gain, seg_col, seg_row) = rest[:3], rest[3:]
    queries = [query]
    pieces = [lax.ppermute(piece, "dp", ring) for piece in pieces]
    pieces[0], keyval = lax.optimization_barrier((pieces[0], keyval))
    arrived = []
    for s in range(1, shards - 2):
        arrived.append(pieces)
        pieces = [lax.ppermute(piece, "dp", ring) for piece in pieces]
    query, keyval = project(arrived, gain, weights, (0, 1, 2), keyval)
    queries.append(query)
    pieces[0], keyval = lax.optimization_barrier((pieces[0], keyval))
    early = across_chips(keyval, groups)
    _, early = lax.optimization_barrier((pieces[-1], early))
    early = across_cores(early, groups)
    moved = [lax.ppermute(piece, "dp", ring) for piece in pieces]
    moved[0], early = lax.optimization_barrier((moved[0], early))
    both = [pieces, moved]
    start = lead(pieces, moved[:-1], gain, weights[1:])
    keyval = finish(pieces[-1], moved[-1], gain, weights[1:], start)
    gain, keyval = lax.optimization_barrier((gain, keyval))
    late = across_chips(keyval, groups)
    query = project(both, gain, weights, (0,))[0]
    queries.append(query)
    state = attend_early(mine, seg_col, seg_row, queries, early)
    late[1:] = [lax.optimization_barrier((block, state[0]))[0] for block in late[1:]]
    late = across_cores(late, groups)
    results = attend(shards, place, state, late)
    landed = [results[0]]
    for s in range(1, shards):
        landed.append(
            lax.ppermute(results[s], "dp", [(i, i ^ s) for i in range(shards)])
        )
    return place_columns(place, landed)


def solution(mesh):
    placed = (
        P("group", "dp", None),
        P("group"),
        P(),
        P(),
        P(None, "dp"),
        P(None, "dp"),
        P(None, "dp"),
    )
    return jax.shard_map(
        per_device, mesh=mesh, in_specs=placed, out_specs=P("group", "dp", None), check_vma=False
    )
```

```python
import functools
import math

import jax
import jax.numpy as jnp
from jax import lax
from jax.experimental import pallas as pl
from jax.experimental.pallas import tpu as pltpu
from jax.sharding import PartitionSpec as P

HD = 128
LANES = 128
EXTRA = 16
EDGES = (0, 1, 2)
CHUNKS = len(EDGES) - 1
PARTS = 4
AHEAD = 6
VMEM = pltpu.MemorySpace.VMEM
HBM = pltpu.MemorySpace.HBM
SMEM = pltpu.MemorySpace.SMEM
IN_VMEM = pl.BlockSpec(memory_space=VMEM)
IN_HBM = pl.BlockSpec(memory_space=HBM)
IN_SMEM = pl.BlockSpec(memory_space=SMEM)


def spans_of(depth):
    edges = [depth * edge // EDGES[-1] for edge in EDGES]
    return [slice(low, high) for low, high in zip(edges, edges[1:])]


def params(mebibytes):
    return pltpu.CompilerParams(vmem_limit_bytes=mebibytes * 1024 * 1024)


def near(*arrays):
    return [pltpu.with_memory_space_constraint(a, VMEM) for a in arrays]


def far(*arrays):
    return [pltpu.with_memory_space_constraint(a, HBM) for a in arrays]


def split_kernel(x_hbm, *refs):
    outs, sems = refs[:CHUNKS], refs[CHUNKS]
    copies = [
        pltpu.make_async_copy(x_hbm.at[0, :, span], out, sems.at[k])
        for k, (span, out) in enumerate(zip(spans_of(x_hbm.shape[2]), outs))
    ]
    for copy in copies:
        copy.start()
    for copy in copies:
        copy.wait()


def split(latents):
    _, rows, depth = latents.shape
    widths = [span.stop - span.start for span in spans_of(depth)]
    return pl.pallas_call(
        split_kernel,
        in_specs=[IN_HBM],
        out_specs=[IN_VMEM] * CHUNKS,
        out_shape=[VMEM((rows, width), jnp.bfloat16) for width in widths],
        scratch_shapes=[pltpu.SemaphoreType.DMA((CHUNKS,))],
        compiler_params=params(1),
        name="split",
    )(*far(latents))


def squares(piece):
    x = piece[...].astype(jnp.float32)
    return jnp.sum(x * x, axis=-1, keepdims=True)


def scale_from(total, depth):
    return lax.rsqrt(total * (1.0 / depth) + 1e-06)


def scale_of(pieces):
    depth = sum(piece.shape[1] for piece in pieces)
    return scale_from(sum(squares(piece) for piece in pieces), depth)


def modulated(piece, scale, gain, span):
    x = piece[...].astype(jnp.float32)
    return (x * scale * gain[0:1, span] + gain[1:2, span]).astype(jnp.bfloat16)


def begin_kernel(shards, place, steps, seg_hbm, table, *refs):
    sources, refs = refs[:3], refs[3:]
    pieces, refs = refs[:CHUNKS], refs[CHUNKS:]
    query, keyval = refs[:2]
    outs, (gain, seg_col, seg_row, segments, sems, small) = refs[2:5], refs[5:]
    depth = outs[0].shape[0]
    width = query.shape[1]
    chunks = spans_of(depth)
    reads = [
        pltpu.make_async_copy(table.at[steps[0]], gain, small.at[0]),
        pltpu.make_async_copy(seg_hbm, segments, small.at[1]),
    ]
    for copy in reads:
        copy.start()
    short = depth // PARTS
    spans = [slice(k * short, (k + 1) * short) for k in range(PARTS)]
    copies = [
        pltpu.make_async_copy(sources[i].at[span], outs[i].at[span], sems.at[i, k])
        for i in range(3)
        for k, span in enumerate(spans)
    ]
    for copy in copies[:AHEAD]:
        copy.start()
    for copy in reads:
        copy.wait()
    gain[0:1, :] = 1.0 + gain[0:1, :]
    scale = scale_of(pieces)
    own = jnp.concatenate(
        [modulated(piece, scale, gain, chunk) for piece, chunk in zip(pieces, chunks)], axis=1
    )
    tokc = segments.shape[1]
    rows = tokc // shards

    def owner(position):
        shard = place[0] - position // rows
        return jnp.where(shard < 0, shard + shards, shard) * rows + position % rows

    down = lax.broadcasted_iota(jnp.int32, (tokc, tokc), 0)
    across = lax.broadcasted_iota(jnp.int32, (tokc, tokc), 1)
    natural = segments[...]
    column = jnp.sum(jnp.where(down == across, natural, 0), axis=1, keepdims=True)
    seg_col[...] = jnp.sum(jnp.where(owner(down) == across, natural, 0), axis=1, keepdims=True)
    seg_row[...] = jnp.sum(jnp.where(owner(across) == down, column, 0), axis=0, keepdims=True)
    for i in range(3):
        total = None
        for k, span in enumerate(spans):
            index = i * len(spans) + k
            copies[index].wait()
            if index + AHEAD < len(copies):
                copies[index + AHEAD].start()
            part = jnp.dot(own[:, span], outs[i][span], preferred_element_type=jnp.float32)
            total = part if total is None else total + part
        if i == 0:
            query[...] = total.astype(jnp.bfloat16)
        else:
            keyval[:, (i - 1) * width : i * width] = total.astype(jnp.bfloat16)


def begin(weights, segments, steps, mod_table, pieces, place, shards):
    tokc = segments.shape[0]
    rows = pieces[0].shape[0]
    width = weights[0].shape[1]
    return pl.pallas_call(
        functools.partial(begin_kernel, shards),
        in_specs=[IN_SMEM] * 2 + [IN_HBM] * 5 + [IN_VMEM] * CHUNKS,
        out_specs=[IN_VMEM] * 8,
        out_shape=[VMEM((rows, width), jnp.bfloat16), VMEM((rows, 2 * width), jnp.bfloat16)]
        + [VMEM(w.shape, w.dtype) for w in weights]
        + [VMEM(mod_table.shape[1:], jnp.float32)]
        + [VMEM((tokc, 1), jnp.int32), VMEM((1, tokc), jnp.int32)],
        scratch_shapes=[
            pltpu.VMEM((1, tokc), jnp.int32),
            pltpu.SemaphoreType.DMA((3, PARTS)),
            pltpu.SemaphoreType.DMA((2,)),
        ],
        compiler_params=params(2 + tokc * tokc * 32 // 2**20),
        name="begin",
    )(place, steps, *far(segments[None], mod_table, *weights), *near(*pieces))


def project_kernel(count, kinds, older, *refs):
    pieces, refs = refs[: count * CHUNKS], refs[count * CHUNKS :]
    gain, weights, refs = refs[0], refs[1 : 1 + len(kinds)], refs[1 + len(kinds) :]
    if older:
        before, refs = refs[0], refs[1:]
        refs[-1][:older, :] = before[...]
    width = weights[0].shape[1]
    chunks = spans_of(weights[0].shape[0])
    shards = [pieces[s * CHUNKS : (s + 1) * CHUNKS] for s in range(count)]
    scales = [scale_of(shard) for shard in shards]
    stacked = [
        jnp.concatenate(
            [modulated(shard[k], scale, gain, chunk) for shard, scale in zip(shards, scales)],
            axis=0,
        )
        for k, chunk in enumerate(chunks)
    ]
    for kind, weight in zip(kinds, weights):
        total = None
        for rows, chunk in zip(stacked, chunks):
            part = jnp.dot(rows, weight[chunk, :], preferred_element_type=jnp.float32)
            total = part if total is None else total + part
        if kind == 0:
            refs[0][...] = total.astype(jnp.bfloat16)
        else:
            refs[-1][older:, (kind - 1) * width : kind * width] = total.astype(jnp.bfloat16)


def project(shards, gain, weights, kinds, before=None):
    count = len(shards)
    rows = shards[0][0].shape[0] * count
    older = 0 if before is None else before.shape[0]
    width = weights[0].shape[1]
    shapes = [VMEM((rows, width), jnp.bfloat16)] if 0 in kinds else []
    if 1 in kinds:
        shapes.append(VMEM((older + rows, 2 * width), jnp.bfloat16))
    pieces = [piece for shard in shards for piece in shard]
    extra = [] if before is None else [before]
    used = [weights[kind] for kind in kinds]
    return pl.pallas_call(
        functools.partial(project_kernel, count, tuple(kinds), older),
        in_specs=[IN_VMEM] * (len(pieces) + 1 + len(used) + len(extra)),
        out_specs=[IN_VMEM] * len(shapes),
        out_shape=shapes,
        compiler_params=params(max(1, 2 * count - 2)),
        name="project",
    )(*near(*pieces, gain, *used, *extra))


def lead_kernel(*refs):
    whole, refs = refs[:CHUNKS], refs[CHUNKS:]
    parts, refs = refs[: CHUNKS - 1], refs[CHUNKS - 1 :]
    gain, weights, out = refs[0], refs[1:-1], refs[-1]
    width = weights[0].shape[1]
    chunks = spans_of(weights[0].shape[0])
    rows = whole[0].shape[0]
    scale = scale_of(whole)
    row = lax.broadcasted_iota(jnp.int32, (EXTRA, 1), 0)
    stacked = []
    for k, piece in enumerate(parts):
        shift = gain[1:2, chunks[k]]
        high = shift.astype(jnp.bfloat16).astype(jnp.float32)
        added = jnp.where(row == 0, high, jnp.where(row == 1, shift - high, 0.0))
        unscaled = piece[...].astype(jnp.float32) * gain[0:1, chunks[k]]
        stacked.append(
            jnp.concatenate(
                [
                    modulated(whole[k], scale, gain, chunks[k]),
                    unscaled.astype(jnp.bfloat16),
                    added.astype(jnp.bfloat16),
                ],
                axis=0,
            )
        )
    for index, weight in enumerate(weights):
        total = sum(
            jnp.dot(lines, weight[chunk, :], preferred_element_type=jnp.float32)
            for lines, chunk in zip(stacked, chunks)
        )
        out[:, index * width : (index + 1) * width] = total
    seen = sum(squares(piece) for piece in parts)
    last = slice(len(weights) * width, len(weights) * width + LANES)
    out[:rows, last] = jnp.broadcast_to(scale, (rows, LANES))
    out[rows : 2 * rows, last] = jnp.broadcast_to(seen, (rows, LANES))


def lead(whole, parts, gain, weights):
    rows = whole[0].shape[0]
    width = weights[0].shape[1]
    return pl.pallas_call(
        lead_kernel,
        in_specs=[IN_VMEM] * (2 * CHUNKS + len(weights)),
        out_specs=IN_VMEM,
        out_shape=VMEM((2 * rows + EXTRA, len(weights) * width + LANES), jnp.float32),
        compiler_params=params(2),
        name="lead",
    )(*near(*whole, *parts, gain, *weights))


def finish_kernel(whole, piece, gain, *refs):
    weights, (start, out) = refs[:-2], refs[-2:]
    width = weights[0].shape[1]
    depth = weights[0].shape[0]
    chunk = spans_of(depth)[-1]
    rows = whole.shape[0]
    last = len(weights) * width
    scale = scale_from(start[rows : 2 * rows, last : last + 1] + squares(piece), depth)
    lines = jnp.concatenate(
        [
            modulated(whole, start[:rows, last : last + 1], gain, chunk),
            modulated(piece, scale, gain, chunk),
        ],
        axis=0,
    )
    for index, weight in enumerate(weights):
        cols = slice(index * width, (index + 1) * width)
        shift = start[2 * rows : 2 * rows + 1, cols] + start[2 * rows + 1 : 2 * rows + 2, cols]
        total = jnp.dot(lines, weight[chunk, :], preferred_element_type=jnp.float32)
        out[:rows, cols] = (total[:rows] + start[:rows, cols]).astype(jnp.bfloat16)
        known = start[rows : 2 * rows, cols] * scale + shift
        out[rows:, cols] = (total[rows:] + known).astype(jnp.bfloat16)


def finish(whole, piece, gain, weights, start):
    rows = whole.shape[0]
    width = weights[0].shape[1]
    return pl.pallas_call(
        finish_kernel,
        in_specs=[IN_VMEM] * (4 + len(weights)),
        out_specs=IN_VMEM,
        out_shape=VMEM((2 * rows, len(weights) * width), jnp.bfloat16),
        compiler_params=params(2),
        name="finish",
    )(*near(whole, piece, gain, *weights, start))


def bias_of(sources, mine, seg_col, seg_row):
    here = mine[0]
    clip = jnp.concatenate(
        [seg_row + jnp.where((here ^ m) <= here, 0, 1000) for m in range(sources)], axis=1
    )
    return jnp.where(seg_col == clip, 0.0, -1e30)


def stack(blocks, out):
    many = blocks[0].shape[0]
    for m, block in enumerate(blocks):
        out[m * many : (m + 1) * many, :] = block[...]


def blocks_of(tokc):
    block = min(tokc, 128)
    return [slice(start, start + block) for start in range(0, tokc, block)]


def weigh(queries, keys, values, bias, floors):
    scores = [
        lax.dot_general(q, k, (((1,), (1,)), ((), ())), preferred_element_type=jnp.float32)
        for q, k in zip(queries, keys)
    ]
    scores = [s * (1.0 / math.sqrt(HD)) + bias for s in scores]
    bests = [jnp.max(s, axis=-1, keepdims=True) for s in scores]
    if floors is not None:
        bests = [jnp.maximum(best, floor) for best, floor in zip(bests, floors)]
    weights = [jnp.exp(s - best) for s, best in zip(scores, bests)]
    sums = [
        jnp.dot(w.astype(jnp.bfloat16), v, preferred_element_type=jnp.float32)
        for w, v in zip(weights, values)
    ]
    totals = [jnp.sum(w, axis=-1, keepdims=True) for w in weights]
    return bests, totals, sums


def columns(ref, span, count, start=0):
    return [ref[span, start + h * HD : start + (h + 1) * HD] for h in range(count)]


def attend_early_kernel(parts, sources, mine, seg_col, seg_row, *refs):
    queries, refs = refs[:parts], refs[parts:]
    early, refs = refs[:sources], refs[sources:]
    q_all, sums, bests, totals, bias_late, kv_all = refs
    filled = 0
    for query in queries:
        q_all[filled : filled + query.shape[0], :] = query[...]
        filled += query.shape[0]
    stack(early, kv_all)
    many = early[0].shape[0]
    heads = q_all.shape[1] // HD
    every = slice(0, kv_all.shape[0])
    for span in blocks_of(q_all.shape[0]):
        bias = bias_of(sources, mine, seg_col[span, :], seg_row[:, :many])
        state = weigh(
            columns(q_all, span, heads),
            columns(kv_all, every, heads),
            columns(kv_all, every, heads, heads * HD),
            bias,
            None,
        )
        for h, (best, total, summed) in enumerate(zip(*state)):
            bests[span, h * HD : (h + 1) * HD] = jnp.broadcast_to(best, summed.shape)
            totals[span, h * HD : (h + 1) * HD] = jnp.broadcast_to(total, summed.shape)
            sums[span, h * HD : (h + 1) * HD] = summed
        bias_late[span, :] = bias_of(sources, mine, seg_col[span, :], seg_row[:, many:])


def attend_early(mine, seg_col, seg_row, queries, early):
    sources, many = len(early), early[0].shape[0]
    tokc, width = seg_col.shape[0], queries[0].shape[1]
    return pl.pallas_call(
        functools.partial(attend_early_kernel, len(queries), sources),
        in_specs=[IN_SMEM] + [IN_VMEM] * (2 + len(queries) + sources),
        out_specs=[IN_VMEM] * 5,
        out_shape=[VMEM((tokc, width), jnp.bfloat16)]
        + [VMEM((tokc, width), jnp.float32)] * 3
        + [VMEM((tokc, sources * (tokc - many)), jnp.float32)],
        scratch_shapes=[pltpu.VMEM((sources * many, 2 * width), jnp.bfloat16)],
        compiler_params=params(3 * (sources * tokc // 1024)),
        name="attend_early",
    )(mine, *near(seg_col, seg_row, *queries, *early))


def attend_kernel(shards, sources, place, q_all, sums, bests, totals, bias, *refs):
    late, outs, kv_all, held = refs[:sources], refs[sources:-2], refs[-2], refs[-1]
    tokc, width = q_all.shape
    rows = tokc // shards
    heads = width // HD
    stack(late, kv_all)
    every = slice(0, kv_all.shape[0])
    for span in blocks_of(tokc):
        floors = [floor[:, 0:1] for floor in columns(bests, span, heads)]
        state = weigh(
            columns(q_all, span, heads),
            columns(kv_all, every, heads),
            columns(kv_all, every, heads, heads * HD),
            bias[span, :],
            floors,
        )
        before = zip(floors, columns(totals, span, heads), columns(sums, span, heads))
        for h, (best, total, summed) in enumerate(zip(*state)):
            floor, old_total, old_sum = next(before)
            fade = jnp.exp(floor - best)
            scale = 1.0 / (total + old_total[:, 0:1] * fade)
            result = ((summed + old_sum * fade) * scale).astype(jnp.bfloat16)
            held[span, h * HD : (h + 1) * HD] = result
    for m, out in enumerate(outs):
        spot = lax.rem(place[0] - (place[0] ^ m) + shards, shards) * rows
        out[...] = held[pl.ds(pl.multiple_of(spot, rows), rows), :]


def attend(shards, place, state, late):
    sources, many = len(late), late[0].shape[0]
    tokc, width = state[0].shape
    rows = tokc // shards
    return pl.pallas_call(
        functools.partial(attend_kernel, shards, sources),
        in_specs=[IN_SMEM] + [IN_VMEM] * (len(state) + sources),
        out_specs=[IN_VMEM] * shards,
        out_shape=[VMEM((rows, width), jnp.bfloat16)] * shards,
        scratch_shapes=[
            pltpu.VMEM((sources * many, 2 * width), jnp.bfloat16),
            pltpu.VMEM((tokc, width), jnp.bfloat16),
        ],
        compiler_params=params(3 * (sources * tokc // 1024)),
        name="attend",
    )(place, *near(*state, *late))


def place_kernel(order, place, *refs):
    pieces, out = refs[:-1], refs[-1]
    width = pieces[0].shape[1]
    count = len(pieces)
    for s, piece in zip(order, pieces):
        column = (place[0] ^ s) * width
        out[0, :, pl.ds(pl.multiple_of(column, width), width)] = piece[...]


def place_columns(place, pieces):
    rows, width = pieces[0].shape
    order = [0, *range(2, len(pieces)), 1]
    return pl.pallas_call(
        functools.partial(place_kernel, order),
        in_specs=[IN_SMEM] + [IN_VMEM] * len(pieces),
        out_specs=IN_VMEM,
        out_shape=jax.ShapeDtypeStruct((1, rows, width * len(pieces)), jnp.bfloat16),
        compiler_params=params(1),
        name="place",
    )(place, *near(*[pieces[s] for s in order]))


def across_chips(block, groups):
    return [block] + [
        lax.ppermute(block, "group", [(i, i ^ m) for i in range(groups)])
        for m in range(2, groups, 2)
    ]


def across_cores(held, groups):
    swap = [(i, i ^ 1) for i in range(groups)]
    return [each for block in held for each in (block, lax.ppermute(block, "group", swap))]


def per_device(latents, steps, segment_ids, mod_table, w_query, w_key, w_value):
    shards = lax.axis_size("dp")
    groups = lax.axis_size("group")
    rows = latents.shape[1]
    place = lax.axis_index("dp").astype(jnp.int32)
    mine = lax.axis_index("group").astype(jnp.int32)
    ring = [(i, (i + 1) % shards) for i in range(shards)]

    latents, place, mine = lax.optimization_barrier((latents, place[None], mine[None]))
    pieces = list(split(latents))
    query, keyval, *rest = begin(
        (w_query, w_key, w_value), segment_ids, steps, mod_table, pieces, place, shards
    )
    weights, (gain, seg_col, seg_row) = rest[:3], rest[3:]
    queries = [query]
    pieces = [lax.ppermute(piece, "dp", ring) for piece in pieces]
    pieces[0], keyval = lax.optimization_barrier((pieces[0], keyval))
    arrived = []
    for s in range(1, shards - 2):
        arrived.append(pieces)
        pieces = [lax.ppermute(piece, "dp", ring) for piece in pieces]
    query, keyval = project(arrived, gain, weights, (0, 1, 2), keyval)
    queries.append(query)
    pieces[0], _ = lax.optimization_barrier((pieces[0], keyval))
    early = across_chips(keyval, groups)
    _, early = lax.optimization_barrier((pieces[-1], early))
    early = across_cores(early, groups)
    moved = [lax.ppermute(piece, "dp", ring) for piece in pieces]
    moved[0], early = lax.optimization_barrier((moved[0], early))
    both = [pieces, moved]
    start = lead(pieces, moved[:-1], gain, weights[1:])
    keyval = finish(pieces[-1], moved[-1], gain, weights[1:], start)
    gain, keyval = lax.optimization_barrier((gain, keyval))
    late = across_chips(keyval, groups)
    query = project(both, gain, weights, (0,))[0]
    queries.append(query)
    state = attend_early(mine, seg_col, seg_row, queries, early)
    late[1:] = [lax.optimization_barrier((block, state[0]))[0] for block in late[1:]]
    late = across_cores(late, groups)
    results = attend(shards, place, state, late)
    landed = [results[0]]
    for s in range(1, shards):
        landed.append(
            lax.ppermute(results[s], "dp", [(i, i ^ s) for i in range(shards)])
        )
    return place_columns(place, landed)


def solution(mesh):
    placed = (
        P("group", "dp", None),
        P("group"),
        P(),
        P(),
        P(None, "dp"),
        P(None, "dp"),
        P(None, "dp"),
    )
    return jax.shard_map(
        per_device, mesh=mesh, in_specs=placed, out_specs=P("group", "dp", None), check_vma=False
    )
```

```python
import functools
import math

import jax
import jax.numpy as jnp
from jax import lax
from jax.experimental import pallas as pl
from jax.experimental.pallas import tpu as pltpu
from jax.sharding import PartitionSpec as P

HD = 128
LANES = 128
EXTRA = 16
EDGES = (0, 1, 2)
CHUNKS = len(EDGES) - 1
PARTS = 4
AHEAD = 6
VMEM = pltpu.MemorySpace.VMEM
HBM = pltpu.MemorySpace.HBM
SMEM = pltpu.MemorySpace.SMEM
IN_VMEM = pl.BlockSpec(memory_space=VMEM)
IN_HBM = pl.BlockSpec(memory_space=HBM)
IN_SMEM = pl.BlockSpec(memory_space=SMEM)


def spans_of(depth):
    edges = [depth * edge // EDGES[-1] for edge in EDGES]
    return [slice(low, high) for low, high in zip(edges, edges[1:])]


def params(mebibytes):
    return pltpu.CompilerParams(vmem_limit_bytes=mebibytes * 1024 * 1024)


def near(*arrays):
    return [pltpu.with_memory_space_constraint(a, VMEM) for a in arrays]


def far(*arrays):
    return [pltpu.with_memory_space_constraint(a, HBM) for a in arrays]


def split_kernel(x_hbm, *refs):
    outs, sems = refs[:CHUNKS], refs[CHUNKS]
    copies = [
        pltpu.make_async_copy(x_hbm.at[0, :, span], out, sems.at[k])
        for k, (span, out) in enumerate(zip(spans_of(x_hbm.shape[2]), outs))
    ]
    for copy in copies:
        copy.start()
    for copy in copies:
        copy.wait()


def split(latents):
    _, rows, depth = latents.shape
    widths = [span.stop - span.start for span in spans_of(depth)]
    return pl.pallas_call(
        split_kernel,
        in_specs=[IN_HBM],
        out_specs=[IN_VMEM] * CHUNKS,
        out_shape=[VMEM((rows, width), jnp.bfloat16) for width in widths],
        scratch_shapes=[pltpu.SemaphoreType.DMA((CHUNKS,))],
        compiler_params=params(1),
        name="split",
    )(*far(latents))


def squares(piece):
    x = piece[...].astype(jnp.float32)
    return jnp.sum(x * x, axis=-1, keepdims=True)


def scale_from(total, depth):
    return lax.rsqrt(total * (1.0 / depth) + 1e-06)


def scale_of(pieces):
    depth = sum(piece.shape[1] for piece in pieces)
    return scale_from(sum(squares(piece) for piece in pieces), depth)


def modulated(piece, scale, gain, span):
    x = piece[...].astype(jnp.float32)
    return (x * scale * gain[0:1, span] + gain[1:2, span]).astype(jnp.bfloat16)


def begin_kernel(shards, place, steps, seg_hbm, table, *refs):
    sources, refs = refs[:3], refs[3:]
    pieces, refs = refs[:CHUNKS], refs[CHUNKS:]
    query, keyval = refs[:2]
    outs, (gain, seg_col, seg_row, segments, sems, small) = refs[2:5], refs[5:]
    depth = outs[0].shape[0]
    width = query.shape[1]
    chunks = spans_of(depth)
    reads = [
        pltpu.make_async_copy(table.at[steps[0]], gain, small.at[0]),
        pltpu.make_async_copy(seg_hbm, segments, small.at[1]),
    ]
    for copy in reads:
        copy.start()
    short = depth // PARTS
    spans = [slice(k * short, (k + 1) * short) for k in range(PARTS)]
    copies = [
        pltpu.make_async_copy(sources[i].at[span], outs[i].at[span], sems.at[i, k])
        for i in range(3)
        for k, span in enumerate(spans)
    ]
    for copy in copies[:AHEAD]:
        copy.start()
    for copy in reads:
        copy.wait()
    gain[0:1, :] = 1.0 + gain[0:1, :]
    scale = scale_of(pieces)
    own = jnp.concatenate(
        [modulated(piece, scale, gain, chunk) for piece, chunk in zip(pieces, chunks)], axis=1
    )
    tokc = segments.shape[1]
    rows = tokc // shards

    def owner(position):
        shard = place[0] - position // rows
        return jnp.where(shard < 0, shard + shards, shard) * rows + position % rows

    down = lax.broadcasted_iota(jnp.int32, (tokc, tokc), 0)
    across = lax.broadcasted_iota(jnp.int32, (tokc, tokc), 1)
    natural = segments[...]
    column = jnp.sum(jnp.where(down == across, natural, 0), axis=1, keepdims=True)
    seg_col[...] = jnp.sum(jnp.where(owner(down) == across, natural, 0), axis=1, keepdims=True)
    seg_row[...] = jnp.sum(jnp.where(owner(across) == down, column, 0), axis=0, keepdims=True)
    for i in range(3):
        total = None
        for k, span in enumerate(spans):
            index = i * len(spans) + k
            copies[index].wait()
            if index + AHEAD < len(copies):
                copies[index + AHEAD].start()
            part = jnp.dot(own[:, span], outs[i][span], preferred_element_type=jnp.float32)
            total = part if total is None else total + part
        if i == 0:
            query[...] = total.astype(jnp.bfloat16)
        else:
            keyval[:, (i - 1) * width : i * width] = total.astype(jnp.bfloat16)


def begin(weights, segments, steps, mod_table, pieces, place, shards):
    tokc = segments.shape[0]
    rows = pieces[0].shape[0]
    width = weights[0].shape[1]
    return pl.pallas_call(
        functools.partial(begin_kernel, shards),
        in_specs=[IN_SMEM] * 2 + [IN_HBM] * 5 + [IN_VMEM] * CHUNKS,
        out_specs=[IN_VMEM] * 8,
        out_shape=[VMEM((rows, width), jnp.bfloat16), VMEM((rows, 2 * width), jnp.bfloat16)]
        + [VMEM(w.shape, w.dtype) for w in weights]
        + [VMEM(mod_table.shape[1:], jnp.float32)]
        + [VMEM((tokc, 1), jnp.int32), VMEM((1, tokc), jnp.int32)],
        scratch_shapes=[
            pltpu.VMEM((1, tokc), jnp.int32),
            pltpu.SemaphoreType.DMA((3, PARTS)),
            pltpu.SemaphoreType.DMA((2,)),
        ],
        compiler_params=params(2 + tokc * tokc * 32 // 2**20),
        name="begin",
    )(place, steps, *far(segments[None], mod_table, *weights), *near(*pieces))


def project_kernel(count, kinds, older, *refs):
    pieces, refs = refs[: count * CHUNKS], refs[count * CHUNKS :]
    gain, weights, refs = refs[0], refs[1 : 1 + len(kinds)], refs[1 + len(kinds) :]
    if older:
        before, refs = refs[0], refs[1:]
        refs[-1][:older, :] = before[...]
    width = weights[0].shape[1]
    chunks = spans_of(weights[0].shape[0])
    shards = [pieces[s * CHUNKS : (s + 1) * CHUNKS] for s in range(count)]
    scales = [scale_of(shard) for shard in shards]
    stacked = [
        jnp.concatenate(
            [modulated(shard[k], scale, gain, chunk) for shard, scale in zip(shards, scales)],
            axis=0,
        )
        for k, chunk in enumerate(chunks)
    ]
    for kind, weight in zip(kinds, weights):
        total = None
        for rows, chunk in zip(stacked, chunks):
            part = jnp.dot(rows, weight[chunk, :], preferred_element_type=jnp.float32)
            total = part if total is None else total + part
        if kind == 0:
            refs[0][...] = total.astype(jnp.bfloat16)
        else:
            refs[-1][older:, (kind - 1) * width : kind * width] = total.astype(jnp.bfloat16)


def project(shards, gain, weights, kinds, before=None):
    count = len(shards)
    rows = shards[0][0].shape[0] * count
    older = 0 if before is None else before.shape[0]
    width = weights[0].shape[1]
    shapes = [VMEM((rows, width), jnp.bfloat16)] if 0 in kinds else []
    if 1 in kinds:
        shapes.append(VMEM((older + rows, 2 * width), jnp.bfloat16))
    pieces = [piece for shard in shards for piece in shard]
    extra = [] if before is None else [before]
    used = [weights[kind] for kind in kinds]
    return pl.pallas_call(
        functools.partial(project_kernel, count, tuple(kinds), older),
        in_specs=[IN_VMEM] * (len(pieces) + 1 + len(used) + len(extra)),
        out_specs=[IN_VMEM] * len(shapes),
        out_shape=shapes,
        compiler_params=params(max(1, 2 * count - 2)),
        name="project",
    )(*near(*pieces, gain, *used, *extra))


def lead_kernel(*refs):
    whole, refs = refs[:CHUNKS], refs[CHUNKS:]
    parts, refs = refs[: CHUNKS - 1], refs[CHUNKS - 1 :]
    gain, weights, out = refs[0], refs[1:-1], refs[-1]
    width = weights[0].shape[1]
    chunks = spans_of(weights[0].shape[0])
    rows = whole[0].shape[0]
    scale = scale_of(whole)
    row = lax.broadcasted_iota(jnp.int32, (EXTRA, 1), 0)
    stacked = []
    for k, piece in enumerate(parts):
        shift = gain[1:2, chunks[k]]
        high = shift.astype(jnp.bfloat16).astype(jnp.float32)
        added = jnp.where(row == 0, high, jnp.where(row == 1, shift - high, 0.0))
        unscaled = piece[...].astype(jnp.float32) * (gain[0:1, chunks[k]] * 0.125)
        stacked.append(
            jnp.concatenate(
                [
                    modulated(whole[k], scale, gain, chunks[k]),
                    unscaled.astype(jnp.bfloat16),
                    added.astype(jnp.bfloat16),
                ],
                axis=0,
            )
        )
    for index, weight in enumerate(weights):
        total = sum(
            jnp.dot(lines, weight[chunk, :], preferred_element_type=jnp.float32)
            for lines, chunk in zip(stacked, chunks)
        )
        out[:, index * width : (index + 1) * width] = total
    seen = sum(squares(piece) for piece in parts)
    last = slice(len(weights) * width, len(weights) * width + LANES)
    out[:rows, last] = jnp.broadcast_to(scale, (rows, LANES))
    out[rows : 2 * rows, last] = jnp.broadcast_to(seen, (rows, LANES))


def lead(whole, parts, gain, weights):
    rows = whole[0].shape[0]
    width = weights[0].shape[1]
    return pl.pallas_call(
        lead_kernel,
        in_specs=[IN_VMEM] * (2 * CHUNKS + len(weights)),
        out_specs=IN_VMEM,
        out_shape=VMEM((2 * rows + EXTRA, len(weights) * width + LANES), jnp.float32),
        compiler_params=params(2),
        name="lead",
    )(*near(*whole, *parts, gain, *weights))


def finish_kernel(whole, piece, gain, *refs):
    weights, (start, out) = refs[:-2], refs[-2:]
    width = weights[0].shape[1]
    depth = weights[0].shape[0]
    chunk = spans_of(depth)[-1]
    rows = whole.shape[0]
    last = len(weights) * width
    scale = scale_from(start[rows : 2 * rows, last : last + 1] + squares(piece), depth)
    lines = jnp.concatenate(
        [
            modulated(whole, start[:rows, last : last + 1], gain, chunk),
            modulated(piece, scale, gain, chunk),
        ],
        axis=0,
    )
    for index, weight in enumerate(weights):
        cols = slice(index * width, (index + 1) * width)
        shift = start[2 * rows : 2 * rows + 1, cols] + start[2 * rows + 1 : 2 * rows + 2, cols]
        total = jnp.dot(lines, weight[chunk, :], preferred_element_type=jnp.float32)
        out[:rows, cols] = (total[:rows] + start[:rows, cols]).astype(jnp.bfloat16)
        known = start[rows : 2 * rows, cols] * (scale * 8.0) + shift
        out[rows:, cols] = (total[rows:] + known).astype(jnp.bfloat16)


def finish(whole, piece, gain, weights, start):
    rows = whole.shape[0]
    width = weights[0].shape[1]
    return pl.pallas_call(
        finish_kernel,
        in_specs=[IN_VMEM] * (4 + len(weights)),
        out_specs=IN_VMEM,
        out_shape=VMEM((2 * rows, len(weights) * width), jnp.bfloat16),
        compiler_params=params(2),
        name="finish",
    )(*near(whole, piece, gain, *weights, start))


def barred_of(sources, mine, seg_col, seg_row):
    here = mine[0]
    clip = jnp.concatenate(
        [seg_row + jnp.where((here ^ m) <= here, 0, 1000) for m in range(sources)], axis=1
    )
    return jnp.where(seg_col == clip, 0.0, 1.0)


def stack(blocks, out):
    many = blocks[0].shape[0]
    for m, block in enumerate(blocks):
        out[m * many : (m + 1) * many, :] = block[...]


def blocks_of(tokc):
    block = min(tokc, 128)
    return [slice(start, start + block) for start in range(0, tokc, block)]


def weigh(queries, keys, values, barred, floors):
    scores = [
        lax.dot_general(q, k, (((1,), (1,)), ((), ())), preferred_element_type=jnp.float32)
        for q, k in zip(queries, keys)
    ]
    allowed = barred == 0.0
    scores = [jnp.where(allowed, s * (1.0 / math.sqrt(HD)), -1e30) for s in scores]
    bests = [jnp.max(s, axis=-1, keepdims=True) for s in scores]
    if floors is not None:
        bests = [jnp.maximum(best, floor) for best, floor in zip(bests, floors)]
    weights = [jnp.where(allowed, jnp.exp(s - best), 0.0) for s, best in zip(scores, bests)]
    sums = [
        jnp.dot(w.astype(jnp.bfloat16), v, preferred_element_type=jnp.float32)
        for w, v in zip(weights, values)
    ]
    totals = [jnp.sum(w, axis=-1, keepdims=True) for w in weights]
    return bests, totals, sums


def columns(ref, span, count, start=0):
    return [ref[span, start + h * HD : start + (h + 1) * HD] for h in range(count)]


def attend_early_kernel(parts, sources, mine, seg_col, seg_row, *refs):
    queries, refs = refs[:parts], refs[parts:]
    early, refs = refs[:sources], refs[sources:]
    q_all, sums, bests, totals, barred_late, kv_all = refs
    filled = 0
    for query in queries:
        q_all[filled : filled + query.shape[0], :] = query[...]
        filled += query.shape[0]
    stack(early, kv_all)
    many = early[0].shape[0]
    heads = q_all.shape[1] // HD
    every = slice(0, kv_all.shape[0])
    for span in blocks_of(q_all.shape[0]):
        barred = barred_of(sources, mine, seg_col[span, :], seg_row[:, :many])
        state = weigh(
            columns(q_all, span, heads),
            columns(kv_all, every, heads),
            columns(kv_all, every, heads, heads * HD),
            barred,
            None,
        )
        for h, (best, total, summed) in enumerate(zip(*state)):
            bests[span, h * HD : (h + 1) * HD] = jnp.broadcast_to(best, summed.shape)
            totals[span, h * HD : (h + 1) * HD] = jnp.broadcast_to(total, summed.shape)
            sums[span, h * HD : (h + 1) * HD] = summed
        barred_late[span, :] = barred_of(sources, mine, seg_col[span, :], seg_row[:, many:])


def attend_early(mine, seg_col, seg_row, queries, early):
    sources, many = len(early), early[0].shape[0]
    tokc, width = seg_col.shape[0], queries[0].shape[1]
    return pl.pallas_call(
        functools.partial(attend_early_kernel, len(queries), sources),
        in_specs=[IN_SMEM] + [IN_VMEM] * (2 + len(queries) + sources),
        out_specs=[IN_VMEM] * 5,
        out_shape=[VMEM((tokc, width), jnp.bfloat16)]
        + [VMEM((tokc, width), jnp.float32)] * 3
        + [VMEM((tokc, sources * (tokc - many)), jnp.float32)],
        scratch_shapes=[pltpu.VMEM((sources * many, 2 * width), jnp.bfloat16)],
        compiler_params=params(3 * (sources * tokc // 1024)),
        name="attend_early",
    )(mine, *near(seg_col, seg_row, *queries, *early))


def attend_kernel(shards, sources, place, q_all, sums, bests, totals, barred, *refs):
    late, outs, kv_all, held = refs[:sources], refs[sources:-2], refs[-2], refs[-1]
    tokc, width = q_all.shape
    rows = tokc // shards
    heads = width // HD
    stack(late, kv_all)
    every = slice(0, kv_all.shape[0])
    for span in blocks_of(tokc):
        floors = [floor[:, 0:1] for floor in columns(bests, span, heads)]
        state = weigh(
            columns(q_all, span, heads),
            columns(kv_all, every, heads),
            columns(kv_all, every, heads, heads * HD),
            barred[span, :],
            floors,
        )
        before = zip(floors, columns(totals, span, heads), columns(sums, span, heads))
        for h, (best, total, summed) in enumerate(zip(*state)):
            floor, old_total, old_sum = next(before)
            fade = jnp.exp(floor - best)
            scale = 1.0 / (total + old_total[:, 0:1] * fade)
            result = ((summed + old_sum * fade) * scale).astype(jnp.bfloat16)
            held[span, h * HD : (h + 1) * HD] = result
    for m, out in enumerate(outs):
        spot = lax.rem(place[0] - (place[0] ^ m) + shards, shards) * rows
        out[...] = held[pl.ds(pl.multiple_of(spot, rows), rows), :]


def attend(shards, place, state, late):
    sources, many = len(late), late[0].shape[0]
    tokc, width = state[0].shape
    rows = tokc // shards
    return pl.pallas_call(
        functools.partial(attend_kernel, shards, sources),
        in_specs=[IN_SMEM] + [IN_VMEM] * (len(state) + sources),
        out_specs=[IN_VMEM] * shards,
        out_shape=[VMEM((rows, width), jnp.bfloat16)] * shards,
        scratch_shapes=[
            pltpu.VMEM((sources * many, 2 * width), jnp.bfloat16),
            pltpu.VMEM((tokc, width), jnp.bfloat16),
        ],
        compiler_params=params(3 * (sources * tokc // 1024)),
        name="attend",
    )(place, *near(*state, *late))


def place_kernel(order, place, *refs):
    pieces, out = refs[:-1], refs[-1]
    width = pieces[0].shape[1]
    count = len(pieces)
    for s, piece in zip(order, pieces):
        column = (place[0] ^ s) * width
        out[0, :, pl.ds(pl.multiple_of(column, width), width)] = piece[...]


def place_columns(place, pieces):
    rows, width = pieces[0].shape
    order = [0, *range(2, len(pieces)), 1]
    return pl.pallas_call(
        functools.partial(place_kernel, order),
        in_specs=[IN_SMEM] + [IN_VMEM] * len(pieces),
        out_specs=IN_VMEM,
        out_shape=jax.ShapeDtypeStruct((1, rows, width * len(pieces)), jnp.bfloat16),
        compiler_params=params(1),
        name="place",
    )(place, *near(*[pieces[s] for s in order]))


def across_chips(block, groups):
    return [block] + [
        lax.ppermute(block, "group", [(i, i ^ m) for i in range(groups)])
        for m in range(2, groups, 2)
    ]


def across_cores(held, groups):
    swap = [(i, i ^ 1) for i in range(groups)]
    return [each for block in held for each in (block, lax.ppermute(block, "group", swap))]


def per_device(latents, steps, segment_ids, mod_table, w_query, w_key, w_value):
    shards = lax.axis_size("dp")
    groups = lax.axis_size("group")
    rows = latents.shape[1]
    place = lax.axis_index("dp").astype(jnp.int32)
    mine = lax.axis_index("group").astype(jnp.int32)
    ring = [(i, (i + 1) % shards) for i in range(shards)]

    latents, place, mine = lax.optimization_barrier((latents, place[None], mine[None]))
    pieces = list(split(latents))
    query, keyval, *rest = begin(
        (w_query, w_key, w_value), segment_ids, steps, mod_table, pieces, place, shards
    )
    weights, (gain, seg_col, seg_row) = rest[:3], rest[3:]
    queries = [query]
    pieces = [lax.ppermute(piece, "dp", ring) for piece in pieces]
    pieces[0], keyval = lax.optimization_barrier((pieces[0], keyval))
    arrived = []
    for s in range(1, shards - 2):
        arrived.append(pieces)
        pieces = [lax.ppermute(piece, "dp", ring) for piece in pieces]
    query, keyval = project(arrived, gain, weights, (0, 1, 2), keyval)
    queries.append(query)
    pieces[0], _ = lax.optimization_barrier((pieces[0], keyval))
    early = across_chips(keyval, groups)
    _, early = lax.optimization_barrier((pieces[-1], early))
    early = across_cores(early, groups)
    moved = [lax.ppermute(piece, "dp", ring) for piece in pieces]
    moved[0], early = lax.optimization_barrier((moved[0], early))
    both = [pieces, moved]
    start = lead(pieces, moved[:-1], gain, weights[1:])
    keyval = finish(pieces[-1], moved[-1], gain, weights[1:], start)
    gain, keyval = lax.optimization_barrier((gain, keyval))
    late = across_chips(keyval, groups)
    query = project(both, gain, weights, (0,))[0]
    queries.append(query)
    state = attend_early(mine, seg_col, seg_row, queries, early)
    late[1:] = [lax.optimization_barrier((block, state[0]))[0] for block in late[1:]]
    late = across_cores(late, groups)
    results = attend(shards, place, state, late)
    landed = [results[0]]
    for s in range(1, shards):
        landed.append(
            lax.ppermute(results[s], "dp", [(i, i ^ s) for i in range(shards)])
        )
    return place_columns(place, landed)


def solution(mesh):
    placed = (
        P("group", "dp", None),
        P("group"),
        P(),
        P(),
        P(None, "dp"),
        P(None, "dp"),
        P(None, "dp"),
    )
    return jax.shard_map(
        per_device, mesh=mesh, in_specs=placed, out_specs=P("group", "dp", None), check_vma=False
    )
```

```python
import functools
import math

import jax
import jax.numpy as jnp
from jax import lax
from jax.experimental import pallas as pl
from jax.experimental.pallas import tpu as pltpu
from jax.sharding import PartitionSpec as P

HD = 128
LANES = 128
EXTRA = 16
EDGES = (0, 1, 2)
CHUNKS = len(EDGES) - 1
PARTS = 4
AHEAD = 6
VMEM = pltpu.MemorySpace.VMEM
HBM = pltpu.MemorySpace.HBM
SMEM = pltpu.MemorySpace.SMEM
IN_VMEM = pl.BlockSpec(memory_space=VMEM)
IN_HBM = pl.BlockSpec(memory_space=HBM)
IN_SMEM = pl.BlockSpec(memory_space=SMEM)


def spans_of(depth):
    edges = [depth * edge // EDGES[-1] for edge in EDGES]
    return [slice(low, high) for low, high in zip(edges, edges[1:])]


def params(mebibytes):
    return pltpu.CompilerParams(vmem_limit_bytes=mebibytes * 1024 * 1024)


def near(*arrays):
    return [pltpu.with_memory_space_constraint(a, VMEM) for a in arrays]


def far(*arrays):
    return [pltpu.with_memory_space_constraint(a, HBM) for a in arrays]


def split_kernel(x_hbm, *refs):
    outs, sems = refs[:CHUNKS], refs[CHUNKS]
    copies = [
        pltpu.make_async_copy(x_hbm.at[0, :, span], out, sems.at[k])
        for k, (span, out) in enumerate(zip(spans_of(x_hbm.shape[2]), outs))
    ]
    for copy in copies:
        copy.start()
    for copy in copies:
        copy.wait()


def split(latents):
    _, rows, depth = latents.shape
    widths = [span.stop - span.start for span in spans_of(depth)]
    return pl.pallas_call(
        split_kernel,
        in_specs=[IN_HBM],
        out_specs=[IN_VMEM] * CHUNKS,
        out_shape=[VMEM((rows, width), jnp.bfloat16) for width in widths],
        scratch_shapes=[pltpu.SemaphoreType.DMA((CHUNKS,))],
        compiler_params=params(1),
        name="split",
    )(*far(latents))


def squares(piece):
    x = piece[...].astype(jnp.float32)
    return jnp.sum(x * x, axis=-1, keepdims=True)


def scale_from(total, depth):
    return lax.rsqrt(total * (1.0 / depth) + 1e-06)


def scale_of(pieces):
    depth = sum(piece.shape[1] for piece in pieces)
    return scale_from(sum(squares(piece) for piece in pieces), depth)


def modulated(piece, scale, gain, span):
    x = piece[...].astype(jnp.float32)
    return (x * scale * gain[0:1, span] + gain[1:2, span]).astype(jnp.bfloat16)


def begin_kernel(shards, place, steps, seg_hbm, table, *refs):
    sources, refs = refs[:3], refs[3:]
    pieces, refs = refs[:CHUNKS], refs[CHUNKS:]
    query, keyval = refs[:2]
    outs, (gain, seg_col, seg_row, segments, sems, small) = refs[2:5], refs[5:]
    depth = outs[0].shape[0]
    width = query.shape[1]
    chunks = spans_of(depth)
    reads = [
        pltpu.make_async_copy(table.at[steps[0]], gain, small.at[0]),
        pltpu.make_async_copy(seg_hbm, segments, small.at[1]),
    ]
    for copy in reads:
        copy.start()
    short = depth // PARTS
    spans = [slice(k * short, (k + 1) * short) for k in range(PARTS)]
    copies = [
        pltpu.make_async_copy(sources[i].at[span], outs[i].at[span], sems.at[i, k])
        for i in range(3)
        for k, span in enumerate(spans)
    ]
    for copy in copies[:AHEAD]:
        copy.start()
    for copy in reads:
        copy.wait()
    gain[0:1, :] = 1.0 + gain[0:1, :]
    scale = scale_of(pieces)
    own = jnp.concatenate(
        [modulated(piece, scale, gain, chunk) for piece, chunk in zip(pieces, chunks)], axis=1
    )
    tokc = segments.shape[1]
    rows = tokc // shards

    def owner(position):
        shard = place[0] - position // rows
        return jnp.where(shard < 0, shard + shards, shard) * rows + position % rows

    down = lax.broadcasted_iota(jnp.int32, (tokc, tokc), 0)
    across = lax.broadcasted_iota(jnp.int32, (tokc, tokc), 1)
    natural = segments[...]
    column = jnp.sum(jnp.where(down == across, natural, 0), axis=1, keepdims=True)
    seg_col[...] = jnp.sum(jnp.where(owner(down) == across, natural, 0), axis=1, keepdims=True)
    seg_row[...] = jnp.sum(jnp.where(owner(across) == down, column, 0), axis=0, keepdims=True)
    for i in range(3):
        total = None
        for k, span in enumerate(spans):
            index = i * len(spans) + k
            copies[index].wait()
            if index + AHEAD < len(copies):
                copies[index + AHEAD].start()
            part = jnp.dot(own[:, span], outs[i][span], preferred_element_type=jnp.float32)
            total = part if total is None else total + part
        if i == 0:
            query[...] = total.astype(jnp.bfloat16)
        else:
            keyval[:, (i - 1) * width : i * width] = total.astype(jnp.bfloat16)


def begin(weights, segments, steps, mod_table, pieces, place, shards):
    tokc = segments.shape[0]
    rows = pieces[0].shape[0]
    width = weights[0].shape[1]
    return pl.pallas_call(
        functools.partial(begin_kernel, shards),
        in_specs=[IN_SMEM] * 2 + [IN_HBM] * 5 + [IN_VMEM] * CHUNKS,
        out_specs=[IN_VMEM] * 8,
        out_shape=[VMEM((rows, width), jnp.bfloat16), VMEM((rows, 2 * width), jnp.bfloat16)]
        + [VMEM(w.shape, w.dtype) for w in weights]
        + [VMEM(mod_table.shape[1:], jnp.float32)]
        + [VMEM((tokc, 1), jnp.int32), VMEM((1, tokc), jnp.int32)],
        scratch_shapes=[
            pltpu.VMEM((1, tokc), jnp.int32),
            pltpu.SemaphoreType.DMA((3, PARTS)),
            pltpu.SemaphoreType.DMA((2,)),
        ],
        compiler_params=params(2 + tokc * tokc * 32 // 2**20),
        name="begin",
    )(place, steps, *far(segments[None], mod_table, *weights), *near(*pieces))


def project_kernel(count, kinds, older, *refs):
    pieces, refs = refs[: count * CHUNKS], refs[count * CHUNKS :]
    gain, weights, refs = refs[0], refs[1 : 1 + len(kinds)], refs[1 + len(kinds) :]
    if older:
        before, refs = refs[0], refs[1:]
        refs[-1][:older, :] = before[...]
    width = weights[0].shape[1]
    chunks = spans_of(weights[0].shape[0])
    shards = [pieces[s * CHUNKS : (s + 1) * CHUNKS] for s in range(count)]
    scales = [scale_of(shard) for shard in shards]
    stacked = [
        jnp.concatenate(
            [modulated(shard[k], scale, gain, chunk) for shard, scale in zip(shards, scales)],
            axis=0,
        )
        for k, chunk in enumerate(chunks)
    ]
    for kind, weight in zip(kinds, weights):
        total = None
        for rows, chunk in zip(stacked, chunks):
            part = jnp.dot(rows, weight[chunk, :], preferred_element_type=jnp.float32)
            total = part if total is None else total + part
        if kind == 0:
            refs[0][...] = total.astype(jnp.bfloat16)
        else:
            refs[-1][older:, (kind - 1) * width : kind * width] = total.astype(jnp.bfloat16)


def project(shards, gain, weights, kinds, before=None):
    count = len(shards)
    rows = shards[0][0].shape[0] * count
    older = 0 if before is None else before.shape[0]
    width = weights[0].shape[1]
    shapes = [VMEM((rows, width), jnp.bfloat16)] if 0 in kinds else []
    if 1 in kinds:
        shapes.append(VMEM((older + rows, 2 * width), jnp.bfloat16))
    pieces = [piece for shard in shards for piece in shard]
    extra = [] if before is None else [before]
    used = [weights[kind] for kind in kinds]
    return pl.pallas_call(
        functools.partial(project_kernel, count, tuple(kinds), older),
        in_specs=[IN_VMEM] * (len(pieces) + 1 + len(used) + len(extra)),
        out_specs=[IN_VMEM] * len(shapes),
        out_shape=shapes,
        compiler_params=params(max(1, 2 * count - 2)),
        name="project",
    )(*near(*pieces, gain, *used, *extra))


def lead_kernel(*refs):
    whole, refs = refs[:CHUNKS], refs[CHUNKS:]
    parts, refs = refs[: CHUNKS - 1], refs[CHUNKS - 1 :]
    gain, weights, out = refs[0], refs[1:-1], refs[-1]
    width = weights[0].shape[1]
    chunks = spans_of(weights[0].shape[0])
    rows = whole[0].shape[0]
    scale = scale_of(whole)
    row = lax.broadcasted_iota(jnp.int32, (EXTRA, 1), 0)
    stacked = []
    for k, piece in enumerate(parts):
        shift = gain[1:2, chunks[k]]
        high = shift.astype(jnp.bfloat16).astype(jnp.float32)
        added = jnp.where(row == 0, high, jnp.where(row == 1, shift - high, 0.0))
        unscaled = piece[...].astype(jnp.float32) * (gain[0:1, chunks[k]] * 0.125)
        stacked.append(
            jnp.concatenate(
                [
                    modulated(whole[k], scale, gain, chunks[k]),
                    unscaled.astype(jnp.bfloat16),
                    added.astype(jnp.bfloat16),
                ],
                axis=0,
            )
        )
    for index, weight in enumerate(weights):
        total = sum(
            jnp.dot(lines, weight[chunk, :], preferred_element_type=jnp.float32)
            for lines, chunk in zip(stacked, chunks)
        )
        out[:, index * width : (index + 1) * width] = total
    seen = sum(squares(piece) for piece in parts)
    last = slice(len(weights) * width, len(weights) * width + LANES)
    out[:rows, last] = jnp.broadcast_to(scale, (rows, LANES))
    out[rows : 2 * rows, last] = jnp.broadcast_to(seen, (rows, LANES))


def lead(whole, parts, gain, weights):
    rows = whole[0].shape[0]
    width = weights[0].shape[1]
    return pl.pallas_call(
        lead_kernel,
        in_specs=[IN_VMEM] * (2 * CHUNKS + len(weights)),
        out_specs=IN_VMEM,
        out_shape=VMEM((2 * rows + EXTRA, len(weights) * width + LANES), jnp.float32),
        compiler_params=params(2),
        name="lead",
    )(*near(*whole, *parts, gain, *weights))


def finish_kernel(whole, piece, gain, *refs):
    weights, (start, out) = refs[:-2], refs[-2:]
    width = weights[0].shape[1]
    depth = weights[0].shape[0]
    chunk = spans_of(depth)[-1]
    rows = whole.shape[0]
    last = len(weights) * width
    scale = scale_from(start[rows : 2 * rows, last : last + 1] + squares(piece), depth)
    lines = jnp.concatenate(
        [
            modulated(whole, start[:rows, last : last + 1], gain, chunk),
            modulated(piece, scale, gain, chunk),
        ],
        axis=0,
    )
    for index, weight in enumerate(weights):
        cols = slice(index * width, (index + 1) * width)
        shift = start[2 * rows : 2 * rows + 1, cols] + start[2 * rows + 1 : 2 * rows + 2, cols]
        total = jnp.dot(lines, weight[chunk, :], preferred_element_type=jnp.float32)
        out[:rows, cols] = (total[:rows] + start[:rows, cols]).astype(jnp.bfloat16)
        known = start[rows : 2 * rows, cols] * (scale * 8.0) + shift
        out[rows:, cols] = (total[rows:] + known).astype(jnp.bfloat16)


def finish(whole, piece, gain, weights, start):
    rows = whole.shape[0]
    width = weights[0].shape[1]
    return pl.pallas_call(
        finish_kernel,
        in_specs=[IN_VMEM] * (4 + len(weights)),
        out_specs=IN_VMEM,
        out_shape=VMEM((2 * rows, len(weights) * width), jnp.bfloat16),
        compiler_params=params(2),
        name="finish",
    )(*near(whole, piece, gain, *weights, start))


def barred_of(sources, mine, seg_col, seg_row):
    here = mine[0]
    clip = jnp.concatenate(
        [seg_row + jnp.where((here ^ m) <= here, 0, 1000) for m in range(sources)], axis=1
    )
    return jnp.where(seg_col == clip, 0.0, 1.0)


def stack(blocks, out):
    many = blocks[0].shape[0]
    for m, block in enumerate(blocks):
        out[m * many : (m + 1) * many, :] = block[...]


def blocks_of(tokc):
    block = min(tokc, 128)
    return [slice(start, start + block) for start in range(0, tokc, block)]


def weigh(queries, keys, values, barred, floors):
    scores = [
        lax.dot_general(q, k, (((1,), (1,)), ((), ())), preferred_element_type=jnp.float32)
        for q, k in zip(queries, keys)
    ]
    allowed = barred == 0.0
    scores = [jnp.where(allowed, s * (1.0 / math.sqrt(HD)), -1e30) for s in scores]
    bests = [jnp.max(s, axis=-1, keepdims=True) for s in scores]
    if floors is not None:
        bests = [jnp.maximum(best, floor) for best, floor in zip(bests, floors)]
    weights = [jnp.where(allowed, jnp.exp(s - best), 0.0) for s, best in zip(scores, bests)]
    sums = [
        jnp.dot(w.astype(jnp.bfloat16), v, preferred_element_type=jnp.float32)
        for w, v in zip(weights, values)
    ]
    totals = [jnp.sum(w, axis=-1, keepdims=True) for w in weights]
    return bests, totals, sums


def columns(ref, span, count, start=0):
    return [ref[span, start + h * HD : start + (h + 1) * HD] for h in range(count)]


def attend_early_kernel(parts, sources, mine, seg_col, seg_row, *refs):
    queries, refs = refs[:parts], refs[parts:]
    early, refs = refs[:sources], refs[sources:]
    q_all, sums, bests, totals, barred_late, kv_all = refs
    filled = 0
    for query in queries:
        q_all[filled : filled + query.shape[0], :] = query[...]
        filled += query.shape[0]
    stack(early, kv_all)
    many = early[0].shape[0]
    heads = q_all.shape[1] // HD
    every = slice(0, kv_all.shape[0])
    for span in blocks_of(q_all.shape[0]):
        barred = barred_of(sources, mine, seg_col[span, :], seg_row[:, :many])
        state = weigh(
            columns(q_all, span, heads),
            columns(kv_all, every, heads),
            columns(kv_all, every, heads, heads * HD),
            barred,
            None,
        )
        for h, (best, total, summed) in enumerate(zip(*state)):
            bests[span, h * HD : (h + 1) * HD] = jnp.broadcast_to(best, summed.shape)
            totals[span, h * HD : (h + 1) * HD] = jnp.broadcast_to(total, summed.shape)
            sums[span, h * HD : (h + 1) * HD] = summed
        barred_late[span, :] = barred_of(sources, mine, seg_col[span, :], seg_row[:, many:])


def attend_early(mine, seg_col, seg_row, queries, early):
    sources, many = len(early), early[0].shape[0]
    tokc, width = seg_col.shape[0], queries[0].shape[1]
    return pl.pallas_call(
        functools.partial(attend_early_kernel, len(queries), sources),
        in_specs=[IN_SMEM] + [IN_VMEM] * (2 + len(queries) + sources),
        out_specs=[IN_VMEM] * 5,
        out_shape=[VMEM((tokc, width), jnp.bfloat16)]
        + [VMEM((tokc, width), jnp.float32)] * 3
        + [VMEM((tokc, sources * (tokc - many)), jnp.float32)],
        scratch_shapes=[pltpu.VMEM((sources * many, 2 * width), jnp.bfloat16)],
        compiler_params=params(3 * (sources * tokc // 1024)),
        name="attend_early",
    )(mine, *near(seg_col, seg_row, *queries, *early))


def attend_kernel(shards, sources, place, q_all, sums, bests, totals, barred, *refs):
    late, outs, kv_all, held = refs[:sources], refs[sources:-2], refs[-2], refs[-1]
    tokc, width = q_all.shape
    rows = tokc // shards
    heads = width // HD
    stack(late, kv_all)
    every = slice(0, kv_all.shape[0])
    for span in blocks_of(tokc):
        floors = [floor[:, 0:1] for floor in columns(bests, span, heads)]
        state = weigh(
            columns(q_all, span, heads),
            columns(kv_all, every, heads),
            columns(kv_all, every, heads, heads * HD),
            barred[span, :],
            floors,
        )
        before = zip(floors, columns(totals, span, heads), columns(sums, span, heads))
        for h, (best, total, summed) in enumerate(zip(*state)):
            floor, old_total, old_sum = next(before)
            fade = jnp.exp(floor - best)
            scale = 1.0 / (total + old_total[:, 0:1] * fade)
            result = ((summed + old_sum * fade) * scale).astype(jnp.bfloat16)
            held[span, h * HD : (h + 1) * HD] = result
    for m, out in enumerate(outs):
        spot = lax.rem(place[0] - (place[0] ^ m) + shards, shards) * rows
        out[...] = held[pl.ds(pl.multiple_of(spot, rows), rows), :]


def attend(shards, place, state, late):
    sources, many = len(late), late[0].shape[0]
    tokc, width = state[0].shape
    rows = tokc // shards
    return pl.pallas_call(
        functools.partial(attend_kernel, shards, sources),
        in_specs=[IN_SMEM] + [IN_VMEM] * (len(state) + sources),
        out_specs=[IN_VMEM] * shards,
        out_shape=[VMEM((rows, width), jnp.bfloat16)] * shards,
        scratch_shapes=[
            pltpu.VMEM((sources * many, 2 * width), jnp.bfloat16),
            pltpu.VMEM((tokc, width), jnp.bfloat16),
        ],
        compiler_params=params(3 * (sources * tokc // 1024)),
        name="attend",
    )(place, *near(*state, *late))


def place_kernel(order, place, *refs):
    pieces, out = refs[:-1], refs[-1]
    width = pieces[0].shape[1]
    count = len(pieces)
    for s, piece in zip(order, pieces):
        column = (place[0] ^ s) * width
        out[0, :, pl.ds(pl.multiple_of(column, width), width)] = piece[...]


def place_columns(place, pieces):
    rows, width = pieces[0].shape
    order = [0, *range(2, len(pieces)), 1]
    return pl.pallas_call(
        functools.partial(place_kernel, order),
        in_specs=[IN_SMEM] + [IN_VMEM] * len(pieces),
        out_specs=IN_VMEM,
        out_shape=jax.ShapeDtypeStruct((1, rows, width * len(pieces)), jnp.bfloat16),
        compiler_params=params(1),
        name="place",
    )(place, *near(*[pieces[s] for s in order]))


def across_chips(block, groups):
    return [block] + [
        lax.ppermute(block, "group", [(i, i ^ m) for i in range(groups)])
        for m in range(2, groups, 2)
    ]


def across_cores(held, groups):
    swap = [(i, i ^ 1) for i in range(groups)]
    return [each for block in held for each in (block, lax.ppermute(block, "group", swap))]


def per_device(latents, steps, segment_ids, mod_table, w_query, w_key, w_value):
    shards = lax.axis_size("dp")
    groups = lax.axis_size("group")
    rows = latents.shape[1]
    place = lax.axis_index("dp").astype(jnp.int32)
    mine = lax.axis_index("group").astype(jnp.int32)
    ring = [(i, (i + 1) % shards) for i in range(shards)]

    latents, place, mine = lax.optimization_barrier((latents, place[None], mine[None]))
    pieces = list(split(latents))
    query, keyval, *rest = begin(
        (w_query, w_key, w_value), segment_ids, steps, mod_table, pieces, place, shards
    )
    weights, (gain, seg_col, seg_row) = rest[:3], rest[3:]
    queries = [query]
    pieces = [lax.ppermute(piece, "dp", ring) for piece in pieces]
    pieces[0], keyval = lax.optimization_barrier((pieces[0], keyval))
    arrived = []
    for s in range(1, shards - 2):
        arrived.append(pieces)
        pieces = [lax.ppermute(piece, "dp", ring) for piece in pieces]
    query, keyval = project(arrived, gain, weights, (0, 1, 2), keyval)
    queries.append(query)
    pieces[0], _ = lax.optimization_barrier((pieces[0], keyval))
    early = across_chips(keyval, groups)
    _, early = lax.optimization_barrier((pieces[-1], early))
    early = across_cores(early, groups)
    moved = [lax.ppermute(piece, "dp", ring) for piece in pieces]
    moved[0], early = lax.optimization_barrier((moved[0], early))
    both = [pieces, moved]
    start = lead(pieces, moved[:-1], gain, weights[1:])
    keyval = finish(pieces[-1], moved[-1], gain, weights[1:], start)
    gain, keyval = lax.optimization_barrier((gain, keyval))
    late = across_chips(keyval, groups)
    query = project(both, gain, weights, (0,))[0]
    queries.append(query)
    state = attend_early(mine, seg_col, seg_row, queries, early)
    tail = [lax.optimization_barrier((block, state[0]))[0] for block in late[:0:-1]]
    late[1:] = tail[::-1]
    late = across_cores(late, groups)
    results = attend(shards, place, state, late)
    landed = [results[0]]
    for s in range(1, shards):
        landed.append(
            lax.ppermute(results[s], "dp", [(i, i ^ s) for i in range(shards)])
        )
    return place_columns(place, landed)


def solution(mesh):
    placed = (
        P("group", "dp", None),
        P("group"),
        P(),
        P(),
        P(None, "dp"),
        P(None, "dp"),
        P(None, "dp"),
    )
    return jax.shard_map(
        per_device, mesh=mesh, in_specs=placed, out_specs=P("group", "dp", None), check_vma=False
    )
```

```python
import functools
import math

import jax
import jax.numpy as jnp
from jax import lax
from jax.experimental import pallas as pl
from jax.experimental.pallas import tpu as pltpu
from jax.sharding import PartitionSpec as P

HD = 128
LANES = 128
EXTRA = 16
EDGES = (0, 1, 2)
CHUNKS = len(EDGES) - 1
PARTS = 4
AHEAD = 6
VMEM = pltpu.MemorySpace.VMEM
HBM = pltpu.MemorySpace.HBM
SMEM = pltpu.MemorySpace.SMEM
IN_VMEM = pl.BlockSpec(memory_space=VMEM)
IN_HBM = pl.BlockSpec(memory_space=HBM)
IN_SMEM = pl.BlockSpec(memory_space=SMEM)


def spans_of(depth):
    edges = [depth * edge // EDGES[-1] for edge in EDGES]
    return [slice(low, high) for low, high in zip(edges, edges[1:])]


def params(mebibytes):
    return pltpu.CompilerParams(vmem_limit_bytes=mebibytes * 1024 * 1024)


def near(*arrays):
    return [pltpu.with_memory_space_constraint(a, VMEM) for a in arrays]


def far(*arrays):
    return [pltpu.with_memory_space_constraint(a, HBM) for a in arrays]


def split_kernel(x_hbm, *refs):
    outs, sems = refs[:CHUNKS], refs[CHUNKS]
    copies = [
        pltpu.make_async_copy(x_hbm.at[0, :, span], out, sems.at[k])
        for k, (span, out) in enumerate(zip(spans_of(x_hbm.shape[2]), outs))
    ]
    for copy in copies:
        copy.start()
    for copy in copies:
        copy.wait()


def split(latents):
    _, rows, depth = latents.shape
    widths = [span.stop - span.start for span in spans_of(depth)]
    return pl.pallas_call(
        split_kernel,
        in_specs=[IN_HBM],
        out_specs=[IN_VMEM] * CHUNKS,
        out_shape=[VMEM((rows, width), jnp.bfloat16) for width in widths],
        scratch_shapes=[pltpu.SemaphoreType.DMA((CHUNKS,))],
        compiler_params=params(1),
        name="split",
    )(*far(latents))


def squares(piece):
    x = piece[...].astype(jnp.float32)
    return jnp.sum(x * x, axis=-1, keepdims=True)


def scale_from(total, depth):
    return lax.rsqrt(total * (1.0 / depth) + 1e-06)


def scale_of(pieces):
    depth = sum(piece.shape[1] for piece in pieces)
    return scale_from(sum(squares(piece) for piece in pieces), depth)


def modulated(piece, scale, gain, span):
    x = piece[...].astype(jnp.float32)
    return (x * scale * gain[0:1, span] + gain[1:2, span]).astype(jnp.bfloat16)


def begin_kernel(shards, place, steps, seg_hbm, table, *refs):
    sources, refs = refs[:3], refs[3:]
    pieces, refs = refs[:CHUNKS], refs[CHUNKS:]
    query, keyval = refs[:2]
    outs, (gain, seg_col, seg_row, segments, sems, small) = refs[2:5], refs[5:]
    depth = outs[0].shape[0]
    width = query.shape[1]
    chunks = spans_of(depth)
    reads = [
        pltpu.make_async_copy(table.at[steps[0]], gain, small.at[0]),
        pltpu.make_async_copy(seg_hbm, segments, small.at[1]),
    ]
    for copy in reads:
        copy.start()
    short = depth // PARTS
    spans = [slice(k * short, (k + 1) * short) for k in range(PARTS)]
    copies = [
        pltpu.make_async_copy(sources[i].at[span], outs[i].at[span], sems.at[i, k])
        for i in range(3)
        for k, span in enumerate(spans)
    ]
    for copy in copies[:AHEAD]:
        copy.start()
    for copy in reads:
        copy.wait()
    gain[0:1, :] = 1.0 + gain[0:1, :]
    scale = scale_of(pieces)
    own = jnp.concatenate(
        [modulated(piece, scale, gain, chunk) for piece, chunk in zip(pieces, chunks)], axis=1
    )
    tokc = segments.shape[1]
    rows = tokc // shards

    def owner(position):
        shard = place[0] - position // rows
        return jnp.where(shard < 0, shard + shards, shard) * rows + position % rows

    down = lax.broadcasted_iota(jnp.int32, (tokc, tokc), 0)
    across = lax.broadcasted_iota(jnp.int32, (tokc, tokc), 1)
    natural = segments[...]
    column = jnp.sum(jnp.where(down == across, natural, 0), axis=1, keepdims=True)
    seg_col[...] = jnp.sum(jnp.where(owner(down) == across, natural, 0), axis=1, keepdims=True)
    seg_row[...] = jnp.sum(jnp.where(owner(across) == down, column, 0), axis=0, keepdims=True)
    for i in range(3):
        total = None
        for k, span in enumerate(spans):
            index = i * len(spans) + k
            copies[index].wait()
            if index + AHEAD < len(copies):
                copies[index + AHEAD].start()
            part = jnp.dot(own[:, span], outs[i][span], preferred_element_type=jnp.float32)
            total = part if total is None else total + part
        if i == 0:
            query[...] = total.astype(jnp.bfloat16)
        else:
            keyval[:, (i - 1) * width : i * width] = total.astype(jnp.bfloat16)


def begin(weights, segments, steps, mod_table, pieces, place, shards):
    tokc = segments.shape[0]
    rows = pieces[0].shape[0]
    width = weights[0].shape[1]
    return pl.pallas_call(
        functools.partial(begin_kernel, shards),
        in_specs=[IN_SMEM] * 2 + [IN_HBM] * 5 + [IN_VMEM] * CHUNKS,
        out_specs=[IN_VMEM] * 8,
        out_shape=[VMEM((rows, width), jnp.bfloat16), VMEM((rows, 2 * width), jnp.bfloat16)]
        + [VMEM(w.shape, w.dtype) for w in weights]
        + [VMEM(mod_table.shape[1:], jnp.float32)]
        + [VMEM((tokc, 1), jnp.int32), VMEM((1, tokc), jnp.int32)],
        scratch_shapes=[
            pltpu.VMEM((1, tokc), jnp.int32),
            pltpu.SemaphoreType.DMA((3, PARTS)),
            pltpu.SemaphoreType.DMA((2,)),
        ],
        compiler_params=params(2 + tokc * tokc * 32 // 2**20),
        name="begin",
    )(place, steps, *far(segments[None], mod_table, *weights), *near(*pieces))


def project_kernel(count, kinds, older, *refs):
    pieces, refs = refs[: count * CHUNKS], refs[count * CHUNKS :]
    gain, weights, refs = refs[0], refs[1 : 1 + len(kinds)], refs[1 + len(kinds) :]
    if older:
        before, refs = refs[0], refs[1:]
        refs[-1][:older, :] = before[...]
    width = weights[0].shape[1]
    chunks = spans_of(weights[0].shape[0])
    shards = [pieces[s * CHUNKS : (s + 1) * CHUNKS] for s in range(count)]
    scales = [scale_of(shard) for shard in shards]
    stacked = [
        jnp.concatenate(
            [modulated(shard[k], scale, gain, chunk) for shard, scale in zip(shards, scales)],
            axis=0,
        )
        for k, chunk in enumerate(chunks)
    ]
    for kind, weight in zip(kinds, weights):
        total = None
        for rows, chunk in zip(stacked, chunks):
            part = jnp.dot(rows, weight[chunk, :], preferred_element_type=jnp.float32)
            total = part if total is None else total + part
        if kind == 0:
            refs[0][...] = total.astype(jnp.bfloat16)
        else:
            refs[-1][older:, (kind - 1) * width : kind * width] = total.astype(jnp.bfloat16)


def project(shards, gain, weights, kinds, before=None):
    count = len(shards)
    rows = shards[0][0].shape[0] * count
    older = 0 if before is None else before.shape[0]
    width = weights[0].shape[1]
    shapes = [VMEM((rows, width), jnp.bfloat16)] if 0 in kinds else []
    if 1 in kinds:
        shapes.append(VMEM((older + rows, 2 * width), jnp.bfloat16))
    pieces = [piece for shard in shards for piece in shard]
    extra = [] if before is None else [before]
    used = [weights[kind] for kind in kinds]
    return pl.pallas_call(
        functools.partial(project_kernel, count, tuple(kinds), older),
        in_specs=[IN_VMEM] * (len(pieces) + 1 + len(used) + len(extra)),
        out_specs=[IN_VMEM] * len(shapes),
        out_shape=shapes,
        compiler_params=params(max(1, 2 * count - 2)),
        name="project",
    )(*near(*pieces, gain, *used, *extra))


def lead_kernel(*refs):
    whole, refs = refs[:CHUNKS], refs[CHUNKS:]
    parts, refs = refs[: CHUNKS - 1], refs[CHUNKS - 1 :]
    gain, weights, out = refs[0], refs[1:-1], refs[-1]
    width = weights[0].shape[1]
    chunks = spans_of(weights[0].shape[0])
    rows = whole[0].shape[0]
    scale = scale_of(whole)
    row = lax.broadcasted_iota(jnp.int32, (EXTRA, 1), 0)
    stacked = []
    for k, piece in enumerate(parts):
        shift = gain[1:2, chunks[k]]
        high = shift.astype(jnp.bfloat16).astype(jnp.float32)
        added = jnp.where(row == 0, high, jnp.where(row == 1, shift - high, 0.0))
        unscaled = piece[...].astype(jnp.float32) * (gain[0:1, chunks[k]] * 0.125)
        stacked.append(
            jnp.concatenate(
                [
                    modulated(whole[k], scale, gain, chunks[k]),
                    unscaled.astype(jnp.bfloat16),
                    added.astype(jnp.bfloat16),
                ],
                axis=0,
            )
        )
    for index, weight in enumerate(weights):
        total = sum(
            jnp.dot(lines, weight[chunk, :], preferred_element_type=jnp.float32)
            for lines, chunk in zip(stacked, chunks)
        )
        out[:, index * width : (index + 1) * width] = total
    seen = sum(squares(piece) for piece in parts)
    last = slice(len(weights) * width, len(weights) * width + LANES)
    out[:rows, last] = jnp.broadcast_to(scale, (rows, LANES))
    out[rows : 2 * rows, last] = jnp.broadcast_to(seen, (rows, LANES))


def lead(whole, parts, gain, weights):
    rows = whole[0].shape[0]
    width = weights[0].shape[1]
    return pl.pallas_call(
        lead_kernel,
        in_specs=[IN_VMEM] * (2 * CHUNKS + len(weights)),
        out_specs=IN_VMEM,
        out_shape=VMEM((2 * rows + EXTRA, len(weights) * width + LANES), jnp.float32),
        compiler_params=params(2),
        name="lead",
    )(*near(*whole, *parts, gain, *weights))


def finish_kernel(whole, piece, gain, *refs):
    weights, (start, out) = refs[:-2], refs[-2:]
    width = weights[0].shape[1]
    depth = weights[0].shape[0]
    chunk = spans_of(depth)[-1]
    rows = whole.shape[0]
    last = len(weights) * width
    scale = scale_from(start[rows : 2 * rows, last : last + 1] + squares(piece), depth)
    lines = jnp.concatenate(
        [
            modulated(whole, start[:rows, last : last + 1], gain, chunk),
            modulated(piece, scale, gain, chunk),
        ],
        axis=0,
    )
    for index, weight in enumerate(weights):
        cols = slice(index * width, (index + 1) * width)
        shift = start[2 * rows : 2 * rows + 1, cols] + start[2 * rows + 1 : 2 * rows + 2, cols]
        total = jnp.dot(lines, weight[chunk, :], preferred_element_type=jnp.float32)
        out[:rows, cols] = (total[:rows] + start[:rows, cols]).astype(jnp.bfloat16)
        known = start[rows : 2 * rows, cols] * (scale * 8.0) + shift
        out[rows:, cols] = (total[rows:] + known).astype(jnp.bfloat16)


def finish(whole, piece, gain, weights, start):
    rows = whole.shape[0]
    width = weights[0].shape[1]
    return pl.pallas_call(
        finish_kernel,
        in_specs=[IN_VMEM] * (4 + len(weights)),
        out_specs=IN_VMEM,
        out_shape=VMEM((2 * rows, len(weights) * width), jnp.bfloat16),
        compiler_params=params(2),
        name="finish",
    )(*near(whole, piece, gain, *weights, start))


def barred_of(sources, mine, seg_col, seg_row):
    here = mine[0]
    clip = jnp.concatenate(
        [seg_row + jnp.where((here ^ m) <= here, 0, 1000) for m in range(sources)], axis=1
    )
    return jnp.where(seg_col == clip, 0.0, 1.0)


def stack(blocks, out):
    many = blocks[0].shape[0]
    for m, block in enumerate(blocks):
        out[m * many : (m + 1) * many, :] = block[...]


def blocks_of(tokc):
    block = min(tokc, 128)
    return [slice(start, start + block) for start in range(0, tokc, block)]


def weigh(queries, keys, values, barred, floors):
    scores = [
        lax.dot_general(q, k, (((1,), (1,)), ((), ())), preferred_element_type=jnp.float32)
        for q, k in zip(queries, keys)
    ]
    allowed = barred == 0.0
    scores = [jnp.where(allowed, s * (1.0 / math.sqrt(HD)), -1e30) for s in scores]
    bests = [jnp.max(s, axis=-1, keepdims=True) for s in scores]
    if floors is not None:
        bests = [jnp.maximum(best, floor) for best, floor in zip(bests, floors)]
    weights = [jnp.where(allowed, jnp.exp(s - best), 0.0) for s, best in zip(scores, bests)]
    sums = [
        jnp.dot(w.astype(jnp.bfloat16), v, preferred_element_type=jnp.float32)
        for w, v in zip(weights, values)
    ]
    totals = [jnp.sum(w, axis=-1, keepdims=True) for w in weights]
    return bests, totals, sums


def columns(ref, span, count, start=0):
    return [ref[span, start + h * HD : start + (h + 1) * HD] for h in range(count)]


def attend_early_kernel(shards, parts, sources, mine, place, seg_in, seg_row, *refs):
    queries, refs = refs[:parts], refs[parts:]
    early, refs = refs[:sources], refs[sources:]
    q_all, sums, bests, totals, barred_late, kv_all, q_in, seg_col = refs
    filled = 0
    for query in queries:
        q_in[filled : filled + query.shape[0], :] = query[...]
        filled += query.shape[0]
    rows = filled // shards
    for m in range(shards):
        spot = lax.rem(place[0] - (place[0] ^ m) + shards, shards) * rows
        taken = pl.ds(pl.multiple_of(spot, rows), rows)
        q_all[m * rows : (m + 1) * rows, :] = q_in[taken, :]
        seg_col[m * rows : (m + 1) * rows, :] = seg_in[taken, :]
    stack(early, kv_all)
    many = early[0].shape[0]
    heads = q_all.shape[1] // HD
    every = slice(0, kv_all.shape[0])
    for span in blocks_of(q_all.shape[0]):
        barred = barred_of(sources, mine, seg_col[span, :], seg_row[:, :many])
        state = weigh(
            columns(q_all, span, heads),
            columns(kv_all, every, heads),
            columns(kv_all, every, heads, heads * HD),
            barred,
            None,
        )
        for h, (best, total, summed) in enumerate(zip(*state)):
            bests[span, h * HD : (h + 1) * HD] = jnp.broadcast_to(best, summed.shape)
            totals[span, h * HD : (h + 1) * HD] = jnp.broadcast_to(total, summed.shape)
            sums[span, h * HD : (h + 1) * HD] = summed
        barred_late[span, :] = barred_of(sources, mine, seg_col[span, :], seg_row[:, many:])


def attend_early(shards, mine, place, seg_col, seg_row, queries, early):
    sources, many = len(early), early[0].shape[0]
    tokc, width = seg_col.shape[0], queries[0].shape[1]
    return pl.pallas_call(
        functools.partial(attend_early_kernel, shards, len(queries), sources),
        in_specs=[IN_SMEM] * 2 + [IN_VMEM] * (2 + len(queries) + sources),
        out_specs=[IN_VMEM] * 5,
        out_shape=[VMEM((tokc, width), jnp.bfloat16)]
        + [VMEM((tokc, width), jnp.float32)] * 3
        + [VMEM((tokc, sources * (tokc - many)), jnp.float32)],
        scratch_shapes=[
            pltpu.VMEM((sources * many, 2 * width), jnp.bfloat16),
            pltpu.VMEM((tokc, width), jnp.bfloat16),
            pltpu.VMEM((tokc, 1), jnp.int32),
        ],
        compiler_params=params(3 * (sources * tokc // 1024)),
        name="attend_early",
    )(mine, place, *near(seg_col, seg_row, *queries, *early))


def attend_kernel(shards, sources, q_all, sums, bests, totals, barred, *refs):
    late, outs, kv_all = refs[:sources], refs[sources:-1], refs[-1]
    tokc, width = q_all.shape
    rows = tokc // shards
    heads = width // HD
    stack(late, kv_all)
    every = slice(0, kv_all.shape[0])
    for span in blocks_of(tokc):
        floors = [floor[:, 0:1] for floor in columns(bests, span, heads)]
        state = weigh(
            columns(q_all, span, heads),
            columns(kv_all, every, heads),
            columns(kv_all, every, heads, heads * HD),
            barred[span, :],
            floors,
        )
        before = zip(floors, columns(totals, span, heads), columns(sums, span, heads))
        for h, (best, total, summed) in enumerate(zip(*state)):
            floor, old_total, old_sum = next(before)
            fade = jnp.exp(floor - best)
            scale = 1.0 / (total + old_total[:, 0:1] * fade)
            result = ((summed + old_sum * fade) * scale).astype(jnp.bfloat16)
            for m in range(span.start // rows, span.stop // rows):
                outs[m][:, h * HD : (h + 1) * HD] = result[
                    m * rows - span.start : (m + 1) * rows - span.start
                ]


def attend(shards, state, late):
    sources, many = len(late), late[0].shape[0]
    tokc, width = state[0].shape
    rows = tokc // shards
    return pl.pallas_call(
        functools.partial(attend_kernel, shards, sources),
        in_specs=[IN_VMEM] * (len(state) + sources),
        out_specs=[IN_VMEM] * shards,
        out_shape=[VMEM((rows, width), jnp.bfloat16)] * shards,
        scratch_shapes=[
            pltpu.VMEM((sources * many, 2 * width), jnp.bfloat16),
        ],
        compiler_params=params(3 * (sources * tokc // 1024)),
        name="attend",
    )(*near(*state, *late))


def place_kernel(order, place, *refs):
    pieces, out = refs[:-1], refs[-1]
    width = pieces[0].shape[1]
    count = len(pieces)
    for s, piece in zip(order, pieces):
        column = (place[0] ^ s) * width
        out[0, :, pl.ds(pl.multiple_of(column, width), width)] = piece[...]


def place_columns(place, pieces):
    rows, width = pieces[0].shape
    order = [0, *range(2, len(pieces)), 1]
    return pl.pallas_call(
        functools.partial(place_kernel, order),
        in_specs=[IN_SMEM] + [IN_VMEM] * len(pieces),
        out_specs=IN_VMEM,
        out_shape=jax.ShapeDtypeStruct((1, rows, width * len(pieces)), jnp.bfloat16),
        compiler_params=params(1),
        name="place",
    )(place, *near(*[pieces[s] for s in order]))


def across_chips(block, groups):
    return [block] + [
        lax.ppermute(block, "group", [(i, i ^ m) for i in range(groups)])
        for m in range(2, groups, 2)
    ]


def across_cores(held, groups):
    swap = [(i, i ^ 1) for i in range(groups)]
    return [each for block in held for each in (block, lax.ppermute(block, "group", swap))]


def per_device(latents, steps, segment_ids, mod_table, w_query, w_key, w_value):
    shards = lax.axis_size("dp")
    groups = lax.axis_size("group")
    rows = latents.shape[1]
    place = lax.axis_index("dp").astype(jnp.int32)
    mine = lax.axis_index("group").astype(jnp.int32)
    ring = [(i, (i + 1) % shards) for i in range(shards)]

    latents, place, mine = lax.optimization_barrier((latents, place[None], mine[None]))
    pieces = list(split(latents))
    query, keyval, *rest = begin(
        (w_query, w_key, w_value), segment_ids, steps, mod_table, pieces, place, shards
    )
    weights, (gain, seg_col, seg_row) = rest[:3], rest[3:]
    queries = [query]
    pieces = [lax.ppermute(piece, "dp", ring) for piece in pieces]
    pieces[0], keyval = lax.optimization_barrier((pieces[0], keyval))
    arrived = []
    for s in range(1, shards - 2):
        arrived.append(pieces)
        pieces = [lax.ppermute(piece, "dp", ring) for piece in pieces]
    query, keyval = project(arrived, gain, weights, (0, 1, 2), keyval)
    queries.append(query)
    pieces[0], _ = lax.optimization_barrier((pieces[0], keyval))
    early = across_chips(keyval, groups)
    _, early = lax.optimization_barrier((pieces[-1], early))
    early = across_cores(early, groups)
    moved = [lax.ppermute(piece, "dp", ring) for piece in pieces]
    moved[0], early = lax.optimization_barrier((moved[0], early))
    both = [pieces, moved]
    start = lead(pieces, moved[:-1], gain, weights[1:])
    keyval = finish(pieces[-1], moved[-1], gain, weights[1:], start)
    gain, keyval = lax.optimization_barrier((gain, keyval))
    late = across_chips(keyval, groups)
    query = project(both, gain, weights, (0,))[0]
    queries.append(query)
    state = attend_early(shards, mine, place, seg_col, seg_row, queries, early)
    tail = [lax.optimization_barrier((block, state[0]))[0] for block in late[:0:-1]]
    late[1:] = tail[::-1]
    late = across_cores(late, groups)
    results = attend(shards, state, late)
    landed = [results[0]]
    for s in range(1, shards):
        landed.append(
            lax.ppermute(results[s], "dp", [(i, i ^ s) for i in range(shards)])
        )
    return place_columns(place, landed)


def solution(mesh):
    placed = (
        P("group", "dp", None),
        P("group"),
        P(),
        P(),
        P(None, "dp"),
        P(None, "dp"),
        P(None, "dp"),
    )
    return jax.shard_map(
        per_device, mesh=mesh, in_specs=placed, out_specs=P("group", "dp", None), check_vma=False
    )
```
